32 devices in a mesh: dp: 16 (over z, y, x), tensor: 2 (over core).
Axes of the slice: x: 2, y: 2, z: 4, core: 2. Of those that a mesh axis runs over, the one named last changes fastest.
Arguments:
- patch_embedding_grid: bfloat16 [55296, 384], P(('dp', 'tensor')), may hold values from -6 to 6
- image_size_class: int32 [96], P('dp'), may hold values from 0 to 2, as said below
- loss_sensitivity: bfloat16 [55296, 384], P(('dp', 'tensor'))
- triple_coefficients: float32 [384, 1152], P(None, 'tensor'), may hold values from -0.3125 to 0.3125
- triple_offset: float32 [1152], replicated, may hold values from -1.75 to 1.75
- sharpness: float32 [8], replicated, may hold values from 20 to 50
- mapping_coefficients: float32 [384, 384], P('tensor'), may hold values from -0.875 to 0.875
- expansion_coefficients: float32 [384, 1536], P(None, 'tensor'), may hold values from -0.3125 to 0.3125
- expansion_offset: float32 [1536], replicated, may hold values from -1.75 to 1.75
- contraction_coefficients: float32 [1536, 384], P('tensor'), may hold values from -0.15625 to 0.15625
- normalizer_multipliers: float32 [4, 384], replicated, may hold values from 0.5 to 1.5
- offset_rows_all: float32 [7, 384], replicated, may hold values from -1.75 to 1.75
- spatial_kernels: float32 [18, 384], replicated, may hold values from -2 to 2
- residual_multipliers: float32 [3, 384], replicated, may hold values from 0.5 to 1.5
- triple_velocity: float32 [384, 1152], P(None, 'tensor'), may hold values from -14 to 14
- mapping_velocity: float32 [384, 384], P('tensor'), may hold values from -14 to 14
- expansion_velocity: float32 [384, 1536], P(None, 'tensor'), may hold values from -14 to 14
- contraction_velocity: float32 [1536, 384], P('tensor'), may hold values from -14 to 14
- triple_offset_velocity: float32 [1152], replicated, may hold values from -14 to 14
- sharpness_velocity: float32 [8], replicated, may hold values from -3 to 3
- expansion_offset_velocity: float32 [1536], replicated, may hold values from -3 to 3
- multiplier_velocity: float32 [4, 384], replicated, may hold values from -3 to 3
- offset_velocity: float32 [7, 384], replicated, may hold values from -3 to 3
- kernel_velocity: float32 [18, 384], replicated, may hold values from -3 to 3
- residual_multiplier_velocity: float32 [3, 384], replicated, may hold values from -3 to 3
- triple_residual_buffer: float32 [16, 384, 1152], P('dp', None, 'tensor'), may hold values from -128 to 128
- mapping_residual_store: float32 [16, 384, 384], P('dp', 'tensor'), may hold values from -128 to 128
- expansion_residual_store: float32 [16, 384, 1536], P('dp', None, 'tensor'), may hold values from -128 to 128
- contraction_residual_store: float32 [16, 1536, 384], P('dp', 'tensor'), may hold values from -128 to 128
- triple_right_factor: float32 [1152, 8], P('tensor'), may hold values from -6 to 6
- mapping_right_factor: float32 [384, 8], replicated, may hold values from -6 to 6
- expansion_right_factor: float32 [1536, 8], P('tensor'), may hold values from -6 to 6
- contraction_right_factor: float32 [384, 8], replicated, may hold values from -6 to 6
Outputs:
- block_out: bfloat16 [55296, 384], P(('dp', 'tensor'))
- input_grad: bfloat16 [55296, 384], P(('dp', 'tensor'))
- new_qkv_weight: float32 [384, 1152], P(None, 'tensor')
- new_proj_weight: float32 [384, 384], P('tensor')
- new_in_weight: float32 [384, 1536], P(None, 'tensor')
- new_out_weight: float32 [1536, 384], P('tensor')
- new_qkv_bias: float32 [1152], replicated
- new_temperature: float32 [8], replicated
- new_in_bias: float32 [1536], replicated
- new_gains: float32 [4, 384], replicated
- new_biases: float32 [7, 384], replicated
- new_taps: float32 [18, 384], replicated
- new_scales: float32 [3, 384], replicated
- new_qkv_moment: float32 [384, 1152], P(None, 'tensor')
- new_proj_moment: float32 [384, 384], P('tensor')
- new_in_moment: float32 [384, 1536], P(None, 'tensor')
- new_out_moment: float32 [1536, 384], P('tensor')
- new_qkv_bias_moment: float32 [1152], replicated
- new_temper_moment: float32 [8], replicated
- new_in_bias_moment: float32 [1536], replicated
- new_gains_moment: float32 [4, 384], replicated
- new_biases_moment: float32 [7, 384], replicated
- new_taps_moment: float32 [18, 384], replicated
- new_scales_moment: float32 [3, 384], replicated
- new_qkv_error: float32 [16, 384, 1152], P('dp', None, 'tensor')
- new_proj_error: float32 [16, 384, 384], P('dp', 'tensor')
- new_in_error: float32 [16, 384, 1536], P('dp', None, 'tensor')
- new_out_error: float32 [16, 1536, 384], P('dp', 'tensor')
- new_qkv_basis: float32 [1152, 8], P('tensor')
- new_proj_basis: float32 [384, 8], replicated
- new_in_basis: float32 [1536, 8], P('tensor')
- new_out_basis: float32 [384, 8], replicated
The draws below stay inside these ranges and needn't reach their ends.
Inputs may be any that keep to these rules, and one draw needn't show every extreme that they name: `image_size_class`: bucket 0, 1, 2 gives a square image of side 24 * 7 / 12, 18, 24 in the top-left corner of its canvas; the first image has bucket 0 and the last bucket 2.
All inputs are finite; a program needn't handle non-finite values.
Results may differ from the reference program's by a relative error of at most 0.0095.
The reference program's roundings to bfloat16 on the way count: a program that leaves them out, or rounds other values in their place, can miss the bound.
Values may be sent and summed in bfloat16 or wider, within the bound.
A program may use at most 256 MiB of HBM per device.

```python
import math
import jax
import jax.numpy as jnp
from jax import lax

D = 384
NUM_SUBSPACES = 8
FF = 1536
SIDE = 24
RANK = 8
IMG_DEV = 3
IMAGES = 96
ROWS = 55296
N_DP = 16


def draw_image_size_class(key, part):
    key = jax.random.fold_in(key, 3)
    images = jnp.arange(IMAGES)
    device = images // IMG_DEV
    devices = IMAGES // IMG_DEV
    drawn = jax.random.randint(key, (IMAGES,), 0, 3)
    bucket = jnp.clip(drawn + 4 * device // devices - 1, 0, 2)
    bucket = jnp.where(images == 0, 0, bucket)
    bucket = jnp.where(images == IMAGES - 1, 2, bucket)
    return bucket.astype(jnp.int32)


def draw_loss_sensitivity(key, part):
    key = jax.random.fold_in(key, 5)
    devices = IMAGES // IMG_DEV
    position = (jnp.arange(ROWS) // (IMG_DEV * SIDE * SIDE)).astype(jnp.float32)
    slope = position / max(devices - 1, 1)
    values = jax.random.normal(key, (ROWS, D), jnp.float32)
    factor = 1.0 + 2.0 * slope
    return (values * factor[:, None]).astype(jnp.bfloat16)


def level_of(stream_key, dims, shards, smallest, high):
    loudness, own = 1.0, jax.random.fold_in(stream_key, 6)
    for axis_at, parts in shards:
        draws = jnp.exp(jax.random.uniform(jax.random.fold_in(own, axis_at), (parts,), jnp.float32, smallest / len(shards), high / len(shards)))
        loudness = loudness * jnp.repeat(draws, dims[axis_at] // parts).reshape([-1 if axis == axis_at else 1 for axis in range(len(dims))])
    return loudness


def centred(own_key, shape, deviation, limit, split=(), held_as=jnp.bfloat16):
    result = deviation * jax.random.normal(own_key, shape, jnp.float32)
    if split:
        result = result * level_of(own_key, shape, split, -0.22, 0.18)
    return jnp.clip(result, -limit, limit).astype(held_as)


def setup_inputs(seed: int = 0) -> dict:
    splits = jax.random.split(jax.random.key(seed), 34)
    return {
        "patch_embedding_grid": centred(splits[0], (ROWS, D), 1.0, 6.0, ((0, 32),)),
        "image_size_class": draw_image_size_class(jax.random.fold_in(splits[33], 71), 0),
        "loss_sensitivity": draw_loss_sensitivity(jax.random.fold_in(splits[33], 71), 0),
        "triple_coefficients": centred(splits[3], (D, 3 * D), D ** -0.5, 0.3125, ((1, 2),), jnp.float32),
        "triple_offset": centred(splits[4], (3 * D,), 0.3, 1.75, (), jnp.float32),
        "sharpness": jnp.clip(jnp.exp(jax.random.uniform(splits[5], (NUM_SUBSPACES,), jnp.float32, math.log(20.0), math.log(50.0))), 20.0, 50.0),
        "mapping_coefficients": centred(splits[6], (D, D), (D // 8) ** -0.5, 0.875, ((0, 2),), jnp.float32),
        "expansion_coefficients": centred(splits[7], (D, FF), D ** -0.5, 0.3125, ((1, 2),), jnp.float32),
        "expansion_offset": centred(splits[8], (FF,), 0.3, 1.75, (), jnp.float32),
        "contraction_coefficients": centred(splits[9], (FF, D), FF ** -0.5, 0.15625, ((0, 2),), jnp.float32),
        "normalizer_multipliers": jnp.clip(1.0 + 0.1 * jax.random.normal(splits[10], (4, D), jnp.float32), 0.5, 1.5),
        "offset_rows_all": centred(splits[11], (7, D), 0.3, 1.75, (), jnp.float32),
        "spatial_kernels": centred(splits[12], (18, D), 9 ** -0.5, 2.0, (), jnp.float32),
        "residual_multipliers": jnp.clip(1.0 + 0.1 * jax.random.normal(splits[13], (3, D), jnp.float32), 0.5, 1.5),
        "triple_velocity": centred(splits[14], (D, 3 * D), (0.05 * (IMG_DEV * 800) ** 0.5), 14.0, ((1, 2),), jnp.float32),
        "mapping_velocity": centred(splits[15], (D, D), (0.05 * (IMG_DEV * 800) ** 0.5), 14.0, ((0, 2),), jnp.float32),
        "expansion_velocity": centred(splits[16], (D, FF), (0.05 * (IMG_DEV * 800) ** 0.5), 14.0, ((1, 2),), jnp.float32),
        "contraction_velocity": centred(splits[17], (FF, D), (0.05 * (IMG_DEV * 800) ** 0.5), 14.0, ((0, 2),), jnp.float32),
        "triple_offset_velocity": centred(splits[18], (3 * D,), (0.05 * (IMG_DEV * 800) ** 0.5), 14.0, (), jnp.float32),
        "sharpness_velocity": centred(splits[19], (NUM_SUBSPACES,), 0.5, 3.0, (), jnp.float32),
        "expansion_offset_velocity": centred(splits[20], (FF,), 0.5, 3.0, (), jnp.float32),
        "multiplier_velocity": centred(splits[21], (4, D), 0.5, 3.0, (), jnp.float32),
        "offset_velocity": centred(splits[22], (7, D), 0.5, 3.0, (), jnp.float32),
        "kernel_velocity": centred(splits[23], (18, D), 0.5, 3.0, (), jnp.float32),
        "residual_multiplier_velocity": centred(splits[24], (3, D), 0.5, 3.0, (), jnp.float32),
        "triple_residual_buffer": centred(splits[25], (N_DP, D, 3 * D), (0.5 * (IMG_DEV * 800) ** 0.5), 128.0, ((0, 16), (2, 2)), jnp.float32),
        "mapping_residual_store": centred(splits[26], (N_DP, D, D), (0.5 * (IMG_DEV * 800) ** 0.5), 128.0, ((0, 16), (1, 2)), jnp.float32),
        "expansion_residual_store": centred(splits[27], (N_DP, D, FF), (0.5 * (IMG_DEV * 800) ** 0.5), 128.0, ((0, 16), (2, 2)), jnp.float32),
        "contraction_residual_store": centred(splits[28], (N_DP, FF, D), (0.5 * (IMG_DEV * 800) ** 0.5), 128.0, ((0, 16), (1, 2)), jnp.float32),
        "triple_right_factor": centred(splits[29], (3 * D, RANK), 1.0, 6.0, ((0, 2),), jnp.float32),
        "mapping_right_factor": centred(splits[30], (D, RANK), 1.0, 6.0, (), jnp.float32),
        "expansion_right_factor": centred(splits[31], (FF, RANK), 1.0, 6.0, ((0, 2),), jnp.float32),
        "contraction_right_factor": centred(splits[32], (D, RANK), 1.0, 6.0, (), jnp.float32),
    }


@jax.custom_vjp
def low(v):
    return lax.optimization_barrier(v.astype(jnp.bfloat16)).astype(jnp.float32)

@jax.custom_vjp
def low_back(v):
    return v

def low_keep(v):
    return (low(v), None)

def low_pass(kept, grad):
    return (grad,)

def back_keep(v):
    return (v, None)

def back_low(kept, grad):
    return (low(grad),)
low.defvjp(low_keep, low_pass)
low_back.defvjp(back_keep, back_low)
learn_rate = 0.02
momentum_decay = 0.9

def side_mask(image_size_class, side_len):
    sides = side_len * (7 + 2 * image_size_class + image_size_class // 2) // 12
    places = jnp.arange(side_len)
    inside = (places[None, :, None] < sides[:, None, None]) & (places[None, None, :] < sides[:, None, None])
    return inside.reshape(-1, 1).astype(jnp.float32)

def layer_norm(values, gain, shift):
    center = values - lax.optimization_barrier(jnp.mean(values, -1, keepdims=True))
    scale = lax.rsqrt(lax.optimization_barrier(jnp.mean(center * center, -1, keepdims=True)) + 1e-06)
    return center * scale * gain + shift

def matmul(left, right):
    return jnp.dot(left, right, precision=lax.Precision.HIGHEST)

def depthwise(field, taps):
    side_len = field.shape[1]
    padded = jnp.pad(field, ((0, 0), (1, 1), (1, 1), (0, 0)))
    total = jnp.zeros_like(field)
    for row_tap in range(3):
        for col_tap in range(3):
            total = total + taps[row_tap * 3 + col_tap] * padded[:, row_tap:row_tap + side_len, col_tap:col_tap + side_len, :]
    return total

def exact_gelu(values):
    return jax.nn.gelu(values, approximate=False)

def attention_part(tokens_g, mask_g, triple_piece_own, mapping_piece_own, learnable_collection):
    triple_offset, sharpness, expansion_offset, normalizer_multipliers, offset_rows_all, spatial_kernels, residual_multipliers = learnable_collection
    images = tokens_g.shape[0] // (SIDE * SIDE)
    head_dim = D // NUM_SUBSPACES
    masked = tokens_g * mask_g
    low_one = low(layer_norm(masked, normalizer_multipliers[0], offset_rows_all[0]) * mask_g)
    projected = low_back(matmul(low_one, low(triple_piece_own)) + triple_offset)
    grid = projected.reshape(images, SIDE * SIDE, NUM_SUBSPACES, 3, head_dim) * mask_g.reshape(images, SIDE * SIDE, 1, 1, 1)
    query = grid[:, :, :, 0]
    keys = grid[:, :, :, 1]
    values = grid[:, :, :, 2]
    query_unit = query * lax.rsqrt(lax.optimization_barrier(jnp.sum(query * query, 1, keepdims=True)) + 1e-06)
    key_unit = keys * lax.rsqrt(lax.optimization_barrier(jnp.sum(keys * keys, 1, keepdims=True)) + 1e-06)
    channel_covariance = jnp.einsum('inhc,inhd->ihcd', low(query_unit), low(key_unit), precision=lax.Precision.HIGHEST)
    cross_covariance_mixer = jax.nn.softmax(sharpness[None, :, None, None] * channel_covariance, axis=-1)
    mixed = jnp.einsum('ihcd,inhd->inhc', low(cross_covariance_mixer), low(values), precision=lax.Precision.HIGHEST)
    mixed_low = low(mixed.reshape(-1, D))
    branch = low_back(matmul(mixed_low, low(mapping_piece_own)) + offset_rows_all[4])
    first = masked + residual_multipliers[0] * branch * mask_g
    normed_two = layer_norm(first, normalizer_multipliers[1], offset_rows_all[1]) * mask_g
    conv = depthwise(normed_two.reshape(images, SIDE, SIDE, D), spatial_kernels[0:9]).reshape(-1, D)
    active = exact_gelu(conv) * mask_g
    return (first, active)

def mlp_part(first, active, mask_g, expansion_piece_own, contraction_piece_own, stats, learnable_collection):
    triple_offset, sharpness, expansion_offset, normalizer_multipliers, offset_rows_all, spatial_kernels, residual_multipliers = learnable_collection
    images = first.shape[0] // (SIDE * SIDE)
    bn_mean, bn_rstd = stats
    zhat = (active - bn_mean) * bn_rstd
    shifted = (zhat * normalizer_multipliers[2] + offset_rows_all[2]) * mask_g
    local = (depthwise(shifted.reshape(images, SIDE, SIDE, D), spatial_kernels[9:18]).reshape(-1, D) + offset_rows_all[5]) * mask_g
    second = first + residual_multipliers[1] * local
    low_three = low(layer_norm(second, normalizer_multipliers[3], offset_rows_all[3]) * mask_g)
    hidden_pre = low_back(matmul(low_three, low(expansion_piece_own)) + expansion_offset)
    hidden_low = low(exact_gelu(hidden_pre))
    branch = low_back(matmul(hidden_low, low(contraction_piece_own)) + offset_rows_all[6])
    return second + residual_multipliers[2] * branch * mask_g

def evaluate_block(patch_embeddings, triple_piece_own, mapping_piece_own, expansion_piece_own, contraction_piece_own, triple_offset, sharpness, expansion_offset, normalizer_multipliers, offset_rows_all, spatial_kernels, residual_multipliers, patch_validity):
    learnable_collection = (triple_offset, sharpness, expansion_offset, normalizer_multipliers, offset_rows_all, spatial_kernels, residual_multipliers)
    group_rows = ROWS // N_DP
    tokens_g = patch_embeddings.reshape(N_DP, group_rows, D)
    mask_g = patch_validity.reshape(N_DP, group_rows, 1)
    section_one = jax.checkpoint(lambda items: attention_part(items[0], items[1], items[2], items[3], learnable_collection))
    first, active = lax.map(section_one, (tokens_g, mask_g, triple_piece_own, mapping_piece_own))
    count = jnp.sum(patch_validity)
    bn_mean = lax.optimization_barrier(jnp.sum(active, (0, 1))) / count
    bn_var = lax.optimization_barrier(jnp.sum(active * active, (0, 1))) / count - bn_mean * bn_mean
    bn_rstd = lax.rsqrt(bn_var + 1e-05)
    section_two = jax.checkpoint(lambda items: mlp_part(items[0], items[1], items[2], items[3], items[4], (bn_mean, bn_rstd), learnable_collection))
    block_result = lax.map(section_two, (first, active, mask_g, expansion_piece_own, contraction_piece_own))
    return block_result.reshape(ROWS, D)

def orthonormal(left):
    columns = []
    for index in range(left.shape[1]):
        column = left[:, index]
        for done in columns:
            column = column - jnp.sum(done * column) * done
        column = column * lax.rsqrt(jnp.sum(column * column) + 1e-06)
        columns.append(column)
    return jnp.stack(columns, 1)

def compress(grads_r, errors, basis, moment, weight):
    full = grads_r + errors
    left = jnp.einsum('rab,bk->ak', full, basis, precision=lax.Precision.HIGHEST)
    ortho = orthonormal(left)
    right = jnp.einsum('rab,ak->bk', full, ortho, precision=lax.Precision.HIGHEST) / N_DP
    approx = matmul(ortho, right.T)
    new_moment = momentum_decay * moment + approx
    return (weight - learn_rate * new_moment, new_moment, full - approx[None], right)

def plain_descent_step(grad, moment, weight):
    new_moment = momentum_decay * moment + grad / N_DP
    return (weight - learn_rate * new_moment, new_moment)

def reference(patch_embedding_grid, image_size_class, loss_sensitivity, triple_coefficients, triple_offset, sharpness, mapping_coefficients, expansion_coefficients, expansion_offset, contraction_coefficients, normalizer_multipliers, offset_rows_all, spatial_kernels, residual_multipliers, triple_velocity, mapping_velocity, expansion_velocity, contraction_velocity, triple_offset_velocity, sharpness_velocity, expansion_offset_velocity, multiplier_velocity, offset_velocity, kernel_velocity, residual_multiplier_velocity, triple_residual_buffer, mapping_residual_store, expansion_residual_store, contraction_residual_store, triple_right_factor, mapping_right_factor, expansion_right_factor, contraction_right_factor):
    patch_validity = side_mask(image_size_class, SIDE)

    def complete_assembled(patch_embeddings, triple_piece_own, mapping_piece_own, expansion_piece_own, contraction_piece_own, bias_qkv, temper, bias_in, gain_rows, bias_rows, taps, scales):
        return evaluate_block(patch_embeddings, triple_piece_own, mapping_piece_own, expansion_piece_own, contraction_piece_own, bias_qkv, temper, bias_in, gain_rows, bias_rows, taps, scales, patch_validity)
    triple_all_pieces = jnp.broadcast_to(triple_coefficients, (N_DP,) + triple_coefficients.shape)
    mapping_all_pieces = jnp.broadcast_to(mapping_coefficients, (N_DP,) + mapping_coefficients.shape)
    expansion_all_pieces = jnp.broadcast_to(expansion_coefficients, (N_DP,) + expansion_coefficients.shape)
    contraction_all_pieces = jnp.broadcast_to(contraction_coefficients, (N_DP,) + contraction_coefficients.shape)
    block_result, reverse_mode_rule = jax.vjp(complete_assembled, patch_embedding_grid.astype(jnp.float32), triple_all_pieces, mapping_all_pieces, expansion_all_pieces, contraction_all_pieces, triple_offset, sharpness, expansion_offset, normalizer_multipliers, offset_rows_all, spatial_kernels, residual_multipliers)
    derivative_collection = reverse_mode_rule(loss_sensitivity.astype(jnp.float32))
    triple_piece_own, next_triple_velocity, triple_residual_store, triple_offset_vec = compress(derivative_collection[1], triple_residual_buffer, triple_right_factor, triple_velocity, triple_coefficients)
    mapping_piece_own, next_mapping_velocity, mapped_residual_store, mapped_offset_vec = compress(derivative_collection[2], mapping_residual_store, mapping_right_factor, mapping_velocity, mapping_coefficients)
    expansion_piece_own, next_expansion_velocity, raised_residual_store, raised_offset_vec = compress(derivative_collection[3], expansion_residual_store, expansion_right_factor, expansion_velocity, expansion_coefficients)
    contraction_piece_own, next_contraction_velocity, lowered_residual_store, lowered_offset_vec = compress(derivative_collection[4], contraction_residual_store, contraction_right_factor, contraction_velocity, contraction_coefficients)
    next_triple_offset, next_triple_offset_velocity = plain_descent_step(derivative_collection[5], triple_offset_velocity, triple_offset)
    sharpness_running_square, sharpness_running_mean = plain_descent_step(derivative_collection[6], sharpness_velocity, sharpness)
    next_expansion_offset, next_expansion_offset_velocity = plain_descent_step(derivative_collection[7], expansion_offset_velocity, expansion_offset)
    next_multipliers, next_multiplier_velocity = plain_descent_step(derivative_collection[8], multiplier_velocity, normalizer_multipliers)
    next_offsets, next_offset_velocity = plain_descent_step(derivative_collection[9], offset_velocity, offset_rows_all)
    next_kernels, next_kernel_velocity = plain_descent_step(derivative_collection[10], kernel_velocity, spatial_kernels)
    next_residual_multipliers, next_residual_multiplier_velocity = plain_descent_step(derivative_collection[11], residual_multiplier_velocity, residual_multipliers)
    return (block_result.astype(jnp.bfloat16), derivative_collection[0].astype(jnp.bfloat16), triple_piece_own, mapping_piece_own, expansion_piece_own, contraction_piece_own, next_triple_offset, sharpness_running_square, next_expansion_offset, next_multipliers, next_offsets, next_kernels, next_residual_multipliers, next_triple_velocity, next_mapping_velocity, next_expansion_velocity, next_contraction_velocity, next_triple_offset_velocity, sharpness_running_mean, next_expansion_offset_velocity, next_multiplier_velocity, next_offset_velocity, next_kernel_velocity, next_residual_multiplier_velocity, triple_residual_store, mapped_residual_store, raised_residual_store, lowered_residual_store, triple_offset_vec, mapped_offset_vec, raised_offset_vec, lowered_offset_vec)
```

```python
import numpy as np
import jax
import jax.numpy as jnp
from jax import lax
from jax.experimental import pallas as pl
from jax.experimental.pallas import tpu as pltpu
from jax.sharding import PartitionSpec as P

SIDE = 24
GROUPS = 8
TRIO = 3
LANES = 128
NEAR = 4
learn_rate = 0.02
momentum_decay = 0.9
f32 = jnp.float32
bf16 = jnp.bfloat16
MESH = pl.DeviceIdType.MESH
VMEM_BYTES = 58 << 20
HALF_ROOT = 0.7071067811865476
GAUSS = 0.3989422804014327


def sds(shape, dtype=f32):
    return jax.ShapeDtypeStruct(shape, dtype)


def params(**kw):
    return pltpu.CompilerParams(vmem_limit_bytes=VMEM_BYTES, **kw)


def dg(a, b, ca, cb, precision=None):
    return lax.dot_general(
        a, b, (((ca,), (cb,)), ((), ())), preferred_element_type=f32, precision=precision
    )


def dgh(a, b, ca, cb):
    return dg(a, b, ca, cb, lax.Precision.HIGHEST)


def cat3(m):
    return jnp.concatenate([m, m, m], -1)


def split2(x):
    hi = x.astype(bf16)
    return hi, (x - hi.astype(f32)).astype(bf16)


def split3(x):
    hi = x.astype(bf16)
    rest = x - hi.astype(f32)
    mid = rest.astype(bf16)
    return hi, mid, (rest - mid.astype(f32)).astype(bf16)


def dg2(a, b, ca, cb):
    hi, lo = split2(a)
    return dg(hi, b, ca, cb) + dg(lo, b, ca, cb)


def mean_of(x):
    return jnp.sum(x, -1, keepdims=True) * (1.0 / x.shape[-1])


def layer_stats(x):
    center = x - mean_of(x)
    scale = lax.rsqrt(mean_of(center * center) + 1e-06)
    return center * scale, scale


def norm_back(grad_out, normed, scale, gain):
    grad_normed = grad_out * gain
    return scale * (
        grad_normed - mean_of(grad_normed) - normed * mean_of(grad_normed * normed)
    )


def colsum(x):
    return jnp.sum(x.reshape(x.shape[0] // 8, 8, x.shape[1]), 0)


def rowsum(x):
    return jnp.sum(x, 0, keepdims=True)


def gelu_pair(x):
    phi = 0.5 + 0.5 * lax.erf(x * HALF_ROOT)
    return x * phi, phi + x * jnp.exp(-0.5 * x * x) * GAUSS


def side_of(cls_ref, index):
    bucket = cls_ref[index]
    return SIDE * (7 + 2 * bucket + lax.div(bucket, 2)) // 12


def fill_mask(mask, side):
    shape = (SIDE, GROUPS, LANES)
    col = lax.broadcasted_iota(jnp.int32, shape, 0)
    group = lax.broadcasted_iota(jnp.int32, shape, 1)
    for m in range(TRIO):
        inside = (group * TRIO + m < side) & (col < side)
        mask[pl.ds(m * SIDE, SIDE)] = jnp.where(inside, 1.0, 0.0).astype(f32)


def to_canvas(src, nat, dst):
    per = TRIO * SIDE
    for l in range(3):
        nat[l] = src[:, l * LANES : (l + 1) * LANES].astype(f32)
    for j in range(per):
        for l in range(3):
            dst[pl.ds(j * 8, 8), l * LANES : (l + 1) * LANES] = nat[
                l, pl.ds(j, GROUPS, stride=per), :
            ]


def from_canvas(value, nat, dst):
    per = TRIO * SIDE
    for j in range(per):
        for l in range(3):
            nat[l, pl.ds(j, GROUPS, stride=per), :] = value[
                j * 8 : j * 8 + 8, l * LANES : (l + 1) * LANES
            ]
    for l in range(3):
        dst[:, l * LANES : (l + 1) * LANES] = nat[l].astype(bf16)


def clear_edges(field):
    zero = jnp.zeros((TRIO + 2, 1, GROUPS, field.shape[-1]), f32)
    field[:, 0:1] = zero
    field[:, SIDE + 1 : SIDE + 2] = zero


def put_field(field, value):
    v = value.reshape(TRIO, SIDE, GROUPS, value.shape[-1])
    group = lax.broadcasted_iota(jnp.int32, (SIDE, GROUPS, value.shape[-1]), 1)
    field[1 : TRIO + 1, 1 : SIDE + 1] = v
    field[0, 1 : SIDE + 1] = jnp.where(group == 0, 0.0, pltpu.roll(v[TRIO - 1], 1, 1))
    field[TRIO + 1, 1 : SIDE + 1] = jnp.where(
        group == GROUPS - 1, 0.0, pltpu.roll(v[0], GROUPS - 1, 1)
    )


def conv_chunk(win, weights, width, flip):
    total = None
    for a in range(3):
        for b in range(3):
            ra, rb = (2 - a, 2 - b) if flip else (a, b)
            term = weights[3 * a + b] * win[ra : ra + TRIO, rb : rb + width]
            total = term if total is None else total + term
    return total


def tap_rows(taps, first, lanes):
    return [
        jnp.broadcast_to(taps[first + k : first + k + 1, lanes], (GROUPS, LANES)) for k in range(9)
    ]


CHUNK = 6


def conv_loop(visit):
    for l in range(3):
        lanes = slice(l * LANES, (l + 1) * LANES)
        visit(l, lanes)


def weights_kernel(tri, mapw, expw, conw, perm, wt, wp, win, wout, send, recv):
    t = lax.axis_index("tensor")
    other = {"tensor": 1 - t}
    barrier = pltpu.get_barrier_semaphore()
    pl.semaphore_signal(barrier, inc=1, device_id=other, device_id_type=MESH)
    turned = dg(perm[...], tri[...].astype(bf16), 1, 1).astype(bf16)
    part = turned.shape[0] // 3
    for j in range(3):
        wt[j, t] = turned[j * part : (j + 1) * part]
    wp[t] = mapw[...].astype(bf16)
    win[t] = expw[...].astype(bf16)
    wout[t] = conw[...].astype(bf16)
    pl.semaphore_wait(barrier, 1)
    spots = [wt.at[0], wt.at[1], wt.at[2], wp, win, wout]
    copies = []
    for k, ref in enumerate(spots):
        out = pltpu.make_async_remote_copy(
            src_ref=ref.at[t],
            dst_ref=ref.at[t],
            send_sem=send.at[k],
            recv_sem=recv.at[k],
            device_id=other,
            device_id_type=MESH,
        )
        out.start()
        copies.append(out)
    for k, ref in enumerate(spots):
        copies[k].wait_send()
        pltpu.make_async_remote_copy(
            src_ref=ref.at[1 - t],
            dst_ref=ref.at[1 - t],
            send_sem=send.at[k],
            recv_sem=recv.at[k],
            device_id=other,
            device_id_type=MESH,
        ).wait_recv()


def near_partner(me, hi, k):
    index = lax.rem(me + k, 2 * NEAR)
    return index, {"dp": hi * NEAR + lax.div(index, 2), "tensor": lax.rem(index, 2)}


def place():
    dp = lax.axis_index("dp")
    t = lax.axis_index("tensor")
    hi = lax.div(dp, NEAR)
    lo = lax.rem(dp, NEAR)
    return hi, lo, t, lo * 2 + t


def greet(far):
    hi, lo, t, me = place()
    barrier = pltpu.get_barrier_semaphore()
    for k in range(1, 2 * NEAR):
        pl.semaphore_signal(
            barrier, inc=1, device_id=near_partner(me, hi, k)[1], device_id_type=MESH
        )
    for k in range(1, far):
        there = {"dp": lax.rem(hi + k, far) * NEAR + lo, "tensor": t}
        pl.semaphore_signal(barrier, inc=1, device_id=there, device_id_type=MESH)


def met(far):
    pl.semaphore_wait(pltpu.get_barrier_semaphore(), 2 * NEAR - 1 + far - 1)


def remote(src, dst, send, recv, there):
    return pltpu.make_async_remote_copy(
        src_ref=src, dst_ref=dst, send_sem=send, recv_sem=recv, device_id=there, device_id_type=MESH
    )


def far_partner(hi, lo, t, k, far):
    index = lax.rem(hi + k, far)
    return index, {"dp": index * NEAR + lo, "tensor": t}


def small_sum_kernel(far, x, o, slots, part, tops, s1, r1, s2, r2):
    hi, lo, t, me = place()
    greet(far)
    slots[me] = x[...]
    met(far)
    out = []
    for k in range(1, 2 * NEAR):
        index, there = near_partner(me, hi, k)
        c = remote(x, slots.at[me], s1.at[k], r1.at[me], there)
        c.start()
        out.append(c)
    for k in range(1, 2 * NEAR):
        index, there = near_partner(me, hi, k)
        remote(x, slots.at[index], s1.at[k], r1.at[index], there).wait_recv()
    total = slots[0]
    for k in range(1, 2 * NEAR):
        total = total + slots[k]
    part[...] = total
    tops[hi] = total
    for k in range(1, far):
        index, there = far_partner(hi, lo, t, k, far)
        c = remote(part, tops.at[hi], s2.at[k], r2.at[hi], there)
        c.start()
        out.append(c)
    for k in range(1, far):
        index, there = far_partner(hi, lo, t, k, far)
        remote(part, tops.at[index], s2.at[k], r2.at[index], there).wait_recv()
    total = tops[0]
    for k in range(1, far):
        total = total + tops[k]
    o[...] = total
    for c in out:
        c.wait_send()


def small_sum(x, far, ident):
    import functools

    return pl.pallas_call(
        functools.partial(small_sum_kernel, far),
        out_shape=sds((8, LANES)),
        in_specs=[pl.BlockSpec(memory_space=pltpu.VMEM)],
        out_specs=pl.BlockSpec(memory_space=pltpu.VMEM),
        scratch_shapes=[
            pltpu.VMEM((2 * NEAR, 8, LANES), f32),
            pltpu.VMEM((8, LANES), f32),
            pltpu.VMEM((far, 8, LANES), f32),
            pltpu.SemaphoreType.DMA((2 * NEAR,)),
            pltpu.SemaphoreType.DMA((2 * NEAR,)),
            pltpu.SemaphoreType.DMA((far,)),
            pltpu.SemaphoreType.DMA((far,)),
        ],
        compiler_params=params(collective_id=ident, has_side_effects=True),
        name="small_sum",
    )(x)


def batch_stats(st):
    row = lambda r: jnp.concatenate([st[r : r + 1, :], st[r + 1 : r + 2, :], st[r + 2 : r + 3, :]], -1)
    inv = cat3(1.0 / st[6:7, :])
    mean = row(0) * inv
    var = row(3) * inv - mean * mean
    return mean, lax.rsqrt(var + 1e-05), inv


def first_kernel(
    cls, sharp, tok, wt, bq, wp, gains, offs, taps, scales,
    first_o, active_o, dgelu_o, low_o, q_o, k_o, v_o, mix_o, attn_o, gram_o, rs_o, stat_o,
    nat, mask, xm, field, sharp_rows, off_block, sums,
):
    i = pl.program_id(0)
    t = lax.axis_index("tensor")
    own = cls.shape[0] // 2
    heads = sharp.shape[0]
    width = tok.shape[1]
    head = width // heads

    @pl.when(i == 0)
    def _():
        lane = lax.broadcasted_iota(jnp.int32, (head, width), 1)
        for h in range(heads):
            inside = (lane >= h * head) & (lane < (h + 1) * head)
            sharp_rows[h * head : (h + 1) * head, :] = jnp.where(inside, sharp[h], 0.0)
            off_block[h * head : (h + 1) * head, :] = jnp.where(inside, 0.0, -1e30)
        clear_edges(field)
        sums[...] = jnp.zeros_like(sums)

    fill_mask(mask, side_of(cls, t * own + i))
    mk = cat3(mask[...].reshape(-1, LANES))
    to_canvas(tok, nat, xm)
    x = xm[...] * mk
    normed, _ = layer_stats(x)
    low = ((normed * gains[0:1, :] + offs[0:1, :]) * mk).astype(bf16)
    low_o[...] = low
    lows = []
    for j in range(2):
        value = (dg(low, wt[j], 1, 1) + bq[j : j + 1, :]) * mk
        scale = lax.rsqrt(rowsum(value * value) + 1e-06)
        rs_o[0, j : j + 1, :] = scale
        unit = (value * scale).astype(bf16)
        (q_o, k_o)[j][...] = unit
        lows.append(unit)
    value_low = ((dg(low, wt[2], 1, 1) + bq[2:3, :]) * mk).astype(bf16)
    v_o[...] = value_low
    gram = dg(lows[0], lows[1], 0, 0)
    gram_o[0] = gram
    logits = gram * sharp_rows[...] + off_block[...]
    powers = jnp.exp(logits - jnp.max(logits, -1, keepdims=True))
    attn = powers / jnp.sum(powers, -1, keepdims=True)
    attn_o[0] = attn
    mixed = dg(value_low, attn.astype(bf16), 1, 1).astype(bf16)
    mix_o[...] = mixed
    branch = dg(mixed, wp[...], 1, 0) + offs[4:5, :]
    first = xm[...] * mk + scales[0:1, :] * branch * mk
    first_o[...] = first
    normed, _ = layer_stats(first)
    put_field(field, (normed * gains[1:2, :] + offs[1:2, :]) * mk)
    for l in range(3):
        lanes = slice(l * LANES, (l + 1) * LANES)
        w = tap_rows(taps, 0, lanes)
        tot = jnp.zeros((8, LANES), f32)
        sq = jnp.zeros((8, LANES), f32)
        for c0 in range(0, SIDE, CHUNK):
            conv = conv_chunk(field[:, c0 : c0 + CHUNK + 2, :, lanes], w, CHUNK, False)
            act, back = gelu_pair(conv)
            for m in range(TRIO):
                rows = slice((m * SIDE + c0) * 8, (m * SIDE + c0 + CHUNK) * 8)
                am = act[m] * mask[m * SIDE + c0 : m * SIDE + c0 + CHUNK]
                active_o[rows, lanes] = am.reshape(CHUNK * 8, LANES)
                dgelu_o[rows, lanes] = back[m].reshape(CHUNK * 8, LANES)
                tot = tot + jnp.sum(am, 0)
                sq = sq + jnp.sum(am * am, 0)
        sums[0, :, lanes] += tot
        sums[1, :, lanes] += sq

    @pl.when(i == own - 1)
    def _():
        cells = 0
        for n in range(own):
            s = side_of(cls, t * own + n)
            cells = cells + s * s
        for k in range(2):
            row = rowsum(sums[k])
            for l in range(3):
                stat_o[3 * k + l : 3 * k + l + 1, :] = row[:, l * LANES : (l + 1) * LANES]
        stat_o[6:8, :] = jnp.full((2, LANES), 1.0, f32) * cells.astype(f32)


def middle_kernel(
    cls, first, active, loss, st, win, wout, bin_, gains, offs, taps, scales,
    out_o, gsec_o, gsh_o, gin_o, gout_o, vec_o, inb_o, stat_o,
    nat, mask, field, gfield, loc, go, macc, gacc, l3s, gms, hs, gs, acc, inb,
):
    i = pl.program_id(0)
    t = lax.axis_index("tensor")
    own = cls.shape[0] // 2
    rows_n = first.shape[0]
    hidden = win.shape[0] * win.shape[2]
    half = win.shape[2]

    @pl.when(i == 0)
    def _():
        clear_edges(field)
        clear_edges(gfield)
        acc[...] = jnp.zeros_like(acc)
        inb[...] = jnp.zeros_like(inb)

    fill_mask(mask, side_of(cls, t * own + i))
    mk = cat3(mask[...].reshape(-1, LANES))
    mean, rstd, _ = batch_stats(st)
    zhat = (active[...] - mean) * rstd
    put_field(field, (zhat * gains[2:3, :] + offs[2:3, :]) * mk)
    for l in range(3):
        lanes = slice(l * LANES, (l + 1) * LANES)
        w = tap_rows(taps, 9, lanes)
        bias = offs[5:6, lanes]
        for c0 in range(0, SIDE, CHUNK):
            conv = conv_chunk(field[:, c0 : c0 + CHUNK + 2, :, lanes], w, CHUNK, False)
            for m in range(TRIO):
                rows = slice((m * SIDE + c0) * 8, (m * SIDE + c0 + CHUNK) * 8)
                value = (conv[m] + bias) * mask[m * SIDE + c0 : m * SIDE + c0 + CHUNK]
                loc[rows, lanes] = value.reshape(CHUNK * 8, LANES)
    second = first[...] + scales[1:2, :] * loc[...]
    normed, _ = layer_stats(second)
    base = pl.multiple_of(i * rows_n, 16)
    l3 = ((normed * gains[3:4, :] + offs[3:4, :]) * mk).astype(bf16)
    l3s[pl.ds(base, rows_n), :] = l3
    to_canvas(loss, nat, go)
    grad_out = go[...] * mk
    go[...] = grad_out
    gm = (grad_out * scales[2:3, :]).astype(bf16)
    gms[pl.ds(base, rows_n), :] = gm
    acc[3] += colsum(gm.astype(f32))

    step = 384
    for n in range(hidden // step):
        hf, cols = n * step // half, slice(n * step % half, n * step % half + step)
        allc = slice(n * step, (n + 1) * step)
        pre = dg(l3s[pl.ds(base, rows_n), :], win[hf, :, cols], 1, 0) + bin_[n : n + 1, :]
        act, back = gelu_pair(pre)
        h = act.astype(bf16)
        hs[pl.ds(base, rows_n), allc] = h
        g = (dg(gms[pl.ds(base, rows_n), :], wout[hf, cols, :], 1, 1) * back).astype(bf16)
        gs[pl.ds(base, rows_n), allc] = g
        inb[:, allc] += colsum(g.astype(f32))
        m_part = dg(h, wout[hf, cols, :], 1, 0)
        g_part = dg(g, win[hf, :, cols], 1, 1)
        if n == 0:
            macc[...] = m_part
            gacc[...] = g_part
        else:
            macc[...] += m_part
            gacc[...] += g_part

    mlp = macc[...] + offs[6:7, :]
    second = first[...] + scales[1:2, :] * loc[...]
    from_canvas(second + scales[2:3, :] * mlp * mk, nat, out_o)
    acc[5] += colsum(go[...] * mlp)
    normed, scale = layer_stats(second)
    dout = gacc[...] * mk
    acc[0] += colsum(dout)
    acc[1] += colsum(dout * normed)
    gsec = go[...] + norm_back(dout, normed, scale, gains[3:4, :])
    gsec_o[...] = gsec
    acc[4] += colsum(gsec * loc[...])
    glocal = gsec * scales[1:2, :] * mk
    acc[2] += colsum(glocal)
    put_field(gfield, glocal)
    for l in range(3):
        lanes = slice(l * LANES, (l + 1) * LANES)
        w = tap_rows(taps, 9, lanes)
        tot = jnp.zeros((8, LANES), f32)
        cross = jnp.zeros((8, LANES), f32)
        tap_sum = [jnp.zeros((8, LANES), f32) for _ in range(9)]
        for c0 in range(0, SIDE, CHUNK):
            gwin = gfield[:, c0 : c0 + CHUNK + 2, :, lanes]
            fwin = field[:, c0 : c0 + CHUNK + 2, :, lanes]
            conv = conv_chunk(gwin, w, CHUNK, True)
            center = gwin[1 : 1 + TRIO, 1 : 1 + CHUNK]
            for a in range(3):
                for b in range(3):
                    prod = fwin[a : a + TRIO, b : b + CHUNK] * center
                    tap_sum[3 * a + b] += jnp.sum(prod, (0, 1))
            for m in range(TRIO):
                rows = slice((m * SIDE + c0) * 8, (m * SIDE + c0 + CHUNK) * 8)
                value = conv[m] * mask[m * SIDE + c0 : m * SIDE + c0 + CHUNK]
                flat = value.reshape(CHUNK * 8, LANES)
                gsh_o[rows, lanes] = flat
                z = (active[rows, lanes] - mean[:, lanes]) * rstd[:, lanes]
                tot = tot + jnp.sum(value, 0)
                cross = cross + colsum(flat * z)
        acc[6, :, lanes] += cross
        acc[7, :, lanes] += tot
        for k in range(9):
            acc[8 + k, :, lanes] += tap_sum[k]

    @pl.when(i == own - 1)
    def _():
        vec_o[...] = jnp.zeros_like(vec_o)
        for k in range(17):
            vec_o[k : k + 1, :] = rowsum(acc[k])
        inb_o[...] = jnp.zeros_like(inb_o)
        for k in range(hidden // 256):
            inb_o[k : k + 1, :] = rowsum(inb[:, k * 256 : (k + 1) * 256])
        cross, tot = rowsum(acc[6]), rowsum(acc[7])
        for l in range(3):
            lanes = slice(l * LANES, (l + 1) * LANES)
            stat_o[l : l + 1, :] = tot[:, lanes]
            stat_o[3 + l : 4 + l, :] = cross[:, lanes]
        stat_o[6:8, :] = jnp.zeros((2, LANES), f32)
        l3_t = l3s[...].T
        gm_t = gms[...].T
        for hf in range(2):
            cols = slice(hf * half, (hf + 1) * half)
            gin_o[hf] = dg(l3_t, gs[:, cols], 1, 0)
            gout_o[hf] = dg(gm_t, hs[:, cols], 1, 0)


def last_kernel(
    cls, sharp, tok, first, active, dgelu, gsec, gsh, low, q, k, v, mix, attn, gram, rs,
    st, gst, wt, wp, perm, gains, offs, taps, scales,
    ingrad_o, gt_o, gp_o, vec_o, qb_o,
    nat, mask, xm, field, gfield, gback, gfirst, gproj, acc, bias_acc, sharp_rows,
):
    i = pl.program_id(0)
    t = lax.axis_index("tensor")
    own = cls.shape[0] // 2
    heads = sharp.shape[0]
    width = tok.shape[1]
    head = width // heads

    @pl.when(i == 0)
    def _():
        lane = lax.broadcasted_iota(jnp.int32, (head, width), 1)
        for h in range(heads):
            sharp_rows[h * head : (h + 1) * head, :] = jnp.full((head, width), 1.0, f32) * sharp[h]
        clear_edges(field)
        clear_edges(gfield)
        acc[...] = jnp.zeros_like(acc)
        bias_acc[...] = jnp.zeros_like(bias_acc)

    fill_mask(mask, side_of(cls, t * own + i))
    mk = cat3(mask[...].reshape(-1, LANES))
    mean, rstd, inv = batch_stats(st)
    gsum = lambda r: jnp.concatenate([gst[r : r + 1, :], gst[r + 1 : r + 2, :], gst[r + 2 : r + 3, :]], -1)
    gain_bn = gains[2:3, :]
    zhat = (active[...] - mean) * rstd
    gact = rstd * (gsh[...] * gain_bn - gsum(0) * gain_bn * inv - zhat * (gsum(3) * gain_bn * inv)) * mk
    put_field(gfield, gact * dgelu[...])
    normed, scale = layer_stats(first[...])
    put_field(field, (normed * gains[1:2, :] + offs[1:2, :]) * mk)
    for l in range(3):
        lanes = slice(l * LANES, (l + 1) * LANES)
        w = tap_rows(taps, 0, lanes)
        tap_sum = [jnp.zeros((8, LANES), f32) for _ in range(9)]
        for c0 in range(0, SIDE, CHUNK):
            gwin = gfield[:, c0 : c0 + CHUNK + 2, :, lanes]
            fwin = field[:, c0 : c0 + CHUNK + 2, :, lanes]
            conv = conv_chunk(gwin, w, CHUNK, True)
            center = gwin[1 : 1 + TRIO, 1 : 1 + CHUNK]
            for a in range(3):
                for b in range(3):
                    prod = fwin[a : a + TRIO, b : b + CHUNK] * center
                    tap_sum[3 * a + b] += jnp.sum(prod, (0, 1))
            for m in range(TRIO):
                rows = slice((m * SIDE + c0) * 8, (m * SIDE + c0 + CHUNK) * 8)
                value = conv[m] * mask[m * SIDE + c0 : m * SIDE + c0 + CHUNK]
                gback[rows, lanes] = value.reshape(CHUNK * 8, LANES)
        for n in range(9):
            acc[7 + n, :, lanes] += tap_sum[n]
    dout = gback[...]
    normed, scale = layer_stats(first[...])
    acc[2] += colsum(dout * normed)
    acc[3] += colsum(dout)
    grad = gsec[...] + norm_back(dout, normed, scale, gains[1:2, :])
    gfirst[...] = grad
    to_canvas(tok, nat, xm)
    x = xm[...] * mk
    xm[...] = x
    acc[5] += colsum(grad * (first[...] - x))
    gal = (grad * scales[0:1, :] * mk).astype(bf16)
    acc[4] += colsum(gal.astype(f32))
    gp = dg(mix[...], gal, 0, 0)
    gmix = dg(gal, wp[...], 1, 1)
    ghi, glo = split2(gmix)
    gattn = dg(ghi, v[...], 0, 0) + dg(glo, v[...], 0, 0)
    a_low = attn[0].astype(bf16)
    gval = dg(ghi, a_low, 1, 0) + dg(glo, a_low, 1, 0)
    gsc = attn[0] * (gattn - jnp.sum(gattn * attn[0], -1, keepdims=True))
    sharp_full = sharp_rows[...]
    weighted = gsc * gram[0]
    ones = jnp.ones((8, width), bf16)
    chan = None
    for piece in split3(weighted):
        term = dg(ones, piece, 1, 1)
        chan = term if chan is None else chan + term
    chan = chan[0:1, :]
    acc[6, 0:1, :] += chan
    lane1 = lax.broadcasted_iota(jnp.int32, (1, width), 1)
    sharp_lane = jnp.zeros((1, width), f32)
    for h in range(heads):
        sharp_lane = jnp.where((lane1 >= h * head) & (lane1 < (h + 1) * head), sharp[h], sharp_lane)
    shi, slo = split2(gsc * sharp_full)
    gqu = dg(k[...], shi, 1, 1) + dg(k[...], slo, 1, 1)
    gku = dg(q[...], shi, 1, 0) + dg(q[...], slo, 1, 0)
    gq = rs[0, 0:1, :] * (gqu - q[...].astype(f32) * (chan * sharp_lane))
    gk = rs[0, 1:2, :] * (gku - k[...].astype(f32) * rowsum(weighted * sharp_full))
    low_t = low[...].T
    for j, piece in enumerate((gq, gk, gval)):
        small = piece.astype(bf16)
        gproj[:, j * width : (j + 1) * width] = small
        bias_acc[j] += colsum(small.astype(f32))
        gt = dg(small, low[...], 0, 0)

        @pl.when(i == 0)
        def _():
            gt_o[j] = gt

        @pl.when(i > 0)
        def _():
            gt_o[j] += gt

    @pl.when(i == 0)
    def _():
        gp_o[...] = gp

    @pl.when(i > 0)
    def _():
        gp_o[...] += gp

    dout = dg(gproj[...], wt[...].reshape(3 * width, width), 1, 0) * mk
    normed, scale = layer_stats(xm[...])
    acc[0] += colsum(dout * normed)
    acc[1] += colsum(dout)
    result = (gfirst[...] + norm_back(dout, normed, scale, gains[0:1, :])) * mk
    from_canvas(result, nat, ingrad_o)

    @pl.when(i == own - 1)
    def _():
        for n in range(16):
            vec_o[n : n + 1, :] = rowsum(acc[n])
        vec_o[5:6, :] = rowsum(acc[5]) / scales[0:1, :]
        qb_o[...] = jnp.zeros_like(qb_o)
        part = perm.shape[0] // 3
        lane8 = lax.broadcasted_iota(jnp.int32, (8, width), 1)
        for hf in range(2):
            total = None
            for j in range(3):
                rows = perm[j * part : (j + 1) * part, :]
                both = jnp.concatenate([rows, rows], 0)
                mine = jnp.where((lane8 >= hf * part) & (lane8 < (hf + 1) * part), bias_acc[j], 0.0)
                for piece in split3(mine):
                    term = dg(piece, both, 1, 0)
                    total = term if total is None else total + term
            row = rowsum(total)
            full_tiles = row.shape[1] // LANES
            for n in range(full_tiles):
                qb_o[hf * 8 + n : hf * 8 + n + 1, :] = row[:, n * LANES : (n + 1) * LANES]
            rest = row.shape[1] - full_tiles * LANES
            qb_o[hf * 8 + full_tiles : hf * 8 + full_tiles + 1, 0:rest] = row[:, full_tiles * LANES :]


def orthonormal(rows):
    index = lax.broadcasted_iota(jnp.int32, rows[0].shape[:1] + (1,), 0)
    rank = rows[0].shape[0]
    for n in range(rank):
        done = []
        for v in rows:
            column = v[n : n + 1, :]
            size = jnp.sum(column * column, -1, keepdims=True)
            unit = column * lax.rsqrt(size + 1e-06)
            dots = jnp.sum(v * unit, -1, keepdims=True)
            later = v - dots * unit
            done.append(jnp.where(index > n, later, jnp.where(index == n, unit, v)))
        rows = done
    return rows


def big_sum(pay, slots, part, tops, full, sems, far, rows):
    s1, r1, s2, r2, s3, r3 = sems
    hi, lo, t, me = place()
    count = 2 * NEAR
    out = []
    for k in range(1, count):
        index, there = near_partner(me, hi, k)
        c = remote(pay.at[index], slots.at[me], s1.at[k], r1.at[me], there)
        c.start()
        out.append(c)
    slots[me] = pay[me]
    for k in range(1, count):
        index, there = near_partner(me, hi, k)
        remote(pay.at[index], slots.at[index], s1.at[k], r1.at[index], there).wait_recv()
    total = slots[0]
    for k in range(1, count):
        total = total + slots[k]
    part[...] = total
    tops[hi] = total
    for k in range(1, far):
        index, there = far_partner(hi, lo, t, k, far)
        c = remote(part, tops.at[hi], s2.at[k], r2.at[hi], there)
        c.start()
        out.append(c)
    for k in range(1, far):
        index, there = far_partner(hi, lo, t, k, far)
        remote(part, tops.at[index], s2.at[k], r2.at[index], there).wait_recv()
    total = tops[0]
    for k in range(1, far):
        total = total + tops[k]
    full[me] = total
    for k in range(1, count):
        index, there = near_partner(me, hi, k)
        c = remote(full.at[me], full.at[me], s3.at[k], r3.at[me], there)
        c.start()
        out.append(c)
    for k in range(1, count):
        index, there = near_partner(me, hi, k)
        remote(full.at[me], full.at[index], s3.at[k], r3.at[index], there).wait_recv()
    for c in out:
        c.wait_send()


def tiles(x):
    return [x[:, n * LANES : (n + 1) * LANES] for n in range(x.shape[1] // LANES)]


def stacked(x):
    hi, mid, lo = split3(x)
    hi, mid, lo = hi.astype(f32), mid.astype(f32), lo.astype(f32)
    left = jnp.concatenate([hi, hi, mid, hi, mid, lo], 0)
    right = jnp.concatenate([hi, mid, hi, lo, mid, hi], 0)
    return left, right


def compress_kernel(
    far,
    gt, gp, gin, gout, eq, ep, ei, eo, bq, bp, bi, bo, perm, vec2, inb, vec3, qb,
    mq_o, mp_o, mi_o, mo_o, oq_o, op_o, oi_o, oo_o, rq_o, rp_o, ri_o, ro_o, vec_o,
    hq, hp, hi_, ho, aq, ap, ai, ao, mfull, obuf, pay, pay2, slots, part, tops, full,
    slots2, part2, tops2, full2, lsem, psend, precv,
    a1, a2, a3, a4, a5, a6, b1, b2, b3, b4, b5, b6,
):
    t = lax.axis_index("tensor")
    other = {"tensor": 1 - t}
    greet(far)
    local = []
    spots = [(gt.at[0], hq.at[0], aq.at[0]), (gt.at[1], hq.at[1], aq.at[1]), (gt.at[2], hq.at[2], aq.at[2]),
             (gp, hp, ap), (gin, hi_, ai), (gout, ho, ao)]
    for n, (src, mine, _) in enumerate(spots):
        c = pltpu.make_async_copy(src.at[t], mine, lsem.at[n])
        c.start()
        local.append(c)
    met(far)
    sent = []
    for n, (src, _, land) in enumerate(spots):
        c = remote(src.at[1 - t], land, psend.at[n], precv.at[n], other)
        c.start()
        sent.append(c)
    pay[...] = jnp.zeros_like(pay)
    pay2[...] = jnp.zeros_like(pay2)
    mfull[...] = jnp.zeros_like(mfull)
    for n in range(6):
        local[n].wait()
        sent[n].wait()
    rank = bq.shape[1]
    prows = hp.shape[0]
    turned = (hq[...] + aq[...]).reshape(-1, hq.shape[-1])
    grad = None
    for piece in split3(turned):
        term = dg(piece, perm[...], 0, 0)
        grad = term if grad is None else grad + term
    mq_o[...] = grad + eq[0]
    mp_o[...] = hp[...] + ap[...] + ep[0]
    mi_o[...] = hi_[...] + ai[...] + ei[0]
    mo_o[...] = (ho[...] + ao[...]).T + eo[0]
    own_rows = pl.ds(pl.multiple_of(t * prows, 8), prows)
    mfull[own_rows, :] = mp_o[...]
    lq = dgh(bq[...], mq_o[...], 0, 1)
    li = dgh(bi[...], mi_o[...], 0, 1)
    lp = dgh(bp[...], mfull[...], 0, 1)
    lo = dgh(bo[...], mo_o[...], 0, 1)
    per = pay.shape[1] // 8

    def put(n, value):
        pay[lax.div(n, per), pl.ds(pl.multiple_of(lax.rem(n, per) * 8, 8), 8), :] = value

    n = 0
    for block in (lq, li, lp):
        for tile in tiles(block):
            pay[n // per, (n % per) * 8 : (n % per) * 8 + 8, :] = tile
            n += 1
    own_tiles = tiles(lo)
    for m, tile in enumerate(own_tiles):
        put(n + t * len(own_tiles) + m, tile)
    n += 2 * len(own_tiles)
    lefts = n
    rest = []
    for ref in (vec2, vec3, inb):
        for c in range(ref.shape[1] // LANES):
            for r in range(ref.shape[0] // 8):
                rest.append(ref[r * 8 : r * 8 + 8, c * LANES : (c + 1) * LANES])
    for r in range(2):
        rest.append(qb[r * 8 : r * 8 + 8, :])
    for value in rest:
        pay[n // per, (n % per) * 8 : (n % per) * 8 + 8, :] = value
        n += 1
    big_sum(pay, slots, part, tops, full, (a1, a2, a3, a4, a5, a6), far, pay.shape[1])
    get = lambda m: full[m // per, (m % per) * 8 : (m % per) * 8 + 8, :]
    for m in range(len(rest)):
        vec_o[m * 8 : m * 8 + 8, :] = get(lefts + m)
    sizes = [lq.shape[1] // LANES, li.shape[1] // LANES, lp.shape[1] // LANES, 2 * len(own_tiles)]
    start = 0
    rows = []
    for size in sizes:
        rows.append(jnp.concatenate([get(start + m) for m in range(size)], -1))
        start += size
    oq, oi, op, oo = orthonormal(rows)
    obuf[0] = oo[:, : lo.shape[1]]
    obuf[1] = oo[:, lo.shape[1] :]
    oo_own = obuf[t]
    rq = dgh(oq, mq_o[...], 1, 0)
    ri = dgh(oi, mi_o[...], 1, 0)
    rp = dgh(op, mfull[...], 1, 0)
    ro = dgh(oo_own, mo_o[...], 1, 0)
    per2 = pay2.shape[1] // 8

    def put2(n, value):
        pay2[lax.div(n, per2), pl.ds(pl.multiple_of(lax.rem(n, per2) * 8, 8), 8), 0 : value.shape[1]] = value

    def get2(n):
        return full2[lax.div(n, per2), pl.ds(pl.multiple_of(lax.rem(n, per2) * 8, 8), 8), :]

    cuts = [(rq, True), (ri, True), (rp, False), (ro, False)]
    base = 0
    where = []
    for block, split in cuts:
        count = -(-block.shape[1] // LANES)
        first = base + t * count if split else base
        for m in range(count):
            put2(first + m, block[:, m * LANES : min((m + 1) * LANES, block.shape[1])])
        where.append((first, count))
        base += count * (2 if split else 1)
    big_sum(pay2, slots2, part2, tops2, full2, (b1, b2, b3, b4, b5, b6), far, pay2.shape[1])
    share = 1.0 / (far * NEAR)
    for (first, count), ref in zip(where, (rq_o, ri_o, rp_o, ro_o)):
        for m in range(count):
            lanes = slice(m * LANES, min((m + 1) * LANES, ref.shape[1]))
            ref[:, lanes] = get2(first + m)[:, : lanes.stop - lanes.start] * share
    oq_o[...] = stacked(oq)[0].T
    oi_o[...] = stacked(oi)[0].T
    mfull[:, 0:48] = stacked(op)[0].T
    op_o[...] = mfull[own_rows, 0:48]
    oo_o[...] = stacked(oo_own)[0].T


def update_kernel(
    oq, op, oi, oo, rq, rp, ri, ro, mq, mp, mi, mo, wq, wp, wi, wo, vq, vp, vi, vo,
    vec, gains, offs, taps, scales, bq, sharp, bi, gains_v, offs_v, taps_v, scales_v, bq_v, sharp_v, bi_v,
    wq_o, wp_o, wi_o, wo_o, vq_o, vp_o, vi_o, vo_o, eq_o, ep_o, ei_o, eo_o,
    tq_o, tp_o, ti_o, to_o,
    gains_o, offs_o, taps_o, scales_o, bq_o, sharp_o, bi_o,
    gains_m, offs_m, taps_m, scales_m, bq_m, sharp_m, bi_m,
    *, share,
):
    groups = (
        (oq, rq, mq, wq, vq, wq_o, vq_o, eq_o),
        (op, rp, mp, wp, vp, wp_o, vp_o, ep_o),
        (oi, ri, mi, wi, vi, wi_o, vi_o, ei_o),
        (oo, ro, mo, wo, vo, wo_o, vo_o, eo_o),
    )
    for o, r, m, w, v, w_o, v_o, e_o in groups:
        approx = dg(o[...].astype(bf16), stacked(r[...])[1].astype(bf16), 1, 0)
        moment = momentum_decay * v[...] + approx
        v_o[...] = moment
        w_o[...] = w[...] - learn_rate * moment
        e_o[0] = m[...] - approx

    @pl.when(pl.program_id(0) == 0)
    def _():
        for r, t_o in ((rq, tq_o), (rp, tp_o), (ri, ti_o), (ro, to_o)):
            t_o[...] = r[...].T

        def step(grad, value, moment, v_out, m_out, rows):
            new = momentum_decay * moment[rows, :] + grad * share
            m_out[rows, :] = new
            v_out[rows, :] = value[rows, :] - learn_rate * new

        def row2(a, b):
            return jnp.concatenate([vec[24 * c + a : 24 * c + b, :] for c in range(3)], -1)

        def row3(a, b):
            return jnp.concatenate([vec[72 + 16 * c + a : 72 + 16 * c + b, :] for c in range(3)], -1)

        def each(grads, value, moment, v_out, m_out):
            for n, g in enumerate(grads):
                step(g, value, moment, v_out, m_out, slice(n, n + 1))

        each([row3(0, 1), row3(2, 3), row2(6, 7), row2(1, 2)], gains, gains_v, gains_o, gains_m)
        each(
            [row3(1, 2), row3(3, 4), row2(7, 8), row2(0, 1), row3(4, 5), row2(2, 3), row2(3, 4)],
            offs, offs_v, offs_o, offs_m,
        )
        each([row3(5, 6), row2(4, 5), row2(5, 6)], scales, scales_v, scales_o, scales_m)
        each([row3(7 + n, 8 + n) for n in range(9)] + [row2(8 + n, 9 + n) for n in range(9)],
             taps, taps_v, taps_o, taps_m)
        base = 72 + 48
        half = bi.shape[0]
        grad = jnp.concatenate([vec[base : base + half, :], vec[base + 8 : base + 8 + half, :]], -1)
        step(grad, bi, bi_v, bi_o, bi_m, slice(None))
        base += 16
        cols = bq.shape[1]
        for hf in range(2):
            pieces = []
            for n in range(-(-cols // LANES)):
                pieces.append(vec[base + 8 * hf + n : base + 8 * hf + n + 1, 0 : min(LANES, cols - n * LANES)])
            step(jnp.concatenate(pieces, -1), bq, bq_v, bq_o, bq_m, slice(hf, hf + 1))
        width = gains.shape[1]
        heads = sharp.shape[1]
        head = width // heads
        chan = lax.broadcasted_iota(jnp.int32, (width, heads), 0)
        lane = lax.broadcasted_iota(jnp.int32, (width, heads), 1)
        pick = jnp.where((chan >= lane * head) & (chan < (lane + 1) * head), 1.0, 0.0).astype(f32)
        grad = dgh(jnp.broadcast_to(row3(6, 7), (8, width)), pick, 1, 0)
        step(grad[0:1, :], sharp, sharp_v, sharp_o, sharp_m, slice(None))


def perm_matrix(cols, heads, head):
    new = np.arange(cols)
    j, rest = new // (heads * head), new % (heads * head)
    h, c = rest // head, rest % head
    out = np.zeros((cols, cols), np.float32)
    out[new, h * 3 * head + j * head + c] = 1.0
    return out


def body(
    tokens, classes, loss,
    tri, tri_b, sharp, mapw, expw, exp_b, conw, gains, offs, taps, scales,
    tri_v, map_v, exp_v, con_v, tri_b_v, sharp_v, exp_b_v, gains_v, offs_v, taps_v, scales_v,
    tri_e, map_e, exp_e, con_e, tri_f, map_f, exp_f, con_f,
):
    import functools

    far = lax.axis_size("dp") // NEAR
    rows, width = tokens.shape
    own = classes.shape[0] // 2
    cells = rows // own
    heads = sharp.shape[0]
    head = width // heads
    part = width // 2
    cols = tri.shape[1]
    half = expw.shape[1]
    hidden = 2 * half
    vm = pl.BlockSpec(memory_space=pltpu.VMEM)
    sm = pl.BlockSpec(memory_space=pltpu.SMEM)
    anyspace = pl.BlockSpec(memory_space=pl.ANY)
    perm = jnp.asarray(perm_matrix(cols, heads // 2, head), bf16)

    wt, wp, win, wout = pl.pallas_call(
        weights_kernel,
        out_shape=[
            sds((3, 2, part, width), bf16),
            sds((2, part, width), bf16),
            sds((2, width, half), bf16),
            sds((2, half, width), bf16),
        ],
        in_specs=[vm] * 5,
        out_specs=[vm] * 4,
        scratch_shapes=[pltpu.SemaphoreType.DMA((6,)), pltpu.SemaphoreType.DMA((6,))],
        compiler_params=params(collective_id=0, has_side_effects=True),
        name="weights",
    )(tri, mapw, expw, conw, perm)
    wt = wt.reshape(3, width, width)
    wp = wp.reshape(width, width)
    bias_qkv = tri_b.reshape(heads, 3, head).transpose(1, 0, 2).reshape(3, width)

    def whole(*shape):
        return pl.BlockSpec(shape, lambda i: (0,) * len(shape))

    image = pl.BlockSpec((cells, width), lambda i: (i, 0))
    square = pl.BlockSpec((1, width, width), lambda i: (i, 0, 0))
    eight = pl.BlockSpec((1, 8, width), lambda i: (i, 0, 0))
    smem = pl.BlockSpec(memory_space=pltpu.SMEM)
    vecs = [whole(4, width), whole(7, width), whole(18, width), whole(3, width)]
    field = pltpu.VMEM((TRIO + 2, SIDE + 2, GROUPS, width), f32)
    nat = pltpu.VMEM((3, cells, LANES), f32)
    mask = pltpu.VMEM((TRIO * SIDE, GROUPS, LANES), f32)
    canvas = pltpu.VMEM((cells, width), f32)

    first, active, dgelu, low, q, k, v, mix, attn, gram, rs, stat = pl.pallas_call(
        first_kernel,
        grid=(own,),
        out_shape=[sds((rows, width))] * 3
        + [sds((rows, width), bf16)] * 5
        + [sds((own, width, width))] * 2
        + [sds((own, 8, width)), sds((8, LANES))],
        in_specs=[smem, smem, image, whole(3, width, width), whole(3, width), whole(width, width)] + vecs,
        out_specs=[image] * 8 + [square] * 2 + [eight, whole(8, LANES)],
        scratch_shapes=[
            nat, mask, canvas, field,
            pltpu.VMEM((width, width), f32), pltpu.VMEM((width, width), f32), pltpu.VMEM((2, 8, width), f32),
        ],
        compiler_params=params(),
        name="first_part",
    )(classes, sharp, tokens, wt, bias_qkv, wp, gains, offs, taps, scales)
    stat = small_sum(stat, far, 1)

    block_out, gsec, gsh, gin, gout, vec2, inb, gstat = pl.pallas_call(
        middle_kernel,
        grid=(own,),
        out_shape=[
            sds((rows, width), bf16), sds((rows, width)), sds((rows, width)),
            sds((2, width, half)), sds((2, width, half)), sds((24, width)), sds((8, 256)), sds((8, LANES)),
        ],
        in_specs=[smem, image, image, image, whole(8, LANES), whole(2, width, half), whole(2, half, width),
                  whole(hidden // 384, 384)] + vecs,
        out_specs=[image] * 3 + [whole(2, width, half)] * 2 + [whole(24, width), whole(8, 256), whole(8, LANES)],
        scratch_shapes=[
            nat, mask, field, field, canvas, canvas, canvas, canvas,
            pltpu.VMEM((rows, width), bf16), pltpu.VMEM((rows, width), bf16),
            pltpu.VMEM((rows, hidden), bf16), pltpu.VMEM((rows, hidden), bf16),
            pltpu.VMEM((17, 8, width), f32), pltpu.VMEM((8, hidden), f32),
        ],
        compiler_params=params(),
        name="middle_part",
    )(classes, first, active, loss, stat, win, wout, exp_b.reshape(hidden // 384, 384), gains, offs, taps, scales)
    gstat = small_sum(gstat, far, 2)

    input_grad, gt, gp, vec3, qb = pl.pallas_call(
        last_kernel,
        grid=(own,),
        out_shape=[
            sds((rows, width), bf16), sds((3, width, width)), sds((width, width)), sds((16, width)), sds((16, LANES)),
        ],
        in_specs=[smem, smem] + [image] * 11 + [square, square, eight, whole(8, LANES), whole(8, LANES),
                  whole(3, width, width), whole(width, width), whole(cols, cols)] + vecs,
        out_specs=[image, whole(3, width, width), whole(width, width), whole(16, width), whole(16, LANES)],
        scratch_shapes=[
            nat, mask, canvas, field, field, canvas, canvas, pltpu.VMEM((cells, 3 * width), bf16),
            pltpu.VMEM((16, 8, width), f32), pltpu.VMEM((3, 8, width), f32), pltpu.VMEM((width, width), f32),
        ],
        compiler_params=params(),
        name="last_part",
    )(classes, sharp, tokens, first, active, dgelu, gsec, gsh, low, q, k, v, mix, attn, gram, rs, stat, gstat,
      wt, wp, perm, gains, offs, taps, scales)

    pay_rows, pay_rows2 = 40, 32
    dma = pltpu.SemaphoreType.DMA
    near = 2 * NEAR
    sem_set = [dma((near,)), dma((near,)), dma((far,)), dma((far,)), dma((near,)), dma((near,))]
    mq, mp, mi, mo, oq, op, oi, oo, rq, rp, ri, ro, vec = pl.pallas_call(
        functools.partial(compress_kernel, far),
        out_shape=[
            sds((width, cols)), sds((part, width)), sds((width, half)), sds((half, width)),
            sds((width, 48)), sds((part, 48)), sds((width, 48)), sds((half, 48)),
            sds((8, cols)), sds((8, width)), sds((8, half)), sds((8, width)), sds((152, LANES)),
        ],
        in_specs=[anyspace] * 4 + [vm] * 13,
        out_specs=[vm] * 13,
        scratch_shapes=[
            pltpu.VMEM((3, part, width), f32), pltpu.VMEM((part, width), f32),
            pltpu.VMEM((width, half), f32), pltpu.VMEM((width, half), f32),
            pltpu.VMEM((3, part, width), f32), pltpu.VMEM((part, width), f32),
            pltpu.VMEM((width, half), f32), pltpu.VMEM((width, half), f32),
            pltpu.VMEM((width, width), f32), pltpu.VMEM((2, 8, half), f32),
            pltpu.VMEM((near, pay_rows, LANES), f32), pltpu.VMEM((near, pay_rows2, LANES), f32),
            pltpu.VMEM((near, pay_rows, LANES), f32), pltpu.VMEM((pay_rows, LANES), f32),
            pltpu.VMEM((far, pay_rows, LANES), f32), pltpu.VMEM((near, pay_rows, LANES), f32),
            pltpu.VMEM((near, pay_rows2, LANES), f32), pltpu.VMEM((pay_rows2, LANES), f32),
            pltpu.VMEM((far, pay_rows2, LANES), f32), pltpu.VMEM((near, pay_rows2, LANES), f32),
            dma((6,)), dma((6,)), dma((6,)),
        ] + sem_set + sem_set,
        compiler_params=params(collective_id=3, has_side_effects=True),
        name="compress",
    )(gt.reshape(3, 2, part, width), gp.reshape(2, part, width), gin, gout, tri_e, map_e, exp_e, con_e,
      tri_f, map_f, exp_f, con_f, perm, vec2, inb, vec3, qb)

    steps = 4

    def cut(n, m):
        return pl.BlockSpec((n // steps, m), lambda i: (i, 0))

    def cut3(n, m):
        return pl.BlockSpec((1, n // steps, m), lambda i: (0, i, 0))

    bias_half = lambda x: x.reshape(2, cols)
    hid = lambda x: x.reshape(hidden // 256, 256)
    mats = [cut(width, cols), cut(part, width), cut(width, half), cut(half, width)]
    small_specs = vecs + [whole(2, cols), whole(1, heads), whole(hidden // 256, 256)]
    small_shapes = [sds((4, width)), sds((7, width)), sds((18, width)), sds((3, width)), sds((2, cols)), sds((1, heads)), sds((hidden // 256, 256))]
    mat_shapes = [sds((width, cols)), sds((part, width)), sds((width, half)), sds((half, width))]
    res = pl.pallas_call(
        functools.partial(update_kernel, share=1.0 / (far * NEAR)),
        grid=(steps,),
        out_shape=mat_shapes * 2
        + [sds((1, width, cols)), sds((1, part, width)), sds((1, width, half)), sds((1, half, width))]
        + [sds((cols, 8)), sds((width, 8)), sds((half, 8)), sds((width, 8))]
        + small_shapes * 2,
        in_specs=[cut(width, 48), cut(part, 48), cut(width, 48), cut(half, 48),
                  whole(8, cols), whole(8, width), whole(8, half), whole(8, width)]
        + mats * 3 + [whole(152, LANES)] + small_specs * 2,
        out_specs=mats * 2
        + [cut3(width, cols), cut3(part, width), cut3(width, half), cut3(half, width)]
        + [whole(cols, 8), whole(width, 8), whole(half, 8), whole(width, 8)]
        + small_specs * 2,
        compiler_params=params(),
        name="update",
    )(oq, op, oi, oo, rq, rp, ri, ro, mq, mp, mi, mo, tri, mapw, expw, conw, tri_v, map_v, exp_v, con_v,
      vec, gains, offs, taps, scales, bias_half(tri_b), sharp.reshape(1, heads), hid(exp_b),
      gains_v, offs_v, taps_v, scales_v, bias_half(tri_b_v), sharp_v.reshape(1, heads), hid(exp_b_v))
    nw, nv, ne, nt, sv, smo = res[0:4], res[4:8], res[8:12], res[12:16], res[16:23], res[23:30]

    def small(x):
        g, o, t_, s, b, sh, bi_ = x
        return (b.reshape(-1), sh.reshape(-1), bi_.reshape(-1), g, o, t_, s)

    return (
        (block_out, input_grad) + tuple(nw) + small(sv) + tuple(nv) + small(smo) + tuple(ne) + tuple(nt)
    )


def solution(mesh):
    rows = P(("dp", "tensor"), None)
    col, row = P(None, "tensor"), P("tensor", None)
    rep = P()
    err = (P("dp", None, "tensor"), P("dp", "tensor", None), P("dp", None, "tensor"), P("dp", "tensor", None))
    mats = (col, row, col, row)
    in_specs = (
        (rows, P("dp"), rows, col, rep, rep, row, col, rep, row, rep, rep, rep, rep)
        + mats + (rep,) * 7 + err + (row, rep, row, rep)
    )
    out_specs = (rows, rows) + mats + (rep,) * 7 + mats + (rep,) * 7 + err + (row, rep, row, rep)
    return jax.shard_map(body, mesh=mesh, in_specs=in_specs, out_specs=out_specs, check_vma=False)
```

```python
import numpy as np
import jax
import jax.numpy as jnp
from jax import lax
from jax.experimental import pallas as pl
from jax.experimental.pallas import tpu as pltpu
from jax.sharding import PartitionSpec as P

SIDE = 24
GROUPS = 8
TRIO = 3
LANES = 128
NEAR = 4
learn_rate = 0.02
momentum_decay = 0.9
f32 = jnp.float32
bf16 = jnp.bfloat16
MESH = pl.DeviceIdType.MESH
VMEM_BYTES = 58 << 20
HALF_ROOT = 0.7071067811865476
GAUSS = 0.3989422804014327


def sds(shape, dtype=f32):
    return jax.ShapeDtypeStruct(shape, dtype)


def params(**kw):
    return pltpu.CompilerParams(vmem_limit_bytes=VMEM_BYTES, **kw)


def dg(a, b, ca, cb, precision=None):
    return lax.dot_general(
        a, b, (((ca,), (cb,)), ((), ())), preferred_element_type=f32, precision=precision
    )


def dgh(a, b, ca, cb):
    return dg(a, b, ca, cb, lax.Precision.HIGHEST)


def cat3(m):
    return jnp.concatenate([m, m, m], -1)


def split2(x):
    hi = x.astype(bf16)
    return hi, (x - hi.astype(f32)).astype(bf16)


def split3(x):
    hi = x.astype(bf16)
    rest = x - hi.astype(f32)
    mid = rest.astype(bf16)
    return hi, mid, (rest - mid.astype(f32)).astype(bf16)


def dg2(a, b, ca, cb):
    hi, lo = split2(a)
    return dg(hi, b, ca, cb) + dg(lo, b, ca, cb)


def mean_of(x):
    return jnp.sum(x, -1, keepdims=True) * (1.0 / x.shape[-1])


def layer_stats(x):
    center = x - mean_of(x)
    scale = lax.rsqrt(mean_of(center * center) + 1e-06)
    return center * scale, scale


def norm_back(grad_out, normed, scale, gain):
    grad_normed = grad_out * gain
    return scale * (
        grad_normed - mean_of(grad_normed) - normed * mean_of(grad_normed * normed)
    )


def colsum(x):
    return jnp.sum(x.reshape(x.shape[0] // 8, 8, x.shape[1]), 0)


def rowsum(x):
    return jnp.sum(x, 0, keepdims=True)


def gelu_pair(x):
    phi = 0.5 + 0.5 * lax.erf(x * HALF_ROOT)
    return x * phi, phi + x * jnp.exp(-0.5 * x * x) * GAUSS


def side_of(cls_ref, index):
    bucket = cls_ref[index]
    return SIDE * (7 + 2 * bucket + lax.div(bucket, 2)) // 12


def fill_mask(mask, side):
    shape = (SIDE, GROUPS, LANES)
    col = lax.broadcasted_iota(jnp.int32, shape, 0)
    group = lax.broadcasted_iota(jnp.int32, shape, 1)
    for m in range(TRIO):
        inside = (group * TRIO + m < side) & (col < side)
        mask[pl.ds(m * SIDE, SIDE)] = jnp.where(inside, 1.0, 0.0).astype(f32)


def to_canvas(src, nat, dst):
    per = TRIO * SIDE
    for l in range(3):
        nat[l] = src[:, l * LANES : (l + 1) * LANES].astype(f32)
    for j in range(per):
        for l in range(3):
            dst[pl.ds(j * 8, 8), l * LANES : (l + 1) * LANES] = nat[
                l, pl.ds(j, GROUPS, stride=per), :
            ]


def from_canvas(value, nat, dst):
    per = TRIO * SIDE
    for j in range(per):
        for l in range(3):
            nat[l, pl.ds(j, GROUPS, stride=per), :] = value[
                j * 8 : j * 8 + 8, l * LANES : (l + 1) * LANES
            ]
    for l in range(3):
        dst[:, l * LANES : (l + 1) * LANES] = nat[l].astype(bf16)


def clear_edges(field):
    zero = jnp.zeros((TRIO + 2, 1, GROUPS, field.shape[-1]), f32)
    field[:, 0:1] = zero
    field[:, SIDE + 1 : SIDE + 2] = zero


def put_field(field, value):
    v = value.reshape(TRIO, SIDE, GROUPS, value.shape[-1])
    group = lax.broadcasted_iota(jnp.int32, (SIDE, GROUPS, value.shape[-1]), 1)
    field[1 : TRIO + 1, 1 : SIDE + 1] = v
    field[0, 1 : SIDE + 1] = jnp.where(group == 0, 0.0, pltpu.roll(v[TRIO - 1], 1, 1))
    field[TRIO + 1, 1 : SIDE + 1] = jnp.where(
        group == GROUPS - 1, 0.0, pltpu.roll(v[0], GROUPS - 1, 1)
    )


def conv_chunk(win, weights, width, flip):
    total = None
    for a in range(3):
        for b in range(3):
            ra, rb = (2 - a, 2 - b) if flip else (a, b)
            term = weights[3 * a + b] * win[ra : ra + TRIO, rb : rb + width]
            total = term if total is None else total + term
    return total


def tap_rows(taps, first, lanes):
    return [
        jnp.broadcast_to(taps[first + k : first + k + 1, lanes], (GROUPS, LANES)) for k in range(9)
    ]


CHUNK = 6


def conv_loop(visit):
    for l in range(3):
        lanes = slice(l * LANES, (l + 1) * LANES)
        visit(l, lanes)


def near_partner(me, hi, k):
    index = lax.rem(me + k, 2 * NEAR)
    return index, {"dp": hi * NEAR + lax.div(index, 2), "tensor": lax.rem(index, 2)}


def place():
    dp = lax.axis_index("dp")
    t = lax.axis_index("tensor")
    hi = lax.div(dp, NEAR)
    lo = lax.rem(dp, NEAR)
    return hi, lo, t, lo * 2 + t


def greet(far):
    hi, lo, t, me = place()
    barrier = pltpu.get_barrier_semaphore()
    for k in range(1, 2 * NEAR):
        pl.semaphore_signal(
            barrier, inc=1, device_id=near_partner(me, hi, k)[1], device_id_type=MESH
        )
    for k in range(1, far):
        there = {"dp": lax.rem(hi + k, far) * NEAR + lo, "tensor": t}
        pl.semaphore_signal(barrier, inc=1, device_id=there, device_id_type=MESH)


def met(far):
    pl.semaphore_wait(pltpu.get_barrier_semaphore(), 2 * NEAR - 1 + far - 1)


def remote(src, dst, send, recv, there):
    return pltpu.make_async_remote_copy(
        src_ref=src, dst_ref=dst, send_sem=send, recv_sem=recv, device_id=there, device_id_type=MESH
    )


def far_partner(hi, lo, t, k, far):
    index = lax.rem(hi + k, far)
    return index, {"dp": index * NEAR + lo, "tensor": t}


def all_partners():
    n = lax.axis_size("dp") * 2
    me = lax.axis_index("dp") * 2 + lax.axis_index("tensor")
    out = []
    for k in range(1, n):
        index = lax.rem(me + k, n)
        out.append((index, {"dp": lax.div(index, 2), "tensor": lax.rem(index, 2)}))
    return me, out


def greet_all():
    barrier = pltpu.get_barrier_semaphore()
    for _, there in all_partners()[1]:
        pl.semaphore_signal(barrier, inc=1, device_id=there, device_id_type=MESH)


def met_all():
    pl.semaphore_wait(pltpu.get_barrier_semaphore(), lax.axis_size("dp") * 2 - 1)


def send_tile(tile, slots, sends, recvs):
    me, partners = all_partners()
    for k, (_, there) in enumerate(partners):
        remote(tile, slots.at[me], sends.at[k], recvs.at[me], there).start()
    slots[me] = tile[...]


def sum_tiles(tile, slots, sends, recvs):
    me, partners = all_partners()
    for k, (index, there) in enumerate(partners):
        remote(tile, slots.at[index], sends.at[k], recvs.at[index], there).wait_recv()
    total = jnp.sum(slots[...], 0)
    for k, (index, there) in enumerate(partners):
        remote(tile, slots.at[index], sends.at[k], recvs.at[index], there).wait_send()
    return total


def windows(x):
    return x[:, 0 : 2 * LANES], x[:, LANES : 3 * LANES]


def merge(a, b):
    return jnp.concatenate([a[:, :LANES], a[:, LANES:] + b[:, :LANES], b[:, LANES:]], -1)


def head_spots(heads, head):
    return [(2 * h // heads, h * head - LANES * (2 * h // heads)) for h in range(heads)]


def batch_stats(st):
    row = lambda r: jnp.concatenate([st[r : r + 1, :], st[r + 1 : r + 2, :], st[r + 2 : r + 3, :]], -1)
    inv = cat3(1.0 / st[6:7, :])
    mean = row(0) * inv
    var = row(3) * inv - mean * mean
    return mean, lax.rsqrt(var + 1e-05), inv


def first_kernel(
    cls, sharp, tok, tri, mapw, perm, bq, gains, offs, taps, scales, expw, conw, loss,
    first_o, active_o, dgelu_o, low_o, q_o, k_o, v_o, mix_o, attn_o, gram_o, rs_o, stat_o, lc_o,
    wt_o, wp_o, win_o, wout_o,
    nat, mask, xm, field, sharp_rows, in_block, sums, wt, wp, win, wout, fexp, fcon, floss, masks, tile, slots,
    lsem, wsend, wrecv, sends, recvs,
):
    i = pl.program_id(0)
    t = lax.axis_index("tensor")
    own = cls.shape[0] // 2
    heads = sharp.shape[0]
    cells, width = tok.shape
    head = width // heads
    other = {"tensor": 1 - t}
    spots = [wt.at[0], wt.at[1], wt.at[2], wp, win, wout]

    def out_copy(n):
        ref = spots[n]
        return remote(ref.at[t], ref.at[t], wsend.at[n], wrecv.at[n], other)

    def in_copy(n):
        ref = spots[n]
        return remote(ref.at[1 - t], ref.at[1 - t], wsend.at[n], wrecv.at[n], other)

    loads = [
        pltpu.make_async_copy(expw, fexp, lsem.at[0]),
        pltpu.make_async_copy(conw, fcon, lsem.at[1]),
        pltpu.make_async_copy(loss, floss, lsem.at[2]),
    ]

    @pl.when(i == 0)
    def _():
        greet_all()
        for c in loads:
            c.start()
        turned = dg(perm[...], tri[...].astype(bf16), 1, 0).astype(bf16)
        part = turned.shape[0] // 3
        for j in range(3):
            wt[j, t] = turned[j * part : (j + 1) * part]
        wp[t] = mapw[...].astype(bf16)
        lane = lax.broadcasted_iota(jnp.int32, (head, 2 * LANES), 1)
        sharp_rows[...] = jnp.zeros_like(sharp_rows)
        in_block[...] = jnp.zeros_like(in_block)
        for h, (w, r) in enumerate(head_spots(heads, head)):
            inside = (lane >= r) & (lane < r + head)
            sharp_rows[w, r : r + head, :] = jnp.where(inside, sharp[h], 0.0)
            in_block[w, r : r + head, :] = jnp.where(inside, 1.0, 0.0)
        clear_edges(field)
        sums[...] = jnp.zeros_like(sums)
        loads[0].wait()
        loads[1].wait()
        win[t] = fexp[...].astype(bf16)
        wout[t] = fcon[...].astype(bf16)

    fill_mask(mask, side_of(cls, t * own + i))
    mk = cat3(mask[...].reshape(-1, LANES))
    to_canvas(tok, nat, xm)
    x = xm[...] * mk
    normed, _ = layer_stats(x)
    low_o[...] = ((normed * gains[0:1, :] + offs[0:1, :]) * mk).astype(bf16)

    @pl.when(i == 0)
    def _():
        met_all()
        for n in range(6):
            out_copy(n).start()
        for n in range(4):
            in_copy(n).wait_recv()

    low = low_o[...]
    lows = []
    for j in range(2):
        value = (dg(low, wt[j].reshape(width, width), 1, 1) + bq[j : j + 1, :]) * mk
        scale = lax.rsqrt(rowsum(value * value) + 1e-06)
        rs_o[0, j : j + 1, :] = scale
        unit = (value * scale).astype(bf16)
        (q_o, k_o)[j][...] = unit
        lows.append(windows(unit))
    value_low = ((dg(low, wt[2].reshape(width, width), 1, 1) + bq[2:3, :]) * mk).astype(bf16)
    v_o[...] = value_low
    parts = []
    for w in range(2):
        gram = dg(lows[0][w], lows[1][w], 0, 0)
        gram_o[0, w] = gram
        inside = in_block[w]
        logits = jnp.where(inside > 0.0, gram * sharp_rows[w], -1e30)
        powers = jnp.exp(logits - jnp.max(logits, -1, keepdims=True)) * inside
        attn = powers / jnp.maximum(jnp.sum(powers, -1, keepdims=True), 0.5)
        attn_o[0, w] = attn
        parts.append(dg(windows(value_low)[w], attn.astype(bf16), 1, 1))
    mixed = merge(*parts).astype(bf16)
    mix_o[...] = mixed
    branch = dg(mixed, wp[...].reshape(width, width), 1, 0) + offs[4:5, :]
    first = xm[...] * mk + scales[0:1, :] * branch * mk
    first_o[...] = first
    normed, _ = layer_stats(first)
    put_field(field, (normed * gains[1:2, :] + offs[1:2, :]) * mk)
    for l in range(3):
        lanes = slice(l * LANES, (l + 1) * LANES)
        w = tap_rows(taps, 0, lanes)
        tot = jnp.zeros((8, LANES), f32)
        sq = jnp.zeros((8, LANES), f32)
        for c0 in range(0, SIDE, CHUNK):
            conv = conv_chunk(field[:, c0 : c0 + CHUNK + 2, :, lanes], w, CHUNK, False)
            act, back = gelu_pair(conv)
            for m in range(TRIO):
                rows = slice((m * SIDE + c0) * 8, (m * SIDE + c0 + CHUNK) * 8)
                am = act[m] * mask[m * SIDE + c0 : m * SIDE + c0 + CHUNK]
                active_o[rows, lanes] = am.reshape(CHUNK * 8, LANES)
                dgelu_o[rows, lanes] = back[m].reshape(CHUNK * 8, LANES)
                tot = tot + jnp.sum(am, 0)
                sq = sq + jnp.sum(am * am, 0)
        sums[0, :, lanes] += tot
        sums[1, :, lanes] += sq

    @pl.when(i == own - 1)
    def _():
        cells_in = 0
        for n in range(own):
            s = side_of(cls, t * own + n)
            cells_in = cells_in + s * s
        for k in range(2):
            row = rowsum(sums[k])
            for l in range(3):
                tile[3 * k + l : 3 * k + l + 1, :] = row[:, l * LANES : (l + 1) * LANES]
        tile[6:8, :] = jnp.full((2, LANES), 1.0, f32) * cells_in.astype(f32)
        send_tile(tile, slots, sends, recvs)
        loads[2].wait()
        for n in range(own):
            fill_mask(masks, side_of(cls, t * own + n))
            to_canvas(floss.at[n * cells : (n + 1) * cells], nat, xm)
            value = xm[...] * cat3(masks[...].reshape(-1, LANES))
            lc_o[n * cells : (n + 1) * cells, :] = value.astype(bf16)
        for n in range(4, 6):
            in_copy(n).wait_recv()
        for n in range(6):
            out_copy(n).wait_send()
        stores = [
            pltpu.make_async_copy(src, dst, lsem.at[n])
            for n, (src, dst) in enumerate(((wt, wt_o), (wp, wp_o), (win, win_o), (wout, wout_o)))
        ]
        for c in stores:
            c.start()
        stat_o[...] = sum_tiles(tile, slots, sends, recvs)
        for c in stores:
            c.wait()


def middle_kernel(
    cls, first, active, lc, st, win, wout, bin_, gains, offs, taps, scales,
    out_o, gsec_o, gsh_o, gin_o, gout_o, vec_o, inb_o, stat_o,
    nat, mask, field, gfield, loc, macc, gacc, l3s, gms, hs, gs, acc, inb, tile, slots, sends, recvs,
):
    i = pl.program_id(0)
    t = lax.axis_index("tensor")
    own = cls.shape[0] // 2
    rows_n = first.shape[0]
    hidden = win.shape[0] * win.shape[2]
    half = win.shape[2]

    @pl.when(i == 0)
    def _():
        greet_all()
        clear_edges(field)
        clear_edges(gfield)
        acc[...] = jnp.zeros_like(acc)
        inb[...] = jnp.zeros_like(inb)

    fill_mask(mask, side_of(cls, t * own + i))
    mk = cat3(mask[...].reshape(-1, LANES))
    mean, rstd, _ = batch_stats(st)
    zhat = (active[...] - mean) * rstd
    put_field(field, (zhat * gains[2:3, :] + offs[2:3, :]) * mk)
    for l in range(3):
        lanes = slice(l * LANES, (l + 1) * LANES)
        w = tap_rows(taps, 9, lanes)
        bias = offs[5:6, lanes]
        for c0 in range(0, SIDE, CHUNK):
            conv = conv_chunk(field[:, c0 : c0 + CHUNK + 2, :, lanes], w, CHUNK, False)
            for m in range(TRIO):
                rows = slice((m * SIDE + c0) * 8, (m * SIDE + c0 + CHUNK) * 8)
                value = (conv[m] + bias) * mask[m * SIDE + c0 : m * SIDE + c0 + CHUNK]
                loc[rows, lanes] = value.reshape(CHUNK * 8, LANES)
    second = first[...] + scales[1:2, :] * loc[...]
    normed, _ = layer_stats(second)
    base = pl.multiple_of(i * rows_n, 16)
    l3 = ((normed * gains[3:4, :] + offs[3:4, :]) * mk).astype(bf16)
    l3s[pl.ds(base, rows_n), :] = l3
    gm = (lc[...].astype(f32) * scales[2:3, :]).astype(bf16)
    gms[pl.ds(base, rows_n), :] = gm
    acc[3] += colsum(gm.astype(f32))

    step = 384
    for n in range(hidden // step):
        hf, cols = n * step // half, slice(n * step % half, n * step % half + step)
        allc = slice(n * step, (n + 1) * step)
        pre = dg(l3s[pl.ds(base, rows_n), :], win[hf, :, cols], 1, 0) + jnp.concatenate(
            [bin_[3 * n + r : 3 * n + r + 1, :] for r in range(3)], -1
        )
        act, back = gelu_pair(pre)
        h = act.astype(bf16)
        hs[pl.ds(base, rows_n), allc] = h
        g = (dg(gms[pl.ds(base, rows_n), :], wout[hf, cols, :], 1, 1) * back).astype(bf16)
        gs[pl.ds(base, rows_n), allc] = g
        inb[:, allc] += colsum(g.astype(f32))
        m_part = dg(h, wout[hf, cols, :], 1, 0)
        g_part = dg(g, win[hf, :, cols], 1, 1)
        if n == 0:
            macc[...] = m_part
            gacc[...] = g_part
        else:
            macc[...] += m_part
            gacc[...] += g_part

    mlp = macc[...] + offs[6:7, :]
    second = first[...] + scales[1:2, :] * loc[...]
    from_canvas(second + scales[2:3, :] * mlp * mk, nat, out_o)
    acc[5] += colsum(lc[...].astype(f32) * mlp)
    normed, scale = layer_stats(second)
    dout = gacc[...] * mk
    acc[0] += colsum(dout)
    acc[1] += colsum(dout * normed)
    gsec = lc[...].astype(f32) + norm_back(dout, normed, scale, gains[3:4, :])
    gsec_o[...] = gsec
    acc[4] += colsum(gsec * loc[...])
    glocal = gsec * scales[1:2, :] * mk
    acc[2] += colsum(glocal)
    put_field(gfield, glocal)
    for l in range(3):
        lanes = slice(l * LANES, (l + 1) * LANES)
        w = tap_rows(taps, 9, lanes)
        tot = jnp.zeros((8, LANES), f32)
        cross = jnp.zeros((8, LANES), f32)
        tap_sum = [jnp.zeros((8, LANES), f32) for _ in range(9)]
        for c0 in range(0, SIDE, CHUNK):
            gwin = gfield[:, c0 : c0 + CHUNK + 2, :, lanes]
            fwin = field[:, c0 : c0 + CHUNK + 2, :, lanes]
            conv = conv_chunk(gwin, w, CHUNK, True)
            center = gwin[1 : 1 + TRIO, 1 : 1 + CHUNK]
            for a in range(3):
                for b in range(3):
                    prod = fwin[a : a + TRIO, b : b + CHUNK] * center
                    tap_sum[3 * a + b] += jnp.sum(prod, (0, 1))
            for m in range(TRIO):
                rows = slice((m * SIDE + c0) * 8, (m * SIDE + c0 + CHUNK) * 8)
                value = conv[m] * mask[m * SIDE + c0 : m * SIDE + c0 + CHUNK]
                flat = value.reshape(CHUNK * 8, LANES)
                gsh_o[rows, lanes] = flat
                z = (active[rows, lanes] - mean[:, lanes]) * rstd[:, lanes]
                tot = tot + jnp.sum(value, 0)
                cross = cross + colsum(flat * z)
        acc[6, :, lanes] += cross
        acc[7, :, lanes] += tot
        for k in range(9):
            acc[8 + k, :, lanes] += tap_sum[k]

    @pl.when(i == own - 1)
    def _():
        cross, tot = rowsum(acc[6]), rowsum(acc[7])
        for l in range(3):
            lanes = slice(l * LANES, (l + 1) * LANES)
            tile[l : l + 1, :] = tot[:, lanes]
            tile[3 + l : 4 + l, :] = cross[:, lanes]
        tile[6:8, :] = jnp.zeros((2, LANES), f32)
        met_all()
        send_tile(tile, slots, sends, recvs)
        vec_o[...] = jnp.zeros_like(vec_o)
        for k in range(17):
            vec_o[k : k + 1, :] = rowsum(acc[k])
        inb_o[...] = jnp.zeros_like(inb_o)
        for k in range(hidden // LANES):
            inb_o[k : k + 1, :] = rowsum(inb[:, k * LANES : (k + 1) * LANES])
        l3_t = l3s[...].T
        gm_t = gms[...].T
        for hf in range(2):
            cols = slice(hf * half, (hf + 1) * half)
            gin_o[hf] = dg(l3_t, gs[:, cols], 1, 0)
            gout_o[hf] = dg(gm_t, hs[:, cols], 1, 0)
        stat_o[...] = sum_tiles(tile, slots, sends, recvs)


def last_kernel(
    cls, sharp, tok, first, active, dgelu, gsec, gsh, low, q, k, v, mix, attn, gram, rs,
    st, gst, wt, wp, perm, gains, offs, taps, scales,
    ingrad_o, gt_o, gp_o, vec_o, qb_o,
    nat, mask, xm, field, gfield, gback, gfirst, gproj, gals, acc, bias_acc, sharp_rows,
):
    i = pl.program_id(0)
    t = lax.axis_index("tensor")
    own = cls.shape[0] // 2
    heads = sharp.shape[0]
    cells, width = tok.shape
    head = width // heads

    @pl.when(i == 0)
    def _():
        sharp_rows[...] = jnp.zeros_like(sharp_rows)
        for h, (w, r) in enumerate(head_spots(heads, head)):
            sharp_rows[w, r : r + head, :] = jnp.full((head, 2 * LANES), 1.0, f32) * sharp[h]
        clear_edges(field)
        clear_edges(gfield)
        acc[...] = jnp.zeros_like(acc)
        bias_acc[...] = jnp.zeros_like(bias_acc)

    fill_mask(mask, side_of(cls, t * own + i))
    mk = cat3(mask[...].reshape(-1, LANES))
    mean, rstd, inv = batch_stats(st)
    gsum = lambda r: jnp.concatenate([gst[r : r + 1, :], gst[r + 1 : r + 2, :], gst[r + 2 : r + 3, :]], -1)
    gain_bn = gains[2:3, :]
    zhat = (active[...] - mean) * rstd
    gact = rstd * (gsh[...] * gain_bn - gsum(0) * gain_bn * inv - zhat * (gsum(3) * gain_bn * inv)) * mk
    put_field(gfield, gact * dgelu[...])
    normed, scale = layer_stats(first[...])
    put_field(field, (normed * gains[1:2, :] + offs[1:2, :]) * mk)
    for l in range(3):
        lanes = slice(l * LANES, (l + 1) * LANES)
        w = tap_rows(taps, 0, lanes)
        tap_sum = [jnp.zeros((8, LANES), f32) for _ in range(9)]
        for c0 in range(0, SIDE, CHUNK):
            gwin = gfield[:, c0 : c0 + CHUNK + 2, :, lanes]
            fwin = field[:, c0 : c0 + CHUNK + 2, :, lanes]
            conv = conv_chunk(gwin, w, CHUNK, True)
            center = gwin[1 : 1 + TRIO, 1 : 1 + CHUNK]
            for a in range(3):
                for b in range(3):
                    prod = fwin[a : a + TRIO, b : b + CHUNK] * center
                    tap_sum[3 * a + b] += jnp.sum(prod, (0, 1))
            for m in range(TRIO):
                rows = slice((m * SIDE + c0) * 8, (m * SIDE + c0 + CHUNK) * 8)
                value = conv[m] * mask[m * SIDE + c0 : m * SIDE + c0 + CHUNK]
                gback[rows, lanes] = value.reshape(CHUNK * 8, LANES)
        for n in range(9):
            acc[7 + n, :, lanes] += tap_sum[n]
    dout = gback[...]
    normed, scale = layer_stats(first[...])
    acc[2] += colsum(dout * normed)
    acc[3] += colsum(dout)
    grad = gsec[...] + norm_back(dout, normed, scale, gains[1:2, :])
    gfirst[...] = grad
    to_canvas(tok, nat, xm)
    x = xm[...] * mk
    xm[...] = x
    acc[5] += colsum(grad * (first[...] - x))
    gal = (grad * scales[0:1, :] * mk).astype(bf16)
    acc[4] += colsum(gal.astype(f32))
    base = pl.multiple_of(i * cells, 16)
    gals[pl.ds(base, cells), :] = gal
    gmix = dg(gal, wp[...], 1, 1).astype(bf16)
    lane1 = lax.broadcasted_iota(jnp.int32, (1, width), 1)
    sharp_lane = jnp.zeros((1, width), f32)
    for h in range(heads):
        sharp_lane = jnp.where((lane1 >= h * head) & (lane1 < (h + 1) * head), sharp[h], sharp_lane)
    ones = jnp.ones((8, 2 * LANES), bf16)
    gval, gqu, gku, chan, chan_k = [], [], [], [], []
    for w in range(2):
        cols = slice(w * LANES, (w + 2) * LANES)
        gw, vw, kw, qw = gmix[:, cols], v[:, cols], k[:, cols], q[:, cols]
        a = attn[0, w]
        gattn = dg(gw, vw, 0, 0)
        gval.append(dg(gw, a.astype(bf16), 1, 0))
        gsc = a * (gattn - jnp.sum(gattn * a, -1, keepdims=True))
        weighted = gsc * gram[0, w]
        hi, lo = split2(weighted)
        chan.append(dg(ones, hi, 1, 1) + dg(ones, lo, 1, 1))
        chan_k.append(rowsum(weighted * sharp_rows[w]))
        low_sc = (gsc * sharp_rows[w]).astype(bf16)
        gqu.append(dg(kw, low_sc, 1, 1))
        gku.append(dg(qw, low_sc, 1, 0))
    chan = merge(*chan)[0:1, :]
    acc[6, 0:1, :] += chan
    gq = rs[0, 0:1, :] * (merge(*gqu) - q[...].astype(f32) * (chan * sharp_lane))
    gk = rs[0, 1:2, :] * (merge(*gku) - k[...].astype(f32) * merge(*chan_k))
    for j, piece in enumerate((gq, gk, merge(*gval))):
        small = piece.astype(bf16)
        gproj[pl.ds(base, cells), j * width : (j + 1) * width] = small
        bias_acc[j] += colsum(small.astype(f32))

    dout = dg(gproj[pl.ds(base, cells), :], wt[...].reshape(3 * width, width), 1, 0) * mk
    normed, scale = layer_stats(xm[...])
    acc[0] += colsum(dout * normed)
    acc[1] += colsum(dout)
    result = (gfirst[...] + norm_back(dout, normed, scale, gains[0:1, :])) * mk
    from_canvas(result, nat, ingrad_o)

    @pl.when(i == own - 1)
    def _():
        for j in range(3):
            gt_o[j] = dg(gproj[:, j * width : (j + 1) * width], low[...], 0, 0)
        gp_o[...] = dg(mix[...], gals[...], 0, 0)
        for n in range(16):
            vec_o[n : n + 1, :] = rowsum(acc[n])
        vec_o[5:6, :] = rowsum(acc[5]) / scales[0:1, :]
        qb_o[...] = jnp.zeros_like(qb_o)
        part = perm.shape[0] // 3
        lane8 = lax.broadcasted_iota(jnp.int32, (8, width), 1)
        halves = []
        for hf in range(2):
            total = None
            for j in range(3):
                rows = perm[j * part : (j + 1) * part, :]
                both = jnp.concatenate([rows, rows], 0)
                mine = jnp.where((lane8 >= hf * part) & (lane8 < (hf + 1) * part), bias_acc[j], 0.0)
                for piece in split3(mine):
                    term = dg(piece, both, 1, 0)
                    total = term if total is None else total + term
            halves.append(rowsum(total))
        row = jnp.concatenate(halves, -1)
        for n in range(row.shape[1] // LANES):
            qb_o[n : n + 1, :] = row[:, n * LANES : (n + 1) * LANES]


def orthonormal(rows):
    index = lax.broadcasted_iota(jnp.int32, rows[0].shape[:1] + (1,), 0)
    rank = rows[0].shape[0]
    for n in range(rank):
        done = []
        for v in rows:
            column = v[n : n + 1, :]
            size = jnp.sum(column * column, -1, keepdims=True)
            unit = column * lax.rsqrt(size + 1e-06)
            dots = jnp.sum(v * unit, -1, keepdims=True)
            later = v - dots * unit
            done.append(jnp.where(index > n, later, jnp.where(index == n, unit, v)))
        rows = done
    return rows


def big_sum(pay, slots, part, tops, full, sems, far, rows):
    s1, r1, s2, r2, s3, r3 = sems
    hi, lo, t, me = place()
    count = 2 * NEAR
    out = []
    for k in range(1, count):
        index, there = near_partner(me, hi, k)
        c = remote(pay.at[index], slots.at[me], s1.at[k], r1.at[me], there)
        c.start()
        out.append(c)
    slots[me] = pay[me]
    for k in range(1, count):
        index, there = near_partner(me, hi, k)
        remote(pay.at[index], slots.at[index], s1.at[k], r1.at[index], there).wait_recv()
    total = slots[0]
    for k in range(1, count):
        total = total + slots[k]
    part[...] = total
    tops[hi] = total
    for k in range(1, far):
        index, there = far_partner(hi, lo, t, k, far)
        c = remote(part, tops.at[hi], s2.at[k], r2.at[hi], there)
        c.start()
        out.append(c)
    for k in range(1, far):
        index, there = far_partner(hi, lo, t, k, far)
        remote(part, tops.at[index], s2.at[k], r2.at[index], there).wait_recv()
    total = tops[0]
    for k in range(1, far):
        total = total + tops[k]
    full[me] = total
    for k in range(1, count):
        index, there = near_partner(me, hi, k)
        c = remote(full.at[me], full.at[me], s3.at[k], r3.at[me], there)
        c.start()
        out.append(c)
    for k in range(1, count):
        index, there = near_partner(me, hi, k)
        remote(full.at[me], full.at[index], s3.at[k], r3.at[index], there).wait_recv()
    for c in out:
        c.wait_send()


def tiles(x):
    return [x[:, n * LANES : (n + 1) * LANES] for n in range(x.shape[1] // LANES)]


def stacked(x):
    hi, mid, lo = split3(x)
    hi, mid, lo = hi.astype(f32), mid.astype(f32), lo.astype(f32)
    left = jnp.concatenate([hi, hi, mid, hi, mid, lo], 0)
    right = jnp.concatenate([hi, mid, hi, lo, mid, hi], 0)
    return left, right


def compress_kernel(
    far,
    gt, gp, gin, gout, eq, ep, ei, eo, bq, bp, bi, bo, perm, vec2, inb, vec3, qb,
    mq_o, mp_o, mi_o, mo_o, oq_o, op_o, oi_o, oo_o, rq_o, rp_o, ri_o, ro_o, rqs_o, vec_o,
    hq, hp, hi_, ho, aq, ap, ai, ao, mfull, obuf, pay, pay2, slots, part, tops, full,
    slots2, part2, tops2, full2, lsem, psend, precv,
    a1, a2, a3, a4, a5, a6, b1, b2, b3, b4, b5, b6,
):
    t = lax.axis_index("tensor")
    other = {"tensor": 1 - t}
    greet(far)
    local = []
    spots = [(gt.at[0], hq.at[0], aq.at[0]), (gt.at[1], hq.at[1], aq.at[1]), (gt.at[2], hq.at[2], aq.at[2]),
             (gp, hp, ap), (gin, hi_, ai), (gout, ho, ao)]
    for n, (src, mine, _) in enumerate(spots):
        c = pltpu.make_async_copy(src.at[t], mine, lsem.at[n])
        c.start()
        local.append(c)
    met(far)
    sent = []
    for n, (src, _, land) in enumerate(spots):
        c = remote(src.at[1 - t], land, psend.at[n], precv.at[n], other)
        c.start()
        sent.append(c)
    pay[...] = jnp.zeros_like(pay)
    pay2[...] = jnp.zeros_like(pay2)
    mfull[...] = jnp.zeros_like(mfull)
    for n in range(6):
        local[n].wait()
        sent[n].wait()
    prows = hp.shape[0]
    turned = (hq[...] + aq[...]).reshape(-1, hq.shape[-1])
    grad = None
    for piece in split3(turned):
        term = dg(perm[...], piece, 0, 0)
        grad = term if grad is None else grad + term
    mq_o[...] = grad + eq[0]
    mp_o[...] = hp[...] + ap[...] + ep[0]
    mi_o[...] = hi_[...] + ai[...] + ei[0]
    mo_o[...] = (ho[...] + ao[...]).T + eo[0]
    own_rows = pl.ds(pl.multiple_of(t * prows, 8), prows)
    mfull[own_rows, :] = mp_o[...]
    lq = dgh(bq[...], mq_o[...], 1, 0)
    li = dgh(bi[...], mi_o[...], 1, 1)
    lp = dgh(bp[...], mfull[...], 1, 1)
    lo = dgh(bo[...], mo_o[...], 1, 1)
    per = pay.shape[1] // 8

    def put(n, value):
        pay[lax.div(n, per), pl.ds(pl.multiple_of(lax.rem(n, per) * 8, 8), 8), :] = value

    n = 0
    for block in (lq, li, lp):
        for tile in tiles(block):
            pay[n // per, (n % per) * 8 : (n % per) * 8 + 8, :] = tile
            n += 1
    own_tiles = tiles(lo)
    for m, tile in enumerate(own_tiles):
        put(n + t * len(own_tiles) + m, tile)
    n += 2 * len(own_tiles)
    lefts = n
    rest = []
    for ref in (vec2, vec3, inb):
        for c in range(ref.shape[1] // LANES):
            for r in range(ref.shape[0] // 8):
                rest.append(ref[r * 8 : r * 8 + 8, c * LANES : (c + 1) * LANES])
    for r in range(2):
        rest.append(qb[r * 8 : r * 8 + 8, :])
    for value in rest:
        pay[n // per, (n % per) * 8 : (n % per) * 8 + 8, :] = value
        n += 1
    big_sum(pay, slots, part, tops, full, (a1, a2, a3, a4, a5, a6), far, pay.shape[1])
    get = lambda m: full[m // per, (m % per) * 8 : (m % per) * 8 + 8, :]
    for m in range(len(rest)):
        vec_o[m * 8 : m * 8 + 8, :] = get(lefts + m)
    sizes = [lq.shape[1] // LANES, li.shape[1] // LANES, lp.shape[1] // LANES, 2 * len(own_tiles)]
    start = 0
    rows = []
    for size in sizes:
        rows.append(jnp.concatenate([get(start + m) for m in range(size)], -1))
        start += size
    oq, oi, op, oo = orthonormal(rows)
    obuf[0] = oo[:, : lo.shape[1]]
    obuf[1] = oo[:, lo.shape[1] :]
    oo_own = obuf[t]
    rq = dgh(oq, mq_o[...], 1, 1)
    ri = dgh(oi, mi_o[...], 1, 0)
    rp = dgh(op, mfull[...], 1, 0)
    ro = dgh(oo_own, mo_o[...], 1, 0)
    per2 = pay2.shape[1] // 8

    def put2(n, value):
        pay2[lax.div(n, per2), pl.ds(pl.multiple_of(lax.rem(n, per2) * 8, 8), 8), 0 : value.shape[1]] = value

    def get2(n):
        return full2[lax.div(n, per2), pl.ds(pl.multiple_of(lax.rem(n, per2) * 8, 8), 8), :]

    cuts = [(rq, True), (ri, True), (rp, False), (ro, False)]
    base = 0
    where = []
    for block, split in cuts:
        count = -(-block.shape[1] // LANES)
        first = base + t * count if split else base
        for m in range(count):
            put2(first + m, block[:, m * LANES : min((m + 1) * LANES, block.shape[1])])
        where.append((first, count))
        base += count * (2 if split else 1)
    big_sum(pay2, slots2, part2, tops2, full2, (b1, b2, b3, b4, b5, b6), far, pay2.shape[1])
    share = 1.0 / (far * NEAR)
    for (first, count), ref in zip(where, (rq_o, ri_o, rp_o, ro_o)):
        for m in range(count):
            lanes = slice(m * LANES, min((m + 1) * LANES, ref.shape[1]))
            ref[:, lanes] = get2(first + m)[:, : lanes.stop - lanes.start] * share
    rqs_o[...] = stacked(rq_o[...])[0].T
    oq_o[...] = stacked(oq)[1]
    oi_o[...] = stacked(oi)[0].T
    mfull[:, 0:48] = stacked(op)[0].T
    op_o[...] = mfull[own_rows, 0:48]
    oo_o[...] = stacked(oo_own)[0].T


def update_kernel(
    oq, op, oi, oo, rqs, rp, ri, ro, rq, mq, mp, mi, mo, wq, wp, wi, wo, vq, vp, vi, vo,
    vec, gains, offs, taps, scales, bq, sharp, bi, gains_v, offs_v, taps_v, scales_v, bq_v, sharp_v, bi_v,
    wq_o, wp_o, wi_o, wo_o, vq_o, vp_o, vi_o, vo_o, eq_o, ep_o, ei_o, eo_o,
    gains_o, offs_o, taps_o, scales_o, bq_o, sharp_o, bi_o,
    gains_m, offs_m, taps_m, scales_m, bq_m, sharp_m, bi_m, tq_o, tp_o, ti_o, to_o,
    *, share,
):
    groups = (
        (oq, None, mq, wq, vq, wq_o, vq_o, eq_o),
        (op, rp, mp, wp, vp, wp_o, vp_o, ep_o),
        (oi, ri, mi, wi, vi, wi_o, vi_o, ei_o),
        (oo, ro, mo, wo, vo, wo_o, vo_o, eo_o),
    )
    for o, r, m, w, v, w_o, v_o, e_o in groups:
        if r is None:
            approx = dg(rqs[...].astype(bf16), o[...].astype(bf16), 1, 0)
        else:
            approx = dg(o[...].astype(bf16), stacked(r[...])[1].astype(bf16), 1, 0)
        moment = momentum_decay * v[...] + approx
        v_o[...] = moment
        w_o[...] = w[...] - learn_rate * moment
        e_o[0] = m[...] - approx

    @pl.when(pl.program_id(0) == 0)
    def _():
        for r, t_o in ((rq, tq_o), (rp, tp_o), (ri, ti_o), (ro, to_o)):
            t_o[...] = r[...]

        def step(grad, value, moment, v_out, m_out, rows):
            new = momentum_decay * moment[rows, :] + grad * share
            m_out[rows, :] = new
            v_out[rows, :] = value[rows, :] - learn_rate * new

        def row2(a, b):
            return jnp.concatenate([vec[24 * c + a : 24 * c + b, :] for c in range(3)], -1)

        def row3(a, b):
            return jnp.concatenate([vec[72 + 16 * c + a : 72 + 16 * c + b, :] for c in range(3)], -1)

        def each(grads, value, moment, v_out, m_out):
            for n, g in enumerate(grads):
                step(g, value, moment, v_out, m_out, slice(n, n + 1))

        each([row3(0, 1), row3(2, 3), row2(6, 7), row2(1, 2)], gains, gains_v, gains_o, gains_m)
        each(
            [row3(1, 2), row3(3, 4), row2(7, 8), row2(0, 1), row3(4, 5), row2(2, 3), row2(3, 4)],
            offs, offs_v, offs_o, offs_m,
        )
        each([row3(5, 6), row2(4, 5), row2(5, 6)], scales, scales_v, scales_o, scales_m)
        each([row3(7 + n, 8 + n) for n in range(9)] + [row2(8 + n, 9 + n) for n in range(9)],
             taps, taps_v, taps_o, taps_m)
        base = 72 + 48
        half = bi.shape[0]
        step(vec[base : base + half, :], bi, bi_v, bi_o, bi_m, slice(None))
        base += 16
        step(vec[base : base + bq.shape[0], :], bq, bq_v, bq_o, bq_m, slice(None))
        width = gains.shape[1]
        heads = sharp.shape[1]
        head = width // heads
        chan = lax.broadcasted_iota(jnp.int32, (width, heads), 0)
        lane = lax.broadcasted_iota(jnp.int32, (width, heads), 1)
        pick = jnp.where((chan >= lane * head) & (chan < (lane + 1) * head), 1.0, 0.0).astype(f32)
        grad = dgh(jnp.broadcast_to(row3(6, 7), (8, width)), pick, 1, 0)
        step(grad[0:1, :], sharp, sharp_v, sharp_o, sharp_m, slice(None))


def perm_matrix(cols, heads, head):
    new = np.arange(cols)
    j, rest = new // (heads * head), new % (heads * head)
    h, c = rest // head, rest % head
    out = np.zeros((cols, cols), np.float32)
    out[new, h * 3 * head + j * head + c] = 1.0
    return out


def body(
    tokens, classes, loss,
    tri, tri_b, sharp, mapw, expw, exp_b, conw, gains, offs, taps, scales,
    tri_v, map_v, exp_v, con_v, tri_b_v, sharp_v, exp_b_v, gains_v, offs_v, taps_v, scales_v,
    tri_e, map_e, exp_e, con_e, tri_f, map_f, exp_f, con_f,
):
    import functools

    far = lax.axis_size("dp") // NEAR
    rows, width = tokens.shape
    own = classes.shape[0] // 2
    cells = rows // own
    heads = sharp.shape[0]
    head = width // heads
    part = width // 2
    cols = tri.shape[1]
    half = expw.shape[1]
    hidden = 2 * half
    vm = pl.BlockSpec(memory_space=pltpu.VMEM)
    sm = pl.BlockSpec(memory_space=pltpu.SMEM)
    anyspace = pl.BlockSpec(memory_space=pl.ANY)
    perm = jnp.asarray(perm_matrix(cols, heads // 2, head), bf16)

    bias_qkv = tri_b.reshape(heads, 3, head).transpose(1, 0, 2).reshape(3, width)

    def whole(*shape):
        return pl.BlockSpec(shape, lambda i: (0,) * len(shape))

    image = pl.BlockSpec((cells, width), lambda i: (i, 0))
    square = pl.BlockSpec((1, 2, 2 * LANES, 2 * LANES), lambda i: (i, 0, 0, 0))
    eight = pl.BlockSpec((1, 8, width), lambda i: (i, 0, 0))
    smem = pl.BlockSpec(memory_space=pltpu.SMEM)
    vecs = [whole(4, width), whole(7, width), whole(18, width), whole(3, width)]
    field = pltpu.VMEM((TRIO + 2, SIDE + 2, GROUPS, width), f32)
    nat = pltpu.VMEM((3, cells, LANES), f32)
    mask = pltpu.VMEM((TRIO * SIDE, GROUPS, LANES), f32)
    canvas = pltpu.VMEM((cells, width), f32)

    dma = pltpu.SemaphoreType.DMA
    devices = lax.axis_size("dp") * 2
    two_windows = pltpu.VMEM((2, 2 * LANES, 2 * LANES), f32)
    tile_exchange = [
        pltpu.VMEM((8, LANES), f32), pltpu.VMEM((devices, 8, LANES), f32),
    ]
    first, active, dgelu, low, q, k, v, mix, attn, gram, rs, stat, lc, wt, wp, win, wout = pl.pallas_call(
        first_kernel,
        grid=(own,),
        out_shape=[sds((rows, width))] * 3
        + [sds((rows, width), bf16)] * 5
        + [sds((own, 2, 2 * LANES, 2 * LANES))] * 2
        + [sds((own, 8, width)), sds((8, LANES)), sds((rows, width), bf16)]
        + [sds((3, 2, part, width), bf16), sds((2, part, width), bf16),
           sds((2, width, half), bf16), sds((2, half, width), bf16)],
        in_specs=[smem, smem, image, whole(cols, width), whole(part, width), whole(cols, cols), whole(3, width)]
        + vecs + [anyspace] * 3,
        out_specs=[image] * 8 + [square] * 2 + [eight, whole(8, LANES), whole(rows, width)] + [anyspace] * 4,
        scratch_shapes=[
            nat, mask, canvas, field, two_windows, two_windows, pltpu.VMEM((2, 8, width), f32),
            pltpu.VMEM((3, 2, part, width), bf16), pltpu.VMEM((2, part, width), bf16),
            pltpu.VMEM((2, width, half), bf16), pltpu.VMEM((2, half, width), bf16),
            pltpu.VMEM((width, half), f32), pltpu.VMEM((half, width), f32), pltpu.VMEM((rows, width), bf16), mask,
        ] + tile_exchange + [dma((4,)), dma((6,)), dma((6,)), dma((devices,)), dma((devices,))],
        compiler_params=params(collective_id=0, has_side_effects=True),
        name="first_part",
    )(classes, sharp, tokens, tri.T, mapw, perm, bias_qkv, gains, offs, taps, scales, expw, conw, loss)
    wt = wt.reshape(3, width, width)
    wp = wp.reshape(width, width)

    block_out, gsec, gsh, gin, gout, vec2, inb, gstat = pl.pallas_call(
        middle_kernel,
        grid=(own,),
        out_shape=[
            sds((rows, width), bf16), sds((rows, width)), sds((rows, width)),
            sds((2, width, half)), sds((2, width, half)), sds((24, width)), sds((16, LANES)), sds((8, LANES)),
        ],
        in_specs=[smem, image, image, image, whole(8, LANES), whole(2, width, half), whole(2, half, width),
                  whole(hidden // LANES, LANES)] + vecs,
        out_specs=[image] * 3 + [whole(2, width, half)] * 2 + [whole(24, width), whole(16, LANES), whole(8, LANES)],
        scratch_shapes=[
            nat, mask, field, field, canvas, canvas, canvas,
            pltpu.VMEM((rows, width), bf16), pltpu.VMEM((rows, width), bf16),
            pltpu.VMEM((rows, hidden), bf16), pltpu.VMEM((rows, hidden), bf16),
            pltpu.VMEM((17, 8, width), f32), pltpu.VMEM((8, hidden), f32),
        ] + tile_exchange + [dma((devices,)), dma((devices,))],
        compiler_params=params(collective_id=1, has_side_effects=True),
        name="middle_part",
    )(classes, first, active, lc, stat, win, wout, exp_b.reshape(hidden // LANES, LANES), gains, offs, taps, scales)
    input_grad, gt, gp, vec3, qb = pl.pallas_call(
        last_kernel,
        grid=(own,),
        out_shape=[
            sds((rows, width), bf16), sds((3, width, width)), sds((width, width)), sds((16, width)), sds((16, LANES)),
        ],
        in_specs=[smem, smem] + [image] * 6 + [whole(rows, width)] + [image] * 3 + [whole(rows, width)] + [square, square, eight, whole(8, LANES), whole(8, LANES),
                  whole(3, width, width), whole(width, width), whole(cols, cols)] + vecs,
        out_specs=[image, whole(3, width, width), whole(width, width), whole(16, width), whole(16, LANES)],
        scratch_shapes=[
            nat, mask, canvas, field, field, canvas, canvas, pltpu.VMEM((rows, 3 * width), bf16),
            pltpu.VMEM((rows, width), bf16),
            pltpu.VMEM((16, 8, width), f32), pltpu.VMEM((3, 8, width), f32), two_windows,
        ],
        compiler_params=params(),
        name="last_part",
    )(classes, sharp, tokens, first, active, dgelu, gsec, gsh, low, q, k, v, mix, attn, gram, rs, stat, gstat,
      wt, wp, perm, gains, offs, taps, scales)

    pay_rows, pay_rows2 = 40, 32
    near = 2 * NEAR
    sem_set = [dma((near,)), dma((near,)), dma((far,)), dma((far,)), dma((near,)), dma((near,))]
    mq, mp, mi, mo, oq, op, oi, oo, rq, rp, ri, ro, rqs, vec = pl.pallas_call(
        functools.partial(compress_kernel, far),
        out_shape=[
            sds((cols, width)), sds((part, width)), sds((width, half)), sds((half, width)),
            sds((48, width)), sds((part, 48)), sds((width, 48)), sds((half, 48)),
            sds((8, cols)), sds((8, width)), sds((8, half)), sds((8, width)), sds((cols, 48)), sds((152, LANES)),
        ],
        in_specs=[anyspace] * 4 + [vm] * 13,
        out_specs=[vm] * 14,
        scratch_shapes=[
            pltpu.VMEM((3, part, width), f32), pltpu.VMEM((part, width), f32),
            pltpu.VMEM((width, half), f32), pltpu.VMEM((width, half), f32),
            pltpu.VMEM((3, part, width), f32), pltpu.VMEM((part, width), f32),
            pltpu.VMEM((width, half), f32), pltpu.VMEM((width, half), f32),
            pltpu.VMEM((width, width), f32), pltpu.VMEM((2, 8, half), f32),
            pltpu.VMEM((near, pay_rows, LANES), f32), pltpu.VMEM((near, pay_rows2, LANES), f32),
            pltpu.VMEM((near, pay_rows, LANES), f32), pltpu.VMEM((pay_rows, LANES), f32),
            pltpu.VMEM((far, pay_rows, LANES), f32), pltpu.VMEM((near, pay_rows, LANES), f32),
            pltpu.VMEM((near, pay_rows2, LANES), f32), pltpu.VMEM((pay_rows2, LANES), f32),
            pltpu.VMEM((far, pay_rows2, LANES), f32), pltpu.VMEM((near, pay_rows2, LANES), f32),
            dma((6,)), dma((6,)), dma((6,)),
        ] + sem_set + sem_set,
        compiler_params=params(collective_id=2, has_side_effects=True),
        name="compress",
    )(gt.reshape(3, 2, part, width), gp.reshape(2, part, width), gin, gout, tri_e.swapaxes(1, 2), map_e, exp_e, con_e,
      tri_f.T, map_f.T, exp_f.T, con_f.T, perm, vec2, inb, vec3, qb)

    steps = 4

    def cut(n, m):
        return pl.BlockSpec((n // steps, m), lambda i: (i, 0))

    def cut3(n, m):
        return pl.BlockSpec((1, n // steps, m), lambda i: (0, i, 0))

    wide = lambda x: x.reshape(-1, LANES)
    mats = [cut(cols, width), cut(part, width), cut(width, half), cut(half, width)]
    small_specs = vecs + [whole(2 * cols // LANES, LANES), whole(1, heads), whole(hidden // LANES, LANES)]
    basis_specs = [whole(8, cols), whole(8, width), whole(8, half), whole(8, width)]
    basis_shapes = [sds((8, cols)), sds((8, width)), sds((8, half)), sds((8, width))]
    small_shapes = [sds((4, width)), sds((7, width)), sds((18, width)), sds((3, width)), sds((2 * cols // LANES, LANES)), sds((1, heads)), sds((hidden // LANES, LANES))]
    mat_shapes = [sds((cols, width)), sds((part, width)), sds((width, half)), sds((half, width))]
    res = pl.pallas_call(
        functools.partial(update_kernel, share=1.0 / (far * NEAR)),
        grid=(steps,),
        out_shape=mat_shapes * 2
        + [sds((1, cols, width)), sds((1, part, width)), sds((1, width, half)), sds((1, half, width))]
        + small_shapes * 2 + basis_shapes,
        in_specs=[whole(48, width), cut(part, 48), cut(width, 48), cut(half, 48),
                  cut(cols, 48), whole(8, width), whole(8, half), whole(8, width), whole(8, cols)]
        + mats * 3 + [whole(152, LANES)] + small_specs * 2,
        out_specs=mats * 2
        + [cut3(cols, width), cut3(part, width), cut3(width, half), cut3(half, width)]
        + small_specs * 2 + basis_specs,
        compiler_params=params(),
        name="update",
    )(oq, op, oi, oo, rqs, rp, ri, ro, rq, mq, mp, mi, mo, tri.T, mapw, expw, conw, tri_v.T, map_v, exp_v, con_v,
      vec, gains, offs, taps, scales, wide(tri_b), sharp.reshape(1, heads), wide(exp_b),
      gains_v, offs_v, taps_v, scales_v, wide(tri_b_v), sharp_v.reshape(1, heads), wide(exp_b_v))
    nw, nv, ne, sv, smo, nt = res[0:4], res[4:8], res[8:12], res[12:19], res[19:26], res[26:30]
    nw, nv = [nw[0].T, *nw[1:]], [nv[0].T, *nv[1:]]
    ne = [ne[0].swapaxes(1, 2), *ne[1:]]
    nt = [x.T for x in nt]

    def small(x):
        g, o, t_, s, b, sh, bi_ = x
        return (b.reshape(-1), sh.reshape(-1), bi_.reshape(-1), g, o, t_, s)

    return (
        (block_out, input_grad) + tuple(nw) + small(sv) + tuple(nv) + small(smo) + tuple(ne) + tuple(nt)
    )


def solution(mesh):
    rows = P(("dp", "tensor"), None)
    col, row = P(None, "tensor"), P("tensor", None)
    rep = P()
    err = (P("dp", None, "tensor"), P("dp", "tensor", None), P("dp", None, "tensor"), P("dp", "tensor", None))
    mats = (col, row, col, row)
    in_specs = (
        (rows, P("dp"), rows, col, rep, rep, row, col, rep, row, rep, rep, rep, rep)
        + mats + (rep,) * 7 + err + (row, rep, row, rep)
    )
    out_specs = (rows, rows) + mats + (rep,) * 7 + mats + (rep,) * 7 + err + (row, rep, row, rep)
    return jax.shard_map(body, mesh=mesh, in_specs=in_specs, out_specs=out_specs, check_vma=False)
```

```python
import jax
import jax.numpy as jnp
from jax import lax
from jax.experimental import pallas as pl
from jax.experimental.pallas import tpu as pltpu
from jax.sharding import PartitionSpec as P

SIDE = 24
GROUPS = 8
TRIO = 3
LANES = 128
NEAR = 4
learn_rate = 0.02
momentum_decay = 0.9
f32 = jnp.float32
bf16 = jnp.bfloat16
MESH = pl.DeviceIdType.MESH
VMEM_BYTES = 58 << 20
HALF_ROOT = 0.7071067811865476
GAUSS = 0.3989422804014327


def sds(shape, dtype=f32):
    return jax.ShapeDtypeStruct(shape, dtype)


def params(**kw):
    return pltpu.CompilerParams(vmem_limit_bytes=VMEM_BYTES, **kw)


def dg(a, b, ca, cb):
    return lax.dot_general(
        a, b, (((ca,), (cb,)), ((), ())), preferred_element_type=f32
    )


def thin(a, m, cb):
    pieces = jnp.concatenate([x.astype(f32) for x in split3(a)], 0).astype(bf16)
    hi, lo = split2(m)
    total = dg(pieces, hi, 1, cb) + dg(pieces, lo, 1, cb)
    rows = a.shape[0]
    return total[0:rows] + total[rows : 2 * rows] + total[2 * rows :]


def cat3(m):
    return jnp.concatenate([m, m, m], -1)


def split2(x):
    hi = x.astype(bf16)
    return hi, (x - hi.astype(f32)).astype(bf16)


def split3(x):
    hi = x.astype(bf16)
    rest = x - hi.astype(f32)
    mid = rest.astype(bf16)
    return hi, mid, (rest - mid.astype(f32)).astype(bf16)


def dg2(a, b, ca, cb):
    hi, lo = split2(a)
    return dg(hi, b, ca, cb) + dg(lo, b, ca, cb)


def mean_of(x):
    return jnp.sum(x, -1, keepdims=True) * (1.0 / x.shape[-1])


def layer_stats(x):
    center = x - mean_of(x)
    scale = lax.rsqrt(mean_of(center * center) + 1e-06)
    return center * scale, scale


def norm_back(grad_out, normed, scale, gain):
    grad_normed = grad_out * gain
    return scale * (
        grad_normed - mean_of(grad_normed) - normed * mean_of(grad_normed * normed)
    )


def colsum(x):
    return jnp.sum(x.reshape(x.shape[0] // 8, 8, x.shape[1]), 0)


def rowsum(x):
    return jnp.sum(x, 0, keepdims=True)


def gelu_pair(x):
    phi = 0.5 + 0.5 * lax.erf(x * HALF_ROOT)
    return x * phi, phi + x * jnp.exp(-0.5 * x * x) * GAUSS


def side_of(cls_ref, index):
    bucket = cls_ref[index]
    return SIDE * (7 + 2 * bucket + lax.div(bucket, 2)) // 12


def fill_mask(mask, side):
    shape = (SIDE, GROUPS, LANES)
    col = lax.broadcasted_iota(jnp.int32, shape, 0)
    group = lax.broadcasted_iota(jnp.int32, shape, 1)
    for m in range(TRIO):
        inside = (group * TRIO + m < side) & (col < side)
        mask[pl.ds(m * SIDE, SIDE)] = jnp.where(inside, 1.0, 0.0).astype(f32)


def to_canvas(src, nat, dst):
    per = TRIO * SIDE
    for l in range(3):
        nat[l] = src[:, l * LANES : (l + 1) * LANES].astype(f32)
    for j in range(per):
        for l in range(3):
            dst[pl.ds(j * 8, 8), l * LANES : (l + 1) * LANES] = nat[
                l, pl.ds(j, GROUPS, stride=per), :
            ]


def from_canvas(value, nat, dst):
    per = TRIO * SIDE
    for j in range(per):
        for l in range(3):
            nat[l, pl.ds(j, GROUPS, stride=per), :] = value[
                j * 8 : j * 8 + 8, l * LANES : (l + 1) * LANES
            ]
    for l in range(3):
        dst[:, l * LANES : (l + 1) * LANES] = nat[l].astype(bf16)


def clear_edges(field):
    zero = jnp.zeros((TRIO + 2, 1, GROUPS, field.shape[-1]), f32)
    field[:, 0:1] = zero
    field[:, SIDE + 1 : SIDE + 2] = zero


def put_field(field, value):
    v = value.reshape(TRIO, SIDE, GROUPS, value.shape[-1])
    group = lax.broadcasted_iota(jnp.int32, (SIDE, GROUPS, value.shape[-1]), 1)
    field[1 : TRIO + 1, 1 : SIDE + 1] = v
    field[0, 1 : SIDE + 1] = jnp.where(group == 0, 0.0, pltpu.roll(v[TRIO - 1], 1, 1))
    field[TRIO + 1, 1 : SIDE + 1] = jnp.where(
        group == GROUPS - 1, 0.0, pltpu.roll(v[0], GROUPS - 1, 1)
    )


def conv_chunk(win, weights, width, flip):
    total = None
    for a in range(3):
        for b in range(3):
            ra, rb = (2 - a, 2 - b) if flip else (a, b)
            term = weights[3 * a + b] * win[ra : ra + TRIO, rb : rb + width]
            total = term if total is None else total + term
    return total


def tap_rows(taps, first, lanes):
    return [
        jnp.broadcast_to(taps[first + k : first + k + 1, lanes], (GROUPS, LANES)) for k in range(9)
    ]


CHUNK = 6


def chunk_rows(m, c0):
    return pl.ds(pl.multiple_of((m * SIDE + c0) * 8, 16), CHUNK * 8), pl.ds(m * SIDE + c0, CHUNK)


def near_partner(me, hi, k):
    index = lax.rem(me + k, 2 * NEAR)
    return index, {"dp": hi * NEAR + lax.div(index, 2), "tensor": lax.rem(index, 2)}


def place():
    dp = lax.axis_index("dp")
    t = lax.axis_index("tensor")
    hi = lax.div(dp, NEAR)
    lo = lax.rem(dp, NEAR)
    return hi, lo, t, lo * 2 + t


def greet(far):
    hi, lo, t, me = place()
    barrier = pltpu.get_barrier_semaphore()
    for k in range(1, 2 * NEAR):
        pl.semaphore_signal(
            barrier, inc=1, device_id=near_partner(me, hi, k)[1], device_id_type=MESH
        )
    for k in range(1, far):
        there = {"dp": lax.rem(hi + k, far) * NEAR + lo, "tensor": t}
        pl.semaphore_signal(barrier, inc=1, device_id=there, device_id_type=MESH)


def met(far):
    pl.semaphore_wait(pltpu.get_barrier_semaphore(), 2 * NEAR - 1 + far - 1)


def remote(src, dst, send, recv, there):
    return pltpu.make_async_remote_copy(
        src_ref=src, dst_ref=dst, send_sem=send, recv_sem=recv, device_id=there, device_id_type=MESH
    )


def far_partner(hi, lo, t, k, far):
    index = lax.rem(hi + k, far)
    return index, {"dp": index * NEAR + lo, "tensor": t}


def all_partners():
    n = lax.axis_size("dp") * 2
    me = lax.axis_index("dp") * 2 + lax.axis_index("tensor")
    out = []
    for k in range(1, n):
        index = lax.rem(me + k, n)
        out.append((index, {"dp": lax.div(index, 2), "tensor": lax.rem(index, 2)}))
    return me, out


def greet_all():
    barrier = pltpu.get_barrier_semaphore()
    for _, there in all_partners()[1]:
        pl.semaphore_signal(barrier, inc=1, device_id=there, device_id_type=MESH)


def met_all():
    pl.semaphore_wait(pltpu.get_barrier_semaphore(), lax.axis_size("dp") * 2 - 1)


def send_tile(tile, slots, sends, recvs):
    me, partners = all_partners()
    for k, (_, there) in enumerate(partners):
        remote(tile, slots.at[me], sends.at[k], recvs.at[me], there).start()
    slots[me] = tile[...]


def sum_tiles(tile, slots, sends, recvs):
    me, partners = all_partners()
    for k, (index, there) in enumerate(partners):
        remote(tile, slots.at[index], sends.at[k], recvs.at[index], there).wait_recv()
    total = jnp.sum(slots[...], 0)
    for k, (index, there) in enumerate(partners):
        remote(tile, slots.at[index], sends.at[k], recvs.at[index], there).wait_send()
    return total


def fill_perm(perm, heads, head):
    shape = (head, perm.shape[1])
    row = lax.broadcasted_iota(jnp.int32, shape, 0)
    lane = lax.broadcasted_iota(jnp.int32, shape, 1)
    for j in range(3):
        for h in range(heads):
            at = (j * heads + h) * head
            perm[at : at + head, :] = jnp.where(lane == row + (3 * h + j) * head, 1.0, 0.0).astype(bf16)


def windows(x):
    return x[:, 0 : 2 * LANES], x[:, LANES : 3 * LANES]


def merge(a, b):
    return jnp.concatenate([a[:, :LANES], a[:, LANES:] + b[:, :LANES], b[:, LANES:]], -1)


def head_spots(heads, head):
    return [(2 * h // heads, h * head - LANES * (2 * h // heads)) for h in range(heads)]


def batch_stats(st):
    row = lambda r: jnp.concatenate([st[r : r + 1, :], st[r + 1 : r + 2, :], st[r + 2 : r + 3, :]], -1)
    inv = cat3(1.0 / st[6:7, :])
    mean = row(0) * inv
    var = row(3) * inv - mean * mean
    return mean, lax.rsqrt(var + 1e-05), inv


def first_kernel(
    cls, sharp, tok, tri, mapw, tri_b, gains, offs, taps, scales, expw, conw, loss,
    first_h, active_h, dgelu_h, low_h, q_h, k_h, v_h, mix_h, xc_h, attn_h, gram_h, rs_o, stat_o, lc_h,
    wt_o, wp_o, win_o, wout_o,
    nat, mask, xm, field, sharp_rows, in_block, sums, wt, wp, win, wout, fexp, fcon, floss, masks, perm, bq,
    first_s, active_s, dgelu_s, low_s, q_s, k_s, v_s, mix_s, xc_s, attn_s, gram_s, lc_s, tile, slots,
    osem, lsem, wsend, wrecv, sends, recvs,
):
    i = pl.program_id(0)
    t = lax.axis_index("tensor")
    own = cls.shape[0] // 2
    heads = sharp.shape[0]
    cells, width = tok.shape
    head = width // heads
    other = {"tensor": 1 - t}
    spots = [wt.at[0], wt.at[1], wt.at[2], wp, win, wout]

    def out_copy(n):
        ref = spots[n]
        return remote(ref.at[t], ref.at[t], wsend.at[n], wrecv.at[n], other)

    def in_copy(n):
        ref = spots[n]
        return remote(ref.at[1 - t], ref.at[1 - t], wsend.at[n], wrecv.at[n], other)

    here = pl.ds(pl.multiple_of(i * cells, 16), cells)
    images = [(first_s, first_h), (active_s, active_h), (dgelu_s, dgelu_h), (low_s, low_h), (q_s, q_h), (k_s, k_h),
              (v_s, v_h), (mix_s, mix_h), (xc_s, xc_h)]
    squares = [(attn_s, attn_h), (gram_s, gram_h)]

    def image_outs(n):
        rows = pl.ds(n * cells if isinstance(n, int) else pl.multiple_of(n * cells, 16), cells)
        copies = [pltpu.make_async_copy(a.at[rows], b.at[rows], osem.at[k, n]) for k, (a, b) in enumerate(images)]
        return copies + [
            pltpu.make_async_copy(a.at[n], b.at[n], osem.at[len(images) + k, n]) for k, (a, b) in enumerate(squares)
        ]

    first_o, active_o, dgelu_o, low_o, q_o, k_o, v_o, mix_o, xc_o = [a.at[here] for a, _ in images]
    loads = [
        pltpu.make_async_copy(expw, fexp, lsem.at[0]),
        pltpu.make_async_copy(conw, fcon, lsem.at[1]),
        pltpu.make_async_copy(loss, floss, lsem.at[2]),
    ]

    @pl.when(i == 0)
    def _():
        greet_all()
        for c in loads:
            c.start()
        fill_perm(perm, heads // 2, head)
        turned = dg(perm[...], tri[...].astype(bf16), 1, 0).astype(bf16)
        part = turned.shape[0] // 3
        bias = jnp.concatenate([tri_b[n : n + 1, :] for n in range(tri_b.shape[0])], -1)
        pieces = jnp.concatenate([x.astype(f32) for x in split3(jnp.broadcast_to(bias, (8, bias.shape[1])))], 0)
        pieces = pieces.astype(bf16)
        sides = []
        for hf in range(2):
            turned_b = dg(pieces[:, hf * 3 * part : (hf + 1) * 3 * part], perm[...], 1, 1)
            sides.append(turned_b[0:1] + turned_b[8:9] + turned_b[16:17])
        for j in range(3):
            bq[j : j + 1, :] = jnp.concatenate([side[:, j * part : (j + 1) * part] for side in sides], -1)
        for j in range(3):
            wt[j, t] = turned[j * part : (j + 1) * part]
        wp[t] = mapw[...].astype(bf16)
        lane = lax.broadcasted_iota(jnp.int32, (head, 2 * LANES), 1)
        sharp_rows[...] = jnp.zeros_like(sharp_rows)
        in_block[...] = jnp.zeros_like(in_block)
        for h, (w, r) in enumerate(head_spots(heads, head)):
            inside = (lane >= r) & (lane < r + head)
            sharp_rows[w, r : r + head, :] = jnp.where(inside, sharp[h], 0.0)
            in_block[w, r : r + head, :] = jnp.where(inside, 1.0, 0.0)
        clear_edges(field)
        sums[...] = jnp.zeros_like(sums)
        loads[0].wait()
        loads[1].wait()
        win[t] = fexp[...].astype(bf16)
        wout[t] = fcon[...].astype(bf16)

    fill_mask(mask, side_of(cls, t * own + i))
    mk = cat3(mask[...].reshape(-1, LANES))
    to_canvas(tok, nat, xm)
    x = xm[...] * mk
    xc_o[...] = x.astype(bf16)
    normed, _ = layer_stats(x)
    low_o[...] = ((normed * gains[0:1, :] + offs[0:1, :]) * mk).astype(bf16)

    @pl.when(i == 0)
    def _():
        met_all()
        for n in range(6):
            out_copy(n).start()
        for n in range(4):
            in_copy(n).wait_recv()

    low = low_o[...]
    lows = []
    for j in range(2):
        value = (dg(low, wt[j].reshape(width, width), 1, 1) + bq[j : j + 1, :]) * mk
        scale = lax.rsqrt(rowsum(value * value) + 1e-06)
        rs_o[0, j : j + 1, :] = scale
        unit = (value * scale).astype(bf16)
        (q_o, k_o)[j][...] = unit
        lows.append(windows(unit))
    value_low = ((dg(low, wt[2].reshape(width, width), 1, 1) + bq[2:3, :]) * mk).astype(bf16)
    v_o[...] = value_low
    parts = []
    for w in range(2):
        gram = dg(lows[0][w], lows[1][w], 0, 0)
        gram_s[i, w] = gram
        inside = in_block[w]
        logits = jnp.where(inside > 0.0, gram * sharp_rows[w], -1e30)
        powers = jnp.exp(logits - jnp.max(logits, -1, keepdims=True)) * inside
        attn = powers / jnp.maximum(jnp.sum(powers, -1, keepdims=True), 0.5)
        attn_s[i, w] = attn
        parts.append(dg(windows(value_low)[w], attn.astype(bf16), 1, 1))
    mixed = merge(*parts).astype(bf16)
    mix_o[...] = mixed
    branch = dg(mixed, wp[...].reshape(width, width), 1, 0) + offs[4:5, :]
    first = xm[...] * mk + scales[0:1, :] * branch * mk
    first_o[...] = first
    normed, _ = layer_stats(first)
    put_field(field, (normed * gains[1:2, :] + offs[1:2, :]) * mk)
    for l in range(3):
        lanes = slice(l * LANES, (l + 1) * LANES)
        w = tap_rows(taps, 0, lanes)
        tot = jnp.zeros((8, LANES), f32)
        sq = jnp.zeros((8, LANES), f32)

        def step(n, carry):
            tot, sq = carry
            c0 = n * CHUNK
            conv = conv_chunk(field[:, pl.ds(c0, CHUNK + 2), :, lanes], w, CHUNK, False)
            act, back = gelu_pair(conv)
            for m in range(TRIO):
                rows, cells8 = chunk_rows(m, c0)
                am = act[m] * mask[cells8]
                active_o[rows, lanes] = am.reshape(CHUNK * 8, LANES)
                dgelu_o[rows, lanes] = back[m].reshape(CHUNK * 8, LANES)
                tot = tot + jnp.sum(am, 0)
                sq = sq + jnp.sum(am * am, 0)
            return tot, sq

        tot, sq = lax.fori_loop(0, SIDE // CHUNK, step, (tot, sq))
        sums[0, :, lanes] += tot
        sums[1, :, lanes] += sq
    for c in image_outs(i):
        c.start()

    @pl.when(i == own - 1)
    def _():
        cells_in = 0
        for n in range(own):
            s = side_of(cls, t * own + n)
            cells_in = cells_in + s * s
        for k in range(2):
            row = rowsum(sums[k])
            for l in range(3):
                tile[3 * k + l : 3 * k + l + 1, :] = row[:, l * LANES : (l + 1) * LANES]
        tile[6:8, :] = jnp.full((2, LANES), 1.0, f32) * cells_in.astype(f32)
        send_tile(tile, slots, sends, recvs)
        loads[2].wait()

        @pl.loop(0, own)
        def _(n):
            rows = pl.ds(pl.multiple_of(n * cells, 16), cells)
            fill_mask(masks, side_of(cls, t * own + n))
            to_canvas(floss.at[rows], nat, xm)
            lc_s[rows, :] = (xm[...] * cat3(masks[...].reshape(-1, LANES))).astype(bf16)

        for n in range(4, 6):
            in_copy(n).wait_recv()
        for n in range(6):
            out_copy(n).wait_send()
        stores = [
            pltpu.make_async_copy(src, dst, lsem.at[n])
            for n, (src, dst) in enumerate(
                ((wt, wt_o), (wp, wp_o), (win, win_o), (wout, wout_o), (lc_s, lc_h))
            )
        ]
        for c in stores:
            c.start()
        stat_o[...] = sum_tiles(tile, slots, sends, recvs)
        for c in stores:
            c.wait()
        for n in range(own):
            for c in image_outs(n):
                c.wait()


def middle_kernel(
    cls, first, active, lc, st, win_h, wout_h, bin_, gains, offs, taps, scales,
    out_h, gsec_h, gsh_h, gin_h, gout_h, vec_o, inb_o, stat_o,
    nat, mask, field, gfield, loc, macc, gacc, l3s, gms, hs, gs, acc, inb, win, wout, out_s, gsec_s, gsh_s, gin_o, gout_o, osem, gsem, wsem, tile, slots, sends, recvs,
):
    i = pl.program_id(0)
    t = lax.axis_index("tensor")
    own = cls.shape[0] // 2
    held = [pltpu.make_async_copy(win_h, win, wsem.at[0]), pltpu.make_async_copy(wout_h, wout, wsem.at[1])]
    rows_n = first.shape[0]
    base = pl.multiple_of(i * rows_n, 16)
    images = [(out_s, out_h), (gsec_s, gsec_h), (gsh_s, gsh_h)]

    def image_outs(n):
        rows = pl.ds(n * rows_n if isinstance(n, int) else pl.multiple_of(n * rows_n, 16), rows_n)
        return [pltpu.make_async_copy(a.at[rows], b.at[rows], osem.at[k, n]) for k, (a, b) in enumerate(images)]

    out_o, gsec_o, gsh_o = [a.at[pl.ds(base, rows_n)] for a, _ in images]
    hidden = win.shape[0] * win.shape[2]
    half = win.shape[2]

    @pl.when(i == 0)
    def _():
        greet_all()
        for c in held:
            c.start()
        clear_edges(field)
        clear_edges(gfield)
        acc[...] = jnp.zeros_like(acc)
        inb[...] = jnp.zeros_like(inb)

    fill_mask(mask, side_of(cls, t * own + i))
    mk = cat3(mask[...].reshape(-1, LANES))
    mean, rstd, _ = batch_stats(st)
    zhat = (active[...] - mean) * rstd
    put_field(field, (zhat * gains[2:3, :] + offs[2:3, :]) * mk)
    for l in range(3):
        lanes = slice(l * LANES, (l + 1) * LANES)
        w = tap_rows(taps, 9, lanes)
        bias = offs[5:6, lanes]

        def step(n, carry):
            c0 = n * CHUNK
            conv = conv_chunk(field[:, pl.ds(c0, CHUNK + 2), :, lanes], w, CHUNK, False)
            for m in range(TRIO):
                rows, cells8 = chunk_rows(m, c0)
                loc[rows, lanes] = ((conv[m] + bias) * mask[cells8]).reshape(CHUNK * 8, LANES)
            return carry

        lax.fori_loop(0, SIDE // CHUNK, step, 0)
    second = first[...] + scales[1:2, :] * loc[...]
    normed, _ = layer_stats(second)
    l3 = ((normed * gains[3:4, :] + offs[3:4, :]) * mk).astype(bf16)
    l3s[pl.ds(base, rows_n), :] = l3
    gm = (lc[...].astype(f32) * scales[2:3, :]).astype(bf16)
    gms[pl.ds(base, rows_n), :] = gm
    acc[3] += colsum(gm.astype(f32))

    @pl.when(i == 0)
    def _():
        for c in held:
            c.wait()

    step = 384
    for n in range(hidden // step):
        hf, cols = n * step // half, slice(n * step % half, n * step % half + step)
        allc = slice(n * step, (n + 1) * step)
        pre = dg(l3s[pl.ds(base, rows_n), :], win[hf, :, cols], 1, 0) + jnp.concatenate(
            [bin_[3 * n + r : 3 * n + r + 1, :] for r in range(3)], -1
        )
        act, back = gelu_pair(pre)
        h = act.astype(bf16)
        hs[pl.ds(base, rows_n), allc] = h
        g = (dg(gms[pl.ds(base, rows_n), :], wout[hf, cols, :], 1, 1) * back).astype(bf16)
        gs[pl.ds(base, rows_n), allc] = g
        inb[:, allc] += colsum(g.astype(f32))
        m_part = dg(h, wout[hf, cols, :], 1, 0)
        g_part = dg(g, win[hf, :, cols], 1, 1)
        if n == 0:
            macc[...] = m_part
            gacc[...] = g_part
        else:
            macc[...] += m_part
            gacc[...] += g_part

    mlp = macc[...] + offs[6:7, :]
    second = first[...] + scales[1:2, :] * loc[...]
    from_canvas(second + scales[2:3, :] * mlp * mk, nat, out_o)
    acc[5] += colsum(lc[...].astype(f32) * mlp)
    normed, scale = layer_stats(second)
    dout = gacc[...] * mk
    acc[0] += colsum(dout)
    acc[1] += colsum(dout * normed)
    gsec = lc[...].astype(f32) + norm_back(dout, normed, scale, gains[3:4, :])
    gsec_o[...] = gsec
    acc[4] += colsum(gsec * loc[...])
    glocal = gsec * scales[1:2, :] * mk
    acc[2] += colsum(glocal)
    put_field(gfield, glocal)
    for l in range(3):
        lanes = slice(l * LANES, (l + 1) * LANES)
        w = tap_rows(taps, 9, lanes)
        tot = jnp.zeros((8, LANES), f32)
        cross = jnp.zeros((8, LANES), f32)
        tap_sum = [jnp.zeros((8, LANES), f32) for _ in range(9)]

        def step(n, carry):
            tot, cross, tap_sum = carry[0], carry[1], list(carry[2:])
            c0 = n * CHUNK
            gwin = gfield[:, pl.ds(c0, CHUNK + 2), :, lanes]
            fwin = field[:, pl.ds(c0, CHUNK + 2), :, lanes]
            conv = conv_chunk(gwin, w, CHUNK, True)
            center = gwin[1 : 1 + TRIO, 1 : 1 + CHUNK]
            for a in range(3):
                for b in range(3):
                    prod = fwin[a : a + TRIO, b : b + CHUNK] * center
                    tap_sum[3 * a + b] += jnp.sum(prod, (0, 1))
            for m in range(TRIO):
                rows, cells8 = chunk_rows(m, c0)
                value = conv[m] * mask[cells8]
                flat = value.reshape(CHUNK * 8, LANES)
                gsh_o[rows, lanes] = flat
                z = (active[rows, lanes] - mean[:, lanes]) * rstd[:, lanes]
                tot = tot + jnp.sum(value, 0)
                cross = cross + colsum(flat * z)
            return (tot, cross, *tap_sum)

        tot, cross, *tap_sum = lax.fori_loop(0, SIDE // CHUNK, step, (tot, cross, *tap_sum))
        acc[6, :, lanes] += cross
        acc[7, :, lanes] += tot
        for k in range(9):
            acc[8 + k, :, lanes] += tap_sum[k]
    for c in image_outs(i):
        c.start()

    @pl.when(i == own - 1)
    def _():
        cross, tot = rowsum(acc[6]), rowsum(acc[7])
        for l in range(3):
            lanes = slice(l * LANES, (l + 1) * LANES)
            tile[l : l + 1, :] = tot[:, lanes]
            tile[3 + l : 4 + l, :] = cross[:, lanes]
        tile[6:8, :] = jnp.zeros((2, LANES), f32)
        met_all()
        send_tile(tile, slots, sends, recvs)
        vec_o[...] = jnp.zeros_like(vec_o)
        for k in range(17):
            vec_o[k : k + 1, :] = rowsum(acc[k])
        inb_o[...] = jnp.zeros_like(inb_o)
        for k in range(hidden // LANES):
            inb_o[k : k + 1, :] = rowsum(inb[:, k * LANES : (k + 1) * LANES])
        l3_t = l3s[...].T
        gm_t = gms[...].T
        for hf in range(2):
            cols = slice(hf * half, (hf + 1) * half)
            gin_o[hf] = dg(l3_t, gs[:, cols], 1, 0)
            pltpu.make_async_copy(gin_o.at[hf], gin_h.at[hf], gsem.at[0, hf]).start()
            gout_o[hf] = dg(gm_t, hs[:, cols], 1, 0)
            pltpu.make_async_copy(gout_o.at[hf], gout_h.at[hf], gsem.at[1, hf]).start()
        stat_o[...] = sum_tiles(tile, slots, sends, recvs)
        for n in range(own):
            for c in image_outs(n):
                c.wait()
        for hf in range(2):
            pltpu.make_async_copy(gin_o.at[hf], gin_h.at[hf], gsem.at[0, hf]).wait()
            pltpu.make_async_copy(gout_o.at[hf], gout_h.at[hf], gsem.at[1, hf]).wait()


def last_kernel(
    far,
    cls, sharp, tok_h, first, active, dgelu, gsec, gsh, low_h, q, k, v, mix_h, attn, gram, rs,
    st, gst, wt_h, wp_h, gains, offs, taps, scales,
    gin, gout, eq, ep, ei, eo, bq, bp, bi, bo, vec2, inb,
    ingrad_o, mq_o, mp_o, mi_o, mo_o, oq_o, op_o, oi_o, oo_o, rq_o, rp_o, ri_o, ro_o, rqs_o, vec_o,
    nat, mask, field, gfield, gback, gfirst, gproj, gals, acc, bias_acc, sharp_rows,
    mq, mp, mi, mo, fp, hi_, ho, ai, ao, aq, ap, gt, gp, vec3, qb, obuf, tok, low, mix, wt, wp, perm, hsem, lsem, psend, precv, osem,
    *exchange,
):
    lefts, rights, late = Spread(far, *exchange[0:11]), Spread(far, *exchange[11:22]), Spread(far, *exchange[22:33])
    left_qp = Broadcast(far, 0, *exchange[33:41])
    i = pl.program_id(0)
    t = lax.axis_index("tensor")
    own = cls.shape[0] // 2
    heads = sharp.shape[0]
    width = tok.shape[1]
    cells = tok.shape[0] // own
    head = width // heads
    other = {"tensor": 1 - t}
    part = width // 2
    cols_q = bq.shape[1]
    tiles_q = -(-cols_q // LANES)
    right_qp = Broadcast(far, tiles_q, *exchange[41:49])
    base = pl.multiple_of(i * cells, 16)
    here = pl.ds(base, cells)
    own_rows = pl.ds(pl.multiple_of(t * part, 8), part)
    loads = [
        pltpu.make_async_copy(src, dst, lsem.at[n])
        for n, (src, dst) in enumerate(
            ((gin.at[t], hi_), (gout.at[t], ho), (ei.at[0], mi), (eo.at[0], mo), (eq.at[0], mq), (ep.at[0], fp))
        )
    ]
    held = [
        pltpu.make_async_copy(src, dst, hsem.at[n])
        for n, (src, dst) in enumerate(
            ((tok_h, tok), (wp_h, wp), (low_h, low), (mix_h, mix), (wt_h, wt))
        )
    ]
    pair_in = [remote(gin.at[1 - t], ai, psend.at[0], precv.at[0], other), remote(gout.at[1 - t], ao, psend.at[1], precv.at[1], other)]
    pair_qp = [remote(gt.at[j, 1 - t], aq.at[j], psend.at[2 + j], precv.at[2 + j], other) for j in range(3)]
    pair_qp.append(remote(gp.at[1 - t], ap, psend.at[5], precv.at[5], other))
    stores = [
        pltpu.make_async_copy(src, dst, osem.at[n])
        for n, (src, dst) in enumerate(((mq, mq_o), (mp.at[own_rows], mp_o), (mi, mi_o), (mo, mo_o)))
    ]

    def image_out(n):
        rows = pl.ds(pl.multiple_of(n * cells, 16), cells)
        return pltpu.make_async_copy(gals.at[rows], ingrad_o.at[rows], osem.at[4 + n])

    @pl.when(i == 0)
    def _():
        greet(far)
        for c in held + loads:
            c.start()
        fill_perm(perm, heads // 2, head)
        mp[...] = jnp.zeros_like(mp)
        lefts.pay[...] = jnp.zeros_like(lefts.pay)
        rights.pay[...] = jnp.zeros_like(rights.pay)
        vec3[...] = jnp.zeros_like(vec3)
        qb[...] = jnp.zeros_like(qb)
        right_qp.x[...] = jnp.zeros_like(right_qp.x)
        sharp_rows[...] = jnp.zeros_like(sharp_rows)
        for h, (w, r) in enumerate(head_spots(heads, head)):
            sharp_rows[w, r : r + head, :] = jnp.full((head, 2 * LANES), 1.0, f32) * sharp[h]
        clear_edges(field)
        clear_edges(gfield)
        acc[...] = jnp.zeros_like(acc)
        bias_acc[...] = jnp.zeros_like(bias_acc)

    fill_mask(mask, side_of(cls, t * own + i))
    mk = cat3(mask[...].reshape(-1, LANES))
    mean, rstd, inv = batch_stats(st)
    gsum = lambda r: jnp.concatenate([gst[r : r + 1, :], gst[r + 1 : r + 2, :], gst[r + 2 : r + 3, :]], -1)
    gain_bn = gains[2:3, :]
    zhat = (active[...] - mean) * rstd
    gact = rstd * (gsh[...] * gain_bn - gsum(0) * gain_bn * inv - zhat * (gsum(3) * gain_bn * inv)) * mk
    put_field(gfield, gact * dgelu[...])
    normed, scale = layer_stats(first[...])
    put_field(field, (normed * gains[1:2, :] + offs[1:2, :]) * mk)
    for l in range(3):
        lanes = slice(l * LANES, (l + 1) * LANES)
        w = tap_rows(taps, 0, lanes)
        tap_sum = [jnp.zeros((8, LANES), f32) for _ in range(9)]

        def step(n, carry):
            tap_sum = list(carry)
            c0 = n * CHUNK
            gwin = gfield[:, pl.ds(c0, CHUNK + 2), :, lanes]
            fwin = field[:, pl.ds(c0, CHUNK + 2), :, lanes]
            conv = conv_chunk(gwin, w, CHUNK, True)
            center = gwin[1 : 1 + TRIO, 1 : 1 + CHUNK]
            for a in range(3):
                for b in range(3):
                    prod = fwin[a : a + TRIO, b : b + CHUNK] * center
                    tap_sum[3 * a + b] += jnp.sum(prod, (0, 1))
            for m in range(TRIO):
                rows, cells8 = chunk_rows(m, c0)
                gback[rows, lanes] = (conv[m] * mask[cells8]).reshape(CHUNK * 8, LANES)
            return tuple(tap_sum)

        tap_sum = lax.fori_loop(0, SIDE // CHUNK, step, tuple(tap_sum))
        for n in range(9):
            acc[7 + n, :, lanes] += tap_sum[n]

    @pl.when(i == 0)
    def _():
        met(far)
        for c in pair_in:
            c.start()
        for c in held:
            c.wait()

    @pl.when(i == own - 2)
    def _():
        for c in loads:
            c.wait()
        for c in pair_in:
            c.wait()
        mi[...] += hi_[...] + ai[...]
        mo[...] += (ho[...] + ao[...]).T
        stores[2].start()
        stores[3].start()
        li = tiles(thin(bi[...], mi[...], 1))
        lo = tiles(thin(bo[...], mo[...], 1))
        n = 0
        for tile in li:
            lefts.pay[n] = tile
            n += 1
        for m, tile in enumerate(lo):
            lefts.pay[n + t * len(lo) + m] = tile
        n += 2 * len(lo)
        for tile in row_tiles(vec2) + row_tiles(inb):
            lefts.pay[n] = tile
            n += 1
        lefts.start()

    @pl.when(i == own - 1)
    def _():
        lefts.gather()

    dout = gback[...]
    normed, scale = layer_stats(first[...])
    acc[2] += colsum(dout * normed)
    acc[3] += colsum(dout)
    grad = gsec[...] + norm_back(dout, normed, scale, gains[1:2, :])
    gfirst[here, :] = grad
    acc[5] += colsum(grad * (first[...] - tok[here, :].astype(f32)))
    gal = (grad * scales[0:1, :] * mk).astype(bf16)
    acc[4] += colsum(gal.astype(f32))
    gals[here, :] = gal
    gmix, gmix_lo = split2(dg(gal, wp[...], 1, 1))
    lane1 = lax.broadcasted_iota(jnp.int32, (1, width), 1)
    sharp_lane = jnp.zeros((1, width), f32)
    for h in range(heads):
        sharp_lane = jnp.where((lane1 >= h * head) & (lane1 < (h + 1) * head), sharp[h], sharp_lane)
    ones = jnp.ones((8, 2 * LANES), bf16)
    gval, gqu, gku, chan, chan_k = [], [], [], [], []
    for w in range(2):
        cols = slice(w * LANES, (w + 2) * LANES)
        gw, vw, kw, qw = gmix[:, cols], v[:, cols], k[:, cols], q[:, cols]
        a = attn[0, w]
        gattn = dg(gw, vw, 0, 0) + dg(gmix_lo[:, cols], vw, 0, 0)
        gval.append(dg(gw, a.astype(bf16), 1, 0))
        gsc = a * (gattn - jnp.sum(gattn * a, -1, keepdims=True))
        weighted = gsc * gram[0, w]
        hi, lo = split2(weighted)
        chan.append(dg(ones, hi, 1, 1) + dg(ones, lo, 1, 1))
        chan_k.append(rowsum(weighted * sharp_rows[w]))
        shi, slo = split2(gsc * sharp_rows[w])
        gqu.append(dg(kw, shi, 1, 1) + dg(kw, slo, 1, 1))
        gku.append(dg(qw, shi, 1, 0) + dg(qw, slo, 1, 0))
    chan = merge(*chan)[0:1, :]
    acc[6, 0:1, :] += chan
    gq = rs[0, 0:1, :] * (merge(*gqu) - q[...].astype(f32) * (chan * sharp_lane))
    gk = rs[0, 1:2, :] * (merge(*gku) - k[...].astype(f32) * merge(*chan_k))
    for j, piece in enumerate((gq, gk, merge(*gval))):
        small = piece.astype(bf16)
        gproj[here, j * width : (j + 1) * width] = small
        bias_acc[j] += colsum(small.astype(f32))

    @pl.when(i == own - 2)
    def _():
        lefts.middle()

    @pl.when(i == own - 1)
    def _():
        for j in range(3):
            gt[j] = dg(gproj[:, j * width : (j + 1) * width], low[...], 0, 0).reshape(2, part, width)
            pair_qp[j].start()
        gp[...] = dg(mix[...], gals[...], 0, 0).reshape(2, part, width)
        pair_qp[3].start()
        lefts.finish()
        tiles_i = width // LANES
        tiles_o = 2 * mo.shape[0] // LANES
        get = lambda a, b: jnp.concatenate([lefts.full[m] for m in range(a, b)], -1)
        oi, oo = orthonormal([get(0, tiles_i), get(tiles_i, tiles_i + tiles_o)])
        first_vec = tiles_i + tiles_o
        count2, count3 = vec2.shape[0] * 3 // 8, vec3.shape[0] * 3 // 8
        for m in range(count2):
            vec_o[m * 8 : m * 8 + 8, :] = lefts.full[first_vec + m]
        for m in range(2):
            at = (count2 + count3 + m) * 8
            vec_o[at : at + 8, :] = lefts.full[first_vec + count2 + m]
        half_o = mo.shape[0]
        obuf[0] = oo[:, :half_o]
        obuf[1] = oo[:, half_o:]
        oo_own = obuf[t]
        for c in pair_qp:
            c.wait_recv()
        turned = jnp.concatenate([gt[j, t] + aq[j] for j in range(3)], 0)
        grad_q = None
        for piece in split3(turned):
            term = dg(perm[...], piece, 0, 0)
            grad_q = term if grad_q is None else grad_q + term
        mq[...] += grad_q
        mp[own_rows, :] = gp[t] + ap[...] + fp[...]
        stores[0].start()
        stores[1].start()
        for m, tile in enumerate(tiles(thin(bq[...], mq[...], 0)) + tiles(thin(bp[...], mp[...], 1))):
            left_qp.x[m] = tile
        left_qp.start()
        ri = tiles(thin(oi, mi[...], 0))
        ro = tiles(thin(oo_own, mo[...], 0))
        for m, tile in enumerate(ri):
            rights.pay[t * len(ri) + m] = tile
        for m, tile in enumerate(ro):
            rights.pay[2 * len(ri) + m] = tile
        rights.start()

        def input_dout(n):
            rows = pl.ds(pl.multiple_of(n * cells, 16), cells)
            fill_mask(mask, side_of(cls, t * own + n))
            mk = cat3(mask[...].reshape(-1, LANES))
            dout = dg(gproj[rows, :], wt[...].reshape(3 * width, width), 1, 0) * mk
            normed, scale = layer_stats(tok[rows, :].astype(f32))
            return rows, mk, dout, normed, scale

        @pl.loop(0, own)
        def _(n):
            _, _, dout, normed, _ = input_dout(n)
            acc[0] += colsum(dout * normed)
            acc[1] += colsum(dout)

        def input_out(n):
            rows, mk, dout, normed, scale = input_dout(n)
            result = (gfirst[rows, :] + norm_back(dout, normed, scale, gains[0:1, :])) * mk
            from_canvas(result, nat, gals.at[rows])
            image_out(n).start()

        oi_o[...] = stacked(oi)[0].T
        oo_o[...] = stacked(oo_own)[0].T
        left_qp.middle()
        rights.middle()
        for n in range(16):
            vec3[n : n + 1, :] = rowsum(acc[n])
        vec3[5:6, :] = rowsum(acc[5]) / scales[0:1, :]
        third = perm.shape[0] // 3
        lane8 = lax.broadcasted_iota(jnp.int32, (8, width), 1)
        total = None
        for j in range(3):
            rows = perm[j * third : (j + 1) * third, :]
            both = jnp.concatenate([rows, rows], 0)
            pieces = []
            for hf in range(2):
                mine = jnp.where((lane8 >= hf * third) & (lane8 < (hf + 1) * third), bias_acc[j], 0.0)
                pieces += [piece.astype(f32) for piece in split3(mine)]
            term = dg(jnp.concatenate(pieces, 0).astype(bf16), both, 1, 0)
            total = term if total is None else total + term
        row = jnp.concatenate([rowsum(total[0:24]), rowsum(total[24:48])], -1)
        for n in range(row.shape[1] // LANES):
            qb[n : n + 1, :] = row[:, n * LANES : (n + 1) * LANES]
        for m, tile in enumerate(row_tiles(vec3) + row_tiles(qb)):
            late.pay[m] = tile
        late.start()
        rights.gather()
        pl.loop(0, 1)(input_out)
        total = left_qp.finish()
        oq, op = orthonormal(
            [jnp.concatenate([total[m] for m in range(3)], -1), jnp.concatenate([total[m] for m in range(3, 6)], -1)]
        )
        rq = thin(oq, mq[...], 1)
        for m in range(tiles_q):
            wide = min(LANES, cols_q - m * LANES)
            right_qp.x[m, :, 0:wide] = rq[:, m * LANES : m * LANES + wide]
        for m, tile in enumerate(tiles(thin(op, mp[...], 0))):
            right_qp.x[tiles_q + m] = tile
        right_qp.start()
        share = 1.0 / (far * NEAR)
        oq_o[...] = stacked(oq)[1]
        gback[0:width, 0:48] = stacked(op)[0].T
        op_o[...] = gback[own_rows, 0:48]
        late.middle()
        pl.loop(1, own - 1)(input_out)
        right_qp.middle()
        late.gather()
        pl.loop(own - 1, own)(input_out)
        rights.finish()
        for m in range(len(ri)):
            ri_o[:, m * LANES : (m + 1) * LANES] = rights.full[t * len(ri) + m] * share
        for m in range(len(ro)):
            ro_o[:, m * LANES : (m + 1) * LANES] = rights.full[2 * len(ri) + m] * share
        total = right_qp.finish() * share
        for m in range(tiles_q):
            wide = min(LANES, cols_q - m * LANES)
            rq_o[:, m * LANES : m * LANES + wide] = total[m][:, 0:wide]
        for m in range(3):
            rp_o[:, m * LANES : (m + 1) * LANES] = total[tiles_q + m]
        rqs_o[...] = stacked(rq_o[...])[0].T
        late.finish()
        for m in range(count3):
            vec_o[(count2 + m) * 8 : (count2 + m) * 8 + 8, :] = late.full[m]
        for m in range(2):
            at = (count2 + count3 + 2 + m) * 8
            vec_o[at : at + 8, :] = late.full[count3 + m]
        for c in pair_qp:
            c.wait_send()
        for group in (lefts, rights, late, left_qp, right_qp):
            group.drain()
        for c in stores + [image_out(n) for n in range(own)]:
            c.wait()


def orthonormal(rows):
    index = lax.broadcasted_iota(jnp.int32, rows[0].shape[:1] + (1,), 0)
    rank = rows[0].shape[0]
    for n in range(rank):
        done = []
        for v in rows:
            column = v[n : n + 1, :]
            dots = jnp.sum(v * column, -1, keepdims=True)
            scale = lax.rsqrt(dots[n : n + 1, :] + 1e-06)
            unit = column * scale
            later = v - (dots * scale) * unit
            done.append(jnp.where(index > n, later, jnp.where(index == n, unit, v)))
        rows = done
    return rows


class Spread:
    def __init__(self, far, pay, slots, part, tops, full, s1, r1, s2, r2, s3, r3):
        self.far, self.pay, self.slots, self.part, self.tops, self.full = far, pay, slots, part, tops, full
        self.sems = s1, r1, s2, r2, s3, r3
        self.per = slots.shape[1]
        self.hi, self.lo, self.t, self.me = place()

    def piece(self, ref, index):
        return ref.at[pl.ds(index * self.per, self.per)]

    def first(self, k, incoming):
        index, there = near_partner(self.me, self.hi, k)
        slot = index if incoming else self.me
        return remote(self.piece(self.pay, index), self.slots.at[slot], self.sems[0].at[k], self.sems[1].at[slot], there)

    def second(self, k, incoming):
        index, there = far_partner(self.hi, self.lo, self.t, k, self.far)
        slot = index if incoming else self.hi
        return remote(self.part, self.tops.at[slot], self.sems[2].at[k], self.sems[3].at[slot], there)

    def third(self, k, incoming):
        index, there = near_partner(self.me, self.hi, k)
        slot = index if incoming else self.me
        return remote(
            self.piece(self.full, self.me), self.piece(self.full, slot), self.sems[4].at[k], self.sems[5].at[slot], there
        )

    def start(self):
        for k in range(1, 2 * NEAR):
            self.first(k, False).start()
        self.slots[self.me] = self.pay[pl.ds(self.me * self.per, self.per)]

    def middle(self):
        for k in range(1, 2 * NEAR):
            self.first(k, True).wait_recv()
        total = jnp.sum(self.slots[...], 0)
        self.part[...] = total
        self.tops[self.hi] = total
        for k in range(1, self.far):
            self.second(k, False).start()

    def gather(self):
        for k in range(1, self.far):
            self.second(k, True).wait_recv()
        self.full[pl.ds(self.me * self.per, self.per)] = jnp.sum(self.tops[...], 0)
        for k in range(1, 2 * NEAR):
            self.third(k, False).start()

    def finish(self):
        for k in range(1, 2 * NEAR):
            self.third(k, True).wait_recv()

    def drain(self):
        for k in range(1, 2 * NEAR):
            self.first(k, False).wait_send()
            self.third(k, False).wait_send()
        for k in range(1, self.far):
            self.second(k, False).wait_send()


def spread_scratch(per, far):
    dma = pltpu.SemaphoreType.DMA
    near = 2 * NEAR
    vm = lambda *shape: pltpu.VMEM(shape + (8, LANES), f32)
    return [
        vm(near * per), vm(near, per), vm(per), vm(far, per), vm(near * per),
        dma((near,)), dma((near,)), dma((far,)), dma((far,)), dma((near,)), dma((near,)),
    ]


class Broadcast:
    def __init__(self, far, own, x, slots, part, tops, s1, r1, s2, r2):
        self.far, self.own, self.x, self.slots, self.part, self.tops = far, own, x, slots, part, tops
        self.sems = s1, r1, s2, r2
        self.hi, self.lo, self.t, self.me = place()

    def first(self, k, incoming):
        index, there = near_partner(self.me, self.hi, k)
        slot = index if incoming else self.me
        skip = self.own if k % 2 else 0
        count = self.x.shape[0] - skip
        return remote(
            self.x.at[pl.ds(skip, count)], self.slots.at[slot, pl.ds(skip, count)],
            self.sems[0].at[k], self.sems[1].at[slot], there,
        )

    def second(self, k, incoming):
        index, there = far_partner(self.hi, self.lo, self.t, k, self.far)
        slot = index if incoming else self.hi
        return remote(self.part, self.tops.at[slot], self.sems[2].at[k], self.sems[3].at[slot], there)

    def start(self):
        for k in range(1, 2 * NEAR):
            self.first(k, False).start()
        self.slots[self.me] = self.x[...]

    def middle(self):
        for k in range(1, 2 * NEAR):
            self.first(k, True).wait_recv()
        own = self.own
        if own:
            total = self.slots[self.t, 0:own]
            for k in range(1, NEAR):
                total = total + self.slots[2 * k + self.t, 0:own]
            self.part[0:own] = total
        self.part[own:] = jnp.sum(self.slots[:, own:], 0)
        self.tops[self.hi] = self.part[...]
        for k in range(1, self.far):
            self.second(k, False).start()

    def finish(self):
        for k in range(1, self.far):
            self.second(k, True).wait_recv()
        return jnp.sum(self.tops[...], 0)

    def drain(self):
        for k in range(1, 2 * NEAR):
            self.first(k, False).wait_send()
        for k in range(1, self.far):
            self.second(k, False).wait_send()


def broadcast_scratch(count, far):
    dma = pltpu.SemaphoreType.DMA
    near = 2 * NEAR
    vm = lambda *shape: pltpu.VMEM(shape + (8, LANES), f32)
    return [vm(count), vm(near, count), vm(count), vm(far, count), dma((near,)), dma((near,)), dma((far,)), dma((far,))]


def row_tiles(ref):
    return [
        ref[r * 8 : r * 8 + 8, c * LANES : (c + 1) * LANES]
        for c in range(ref.shape[1] // LANES)
        for r in range(ref.shape[0] // 8)
    ]


def tiles(x):
    return [x[:, n * LANES : (n + 1) * LANES] for n in range(x.shape[1] // LANES)]


def stacked(x):
    hi, mid, lo = split3(x)
    hi, mid, lo = hi.astype(f32), mid.astype(f32), lo.astype(f32)
    left = jnp.concatenate([hi, hi, mid, hi, mid, lo], 0)
    right = jnp.concatenate([hi, mid, hi, lo, mid, hi], 0)
    return left, right


def update_kernel(
    oq, op, oi, oo, rqs, rp, ri, ro, rq, mq, mp, mi, mo, wq, wp, wi, wo, vq, vp, vi, vo,
    vec, one, two, gains, offs, taps, scales, bq, sharp, bi, gains_v, offs_v, taps_v, scales_v, bq_v, sharp_v, bi_v,
    wq_o, wp_o, wi_o, wo_o, vq_o, vp_o, vi_o, vo_o, eq_o, ep_o, ei_o, eo_o,
    gains_o, offs_o, taps_o, scales_o, bq_o, sharp_o, bi_o,
    gains_m, offs_m, taps_m, scales_m, bq_m, sharp_m, bi_m, tq_o, tp_o, ti_o, to_o, one_o, two_o,
    *, share,
):
    one_o[...] = one[...]
    two_o[...] = two[...]
    groups = (
        (oq, None, mq, wq, vq, wq_o, vq_o, eq_o),
        (op, rp, mp, wp, vp, wp_o, vp_o, ep_o),
        (oi, ri, mi, wi, vi, wi_o, vi_o, ei_o),
        (oo, ro, mo, wo, vo, wo_o, vo_o, eo_o),
    )
    for o, r, m, w, v, w_o, v_o, e_o in groups:
        if r is None:
            approx = dg(rqs[...].astype(bf16), o[...].astype(bf16), 1, 0)
        else:
            approx = dg(o[...].astype(bf16), stacked(r[...])[1].astype(bf16), 1, 0)
        moment = momentum_decay * v[...] + approx
        v_o[...] = moment
        w_o[...] = w[...] - learn_rate * moment
        e_o[0] = m[...] - approx

    @pl.when(pl.program_id(0) == 0)
    def _():
        for r, t_o in ((rq, tq_o), (rp, tp_o), (ri, ti_o), (ro, to_o)):
            t_o[...] = r[...]

        def step(grad, value, moment, v_out, m_out, rows):
            new = momentum_decay * moment[rows, :] + grad * share
            m_out[rows, :] = new
            v_out[rows, :] = value[rows, :] - learn_rate * new

        def row2(a, b):
            return jnp.concatenate([vec[24 * c + a : 24 * c + b, :] for c in range(3)], -1)

        def row3(a, b):
            return jnp.concatenate([vec[72 + 16 * c + a : 72 + 16 * c + b, :] for c in range(3)], -1)

        def each(grads, value, moment, v_out, m_out):
            for n, g in enumerate(grads):
                step(g, value, moment, v_out, m_out, slice(n, n + 1))

        each([row3(0, 1), row3(2, 3), row2(6, 7), row2(1, 2)], gains, gains_v, gains_o, gains_m)
        each(
            [row3(1, 2), row3(3, 4), row2(7, 8), row2(0, 1), row3(4, 5), row2(2, 3), row2(3, 4)],
            offs, offs_v, offs_o, offs_m,
        )
        each([row3(5, 6), row2(4, 5), row2(5, 6)], scales, scales_v, scales_o, scales_m)
        each([row3(7 + n, 8 + n) for n in range(9)] + [row2(8 + n, 9 + n) for n in range(9)],
             taps, taps_v, taps_o, taps_m)
        base = 72 + 48
        half = bi.shape[0]
        step(vec[base : base + half, :], bi, bi_v, bi_o, bi_m, slice(None))
        base += 16
        step(vec[base : base + bq.shape[0], :], bq, bq_v, bq_o, bq_m, slice(None))
        width = gains.shape[1]
        heads = sharp.shape[1]
        head = width // heads
        chan = lax.broadcasted_iota(jnp.int32, (width, heads), 0)
        lane = lax.broadcasted_iota(jnp.int32, (width, heads), 1)
        pick = jnp.where((chan >= lane * head) & (chan < (lane + 1) * head), 1.0, 0.0).astype(f32)
        grad = thin(jnp.broadcast_to(row3(6, 7), (8, width)), pick, 0)
        step(grad[0:1, :], sharp, sharp_v, sharp_o, sharp_m, slice(None))


def body(
    tokens, classes, loss,
    tri, tri_b, sharp, mapw, expw, exp_b, conw, gains, offs, taps, scales,
    tri_v, map_v, exp_v, con_v, tri_b_v, sharp_v, exp_b_v, gains_v, offs_v, taps_v, scales_v,
    tri_e, map_e, exp_e, con_e, tri_f, map_f, exp_f, con_f,
):
    import functools

    far = lax.axis_size("dp") // NEAR
    rows, width = tokens.shape
    own = classes.shape[0] // 2
    cells = rows // own
    heads = sharp.shape[0]
    head = width // heads
    part = width // 2
    cols = tri.shape[1]
    half = expw.shape[1]
    hidden = 2 * half
    vm = pl.BlockSpec(memory_space=pltpu.VMEM)
    sm = pl.BlockSpec(memory_space=pltpu.SMEM)
    anyspace = pl.BlockSpec(memory_space=pl.ANY)

    def whole(*shape):
        return pl.BlockSpec(shape, lambda i: (0,) * len(shape), pipeline_mode=pl.Buffered(1))

    image = pl.BlockSpec((cells, width), lambda i: (i, 0))
    square = pl.BlockSpec((1, 2, 2 * LANES, 2 * LANES), lambda i: (i, 0, 0, 0))
    eight = pl.BlockSpec((1, 8, width), lambda i: (i, 0, 0))
    smem = pl.BlockSpec(memory_space=pltpu.SMEM)
    vecs = [whole(4, width), whole(7, width), whole(18, width), whole(3, width)]
    field = pltpu.VMEM((TRIO + 2, SIDE + 2, GROUPS, width), f32)
    nat = pltpu.VMEM((3, cells, LANES), f32)
    mask = pltpu.VMEM((TRIO * SIDE, GROUPS, LANES), f32)
    canvas = pltpu.VMEM((cells, width), f32)

    dma = pltpu.SemaphoreType.DMA
    devices = lax.axis_size("dp") * 2
    two_windows = pltpu.VMEM((2, 2 * LANES, 2 * LANES), f32)
    tile_exchange = [
        pltpu.VMEM((8, LANES), f32), pltpu.VMEM((devices, 8, LANES), f32),
    ]
    first, active, dgelu, low, q, k, v, mix, xc, attn, gram, rs, stat, lc, wt, wp, win, wout = pl.pallas_call(
        first_kernel,
        grid=(own,),
        out_shape=[sds((rows, width))] * 3
        + [sds((rows, width), bf16)] * 6
        + [sds((own, 2, 2 * LANES, 2 * LANES))] * 2
        + [sds((own, 8, width)), sds((8, LANES)), sds((rows, width), bf16)]
        + [sds((3, 2, part, width), bf16), sds((2, part, width), bf16),
           sds((2, width, half), bf16), sds((2, half, width), bf16)],
        in_specs=[smem, smem, image, whole(cols, width), whole(part, width), whole(2 * cols // LANES, LANES)]
        + vecs + [anyspace] * 3,
        out_specs=[anyspace] * 11 + [eight, whole(8, LANES)] + [anyspace] * 5,
        scratch_shapes=[
            nat, mask, canvas, field, two_windows, two_windows, pltpu.VMEM((2, 8, width), f32),
            pltpu.VMEM((3, 2, part, width), bf16), pltpu.VMEM((2, part, width), bf16),
            pltpu.VMEM((2, width, half), bf16), pltpu.VMEM((2, half, width), bf16),
            pltpu.VMEM((width, half), f32), pltpu.VMEM((half, width), f32), pltpu.VMEM((rows, width), bf16), mask,
            pltpu.VMEM((cols, cols), bf16), pltpu.VMEM((8, width), f32),
        ] + [pltpu.VMEM((rows, width), f32)] * 3 + [pltpu.VMEM((rows, width), bf16)] * 6
        + [pltpu.VMEM((own, 2, 2 * LANES, 2 * LANES), f32)] * 2 + [pltpu.VMEM((rows, width), bf16)]
        + tile_exchange + [dma((11, own)), dma((5,)), dma((6,)), dma((6,)), dma((devices,)), dma((devices,))],
        compiler_params=params(collective_id=0, has_side_effects=True),
        name="first_part",
    )(classes, sharp, tokens, tri.T, mapw, tri_b.reshape(-1, LANES), gains, offs, taps, scales, expw, conw, loss)
    wt = wt.reshape(3, width, width)
    wp = wp.reshape(width, width)

    block_out, gsec, gsh, gin, gout, vec2, inb, gstat = pl.pallas_call(
        middle_kernel,
        grid=(own,),
        out_shape=[
            sds((rows, width), bf16), sds((rows, width)), sds((rows, width)),
            sds((2, width, half)), sds((2, width, half)), sds((24, width)), sds((16, LANES)), sds((8, LANES)),
        ],
        in_specs=[smem, image, image, image, whole(8, LANES), anyspace, anyspace,
                  whole(hidden // LANES, LANES)] + vecs,
        out_specs=[anyspace] * 5 + [whole(24, width), whole(16, LANES), whole(8, LANES)],
        scratch_shapes=[
            nat, mask, field, field, canvas, canvas, canvas,
            pltpu.VMEM((rows, width), bf16), pltpu.VMEM((rows, width), bf16),
            pltpu.VMEM((rows, hidden), bf16), pltpu.VMEM((rows, hidden), bf16),
            pltpu.VMEM((17, 8, width), f32), pltpu.VMEM((8, hidden), f32),
            pltpu.VMEM((2, width, half), bf16), pltpu.VMEM((2, half, width), bf16),
            pltpu.VMEM((rows, width), bf16), pltpu.VMEM((rows, width), f32), pltpu.VMEM((rows, width), f32),
            pltpu.VMEM((2, width, half), f32), pltpu.VMEM((2, width, half), f32),
            dma((3, own)), dma((2, 2)), dma((2,)),
        ] + tile_exchange + [dma((devices,)), dma((devices,))],
        compiler_params=params(collective_id=1, has_side_effects=True),
        name="middle_part",
    )(classes, first, active, lc, stat, win, wout, exp_b.reshape(hidden // LANES, LANES), gains, offs, taps, scales)
    input_grad, mq, mp, mi, mo, oq, op, oi, oo, rq, rp, ri, ro, rqs, vec = pl.pallas_call(
        functools.partial(last_kernel, far),
        grid=(own,),
        out_shape=[
            sds((rows, width), bf16),
            sds((cols, width)), sds((part, width)), sds((width, half)), sds((half, width)),
            sds((48, width)), sds((part, 48)), sds((width, 48)), sds((half, 48)),
            sds((8, cols)), sds((8, width)), sds((8, half)), sds((8, width)), sds((cols, 48)), sds((152, LANES)),
        ],
        in_specs=[smem, smem, anyspace] + [image] * 5 + [anyspace] + [image] * 3
        + [anyspace] + [square, square, eight, whole(8, LANES), whole(8, LANES)] + [anyspace] * 2 + vecs
        + [anyspace] * 6 + [whole(8, cols), whole(8, width), whole(8, half), whole(8, width),
                  whole(24, width), whole(16, LANES)],
        out_specs=[anyspace] * 5 + [
            whole(48, width), whole(part, 48), whole(width, 48), whole(half, 48),
            whole(8, cols), whole(8, width), whole(8, half), whole(8, width), whole(cols, 48), whole(152, LANES),
        ],
        scratch_shapes=[
            nat, mask, field, field, canvas, pltpu.VMEM((rows, width), f32),
            pltpu.VMEM((rows, 3 * width), bf16), pltpu.VMEM((rows, width), bf16),
            pltpu.VMEM((16, 8, width), f32), pltpu.VMEM((3, 8, width), f32), two_windows,
            pltpu.VMEM((cols, width), f32), pltpu.VMEM((width, width), f32),
            pltpu.VMEM((width, half), f32), pltpu.VMEM((half, width), f32), pltpu.VMEM((part, width), f32),
            pltpu.VMEM((width, half), f32), pltpu.VMEM((width, half), f32),
            pltpu.VMEM((width, half), f32), pltpu.VMEM((width, half), f32),
            pltpu.VMEM((3, part, width), f32), pltpu.VMEM((part, width), f32),
            pltpu.VMEM((3, 2, part, width), f32), pltpu.VMEM((2, part, width), f32),
            pltpu.VMEM((16, width), f32), pltpu.VMEM((16, LANES), f32),
            pltpu.VMEM((2, 8, half), f32),
            pltpu.VMEM((rows, width), bf16), pltpu.VMEM((rows, width), bf16), pltpu.VMEM((rows, width), bf16),
            pltpu.VMEM((3, width, width), bf16), pltpu.VMEM((width, width), bf16), pltpu.VMEM((cols, cols), bf16),
            dma((6,)), dma((6,)), dma((6,)), dma((6,)), dma((4 + own,)),
        ]
        + spread_scratch(4, far) + spread_scratch(2, far) + spread_scratch(1, far)
        + broadcast_scratch(6, far) + broadcast_scratch(-(-cols // LANES) + 3, far),
        compiler_params=params(collective_id=2, has_side_effects=True),
        name="last_part",
    )(classes, sharp, xc, first, active, dgelu, gsec, gsh, low, q, k, v, mix, attn, gram, rs, stat, gstat,
      wt, wp, gains, offs, taps, scales, gin, gout, tri_e.swapaxes(1, 2), map_e, exp_e, con_e,
      tri_f.T, map_f.T, exp_f.T, con_f.T, vec2, inb)

    steps = 2

    def cut(n, m):
        return pl.BlockSpec((n // steps, m), lambda i: (i, 0))

    def cut3(n, m):
        return pl.BlockSpec((1, n // steps, m), lambda i: (0, i, 0))

    wide = lambda x: x.reshape(-1, LANES)
    mats = [cut(cols, width), cut(part, width), cut(width, half), cut(half, width)]
    small_specs = vecs + [whole(2 * cols // LANES, LANES), whole(1, heads), whole(hidden // LANES, LANES)]
    basis_specs = [whole(8, cols), whole(8, width), whole(8, half), whole(8, width)]
    basis_shapes = [sds((8, cols)), sds((8, width)), sds((8, half)), sds((8, width))]
    small_shapes = [sds((4, width)), sds((7, width)), sds((18, width)), sds((3, width)), sds((2 * cols // LANES, LANES)), sds((1, heads)), sds((hidden // LANES, LANES))]
    mat_shapes = [sds((cols, width)), sds((part, width)), sds((width, half)), sds((half, width))]
    res = pl.pallas_call(
        functools.partial(update_kernel, share=1.0 / (far * NEAR)),
        grid=(steps,),
        out_shape=mat_shapes * 2
        + [sds((1, cols, width)), sds((1, part, width)), sds((1, width, half)), sds((1, half, width))]
        + small_shapes * 2 + basis_shapes + [sds((rows, width), bf16)] * 2,
        in_specs=[whole(48, width), cut(part, 48), cut(width, 48), cut(half, 48),
                  cut(cols, 48), whole(8, width), whole(8, half), whole(8, width), whole(8, cols)]
        + mats * 3 + [whole(152, LANES)] + [cut(rows, width)] * 2 + small_specs * 2,
        out_specs=mats * 2
        + [cut3(cols, width), cut3(part, width), cut3(width, half), cut3(half, width)]
        + small_specs * 2 + basis_specs + [cut(rows, width)] * 2,
        compiler_params=params(),
        name="update",
    )(oq, op, oi, oo, rqs, rp, ri, ro, rq, mq, mp, mi, mo, tri.T, mapw, expw, conw, tri_v.T, map_v, exp_v, con_v,
      vec, block_out, input_grad, gains, offs, taps, scales, wide(tri_b), sharp.reshape(1, heads), wide(exp_b),
      gains_v, offs_v, taps_v, scales_v, wide(tri_b_v), sharp_v.reshape(1, heads), wide(exp_b_v))
    nw, nv, ne, sv, smo, nt = res[0:4], res[4:8], res[8:12], res[12:19], res[19:26], res[26:30]
    block_out, input_grad = res[30:32]
    nw, nv = [nw[0].T, *nw[1:]], [nv[0].T, *nv[1:]]
    ne = [ne[0].swapaxes(1, 2), *ne[1:]]
    nt = [x.T for x in nt]

    def small(x):
        g, o, t_, s, b, sh, bi_ = x
        return (b.reshape(-1), sh.reshape(-1), bi_.reshape(-1), g, o, t_, s)

    return (
        (block_out, input_grad) + tuple(nw) + small(sv) + tuple(nv) + small(smo) + tuple(ne) + tuple(nt)
    )


def solution(mesh):
    rows = P(("dp", "tensor"), None)
    col, row = P(None, "tensor"), P("tensor", None)
    rep = P()
    err = (P("dp", None, "tensor"), P("dp", "tensor", None), P("dp", None, "tensor"), P("dp", "tensor", None))
    mats = (col, row, col, row)
    in_specs = (
        (rows, P("dp"), rows, col, rep, rep, row, col, rep, row, rep, rep, rep, rep)
        + mats + (rep,) * 7 + err + (row, rep, row, rep)
    )
    out_specs = (rows, rows) + mats + (rep,) * 7 + mats + (rep,) * 7 + err + (row, rep, row, rep)
    return jax.shard_map(body, mesh=mesh, in_specs=in_specs, out_specs=out_specs, check_vma=False)
```

```python
import jax
import jax.numpy as jnp
from jax import lax
from jax.experimental import pallas as pl
from jax.experimental.pallas import tpu as pltpu
from jax.sharding import PartitionSpec as P

SIDE = 24
GROUPS = 8
TRIO = 3
LANES = 128
NEAR = 4
learn_rate = 0.02
momentum_decay = 0.9
f32 = jnp.float32
bf16 = jnp.bfloat16
MESH = pl.DeviceIdType.MESH
HALF_ROOT = 0.7071067811865476
GAUSS = 0.3989422804014327


def sds(shape, dtype=f32):
    return jax.ShapeDtypeStruct(shape, dtype)


def params(mib, **kw):
    return pltpu.CompilerParams(vmem_limit_bytes=mib << 20, **kw)


def held(shape, dtype=f32):
    return pltpu.VMEM(shape, dtype)


def dg(a, b, ca, cb):
    return lax.dot_general(
        a, b, (((ca,), (cb,)), ((), ())), preferred_element_type=f32
    )


def thin(a, m, cb):
    pieces = jnp.concatenate([x.astype(f32) for x in split3(a)], 0).astype(bf16)
    hi, lo = split2(m)
    total = dg(pieces, hi, 1, cb) + dg(pieces, lo, 1, cb)
    rows = a.shape[0]
    return total[0:rows] + total[rows : 2 * rows] + total[2 * rows :]


def cat3(m):
    return jnp.concatenate([m, m, m], -1)


def split2(x):
    hi = x.astype(bf16)
    return hi, (x - hi.astype(f32)).astype(bf16)


def split3(x):
    hi = x.astype(bf16)
    rest = x - hi.astype(f32)
    mid = rest.astype(bf16)
    return hi, mid, (rest - mid.astype(f32)).astype(bf16)


def dg2(a, b, ca, cb):
    hi, lo = split2(a)
    return dg(hi, b, ca, cb) + dg(lo, b, ca, cb)


def mean_of(x):
    return jnp.sum(x, -1, keepdims=True) * (1.0 / x.shape[-1])


def layer_stats(x):
    center = x - mean_of(x)
    scale = lax.rsqrt(mean_of(center * center) + 1e-06)
    return center * scale, scale


def norm_back(grad_out, normed, scale, gain):
    grad_normed = grad_out * gain
    return scale * (
        grad_normed - mean_of(grad_normed) - normed * mean_of(grad_normed * normed)
    )


def colsum(x):
    return jnp.sum(x.reshape(x.shape[0] // 8, 8, x.shape[1]), 0)


def rowsum(x):
    return jnp.sum(x, 0, keepdims=True)


def gelu_pair(x):
    phi = 0.5 + 0.5 * lax.erf(x * HALF_ROOT)
    return x * phi, phi + x * jnp.exp(-0.5 * x * x) * GAUSS


def side_of(cls_ref, index):
    bucket = cls_ref[index]
    return SIDE * (7 + 2 * bucket + lax.div(bucket, 2)) // 12


def fill_mask(mask, side):
    shape = (SIDE, GROUPS, LANES)
    col = lax.broadcasted_iota(jnp.int32, shape, 0)
    group = lax.broadcasted_iota(jnp.int32, shape, 1)
    for m in range(TRIO):
        inside = (group * TRIO + m < side) & (col < side)
        mask[pl.ds(m * SIDE, SIDE)] = jnp.where(inside, 1.0, 0.0).astype(f32)


def to_canvas(src, nat, dst):
    per = TRIO * SIDE
    for l in range(3):
        nat[l] = src[:, l * LANES : (l + 1) * LANES].astype(f32)
    for j in range(per):
        for l in range(3):
            dst[pl.ds(j * 8, 8), l * LANES : (l + 1) * LANES] = nat[
                l, pl.ds(j, GROUPS, stride=per), :
            ]


def from_canvas(value, nat, dst):
    per = TRIO * SIDE
    for j in range(per):
        for l in range(3):
            nat[l, pl.ds(j, GROUPS, stride=per), :] = value[
                j * 8 : j * 8 + 8, l * LANES : (l + 1) * LANES
            ]
    for l in range(3):
        dst[:, l * LANES : (l + 1) * LANES] = nat[l].astype(bf16)


def clear_edges(field):
    zero = jnp.zeros((TRIO + 2, 1, GROUPS, field.shape[-1]), f32)
    field[:, 0:1] = zero
    field[:, SIDE + 1 : SIDE + 2] = zero


def put_field(field, value):
    v = value.reshape(TRIO, SIDE, GROUPS, value.shape[-1])
    group = lax.broadcasted_iota(jnp.int32, (SIDE, GROUPS, value.shape[-1]), 1)
    field[1 : TRIO + 1, 1 : SIDE + 1] = v
    field[0, 1 : SIDE + 1] = jnp.where(group == 0, 0.0, pltpu.roll(v[TRIO - 1], 1, 1))
    field[TRIO + 1, 1 : SIDE + 1] = jnp.where(
        group == GROUPS - 1, 0.0, pltpu.roll(v[0], GROUPS - 1, 1)
    )


def conv_chunk(win, weights, width, flip):
    total = None
    for a in range(3):
        for b in range(3):
            ra, rb = (2 - a, 2 - b) if flip else (a, b)
            term = weights[3 * a + b] * win[ra : ra + TRIO, rb : rb + width]
            total = term if total is None else total + term
    return total


def tap_rows(taps, first, lanes):
    return [
        jnp.broadcast_to(taps[first + k : first + k + 1, lanes], (GROUPS, LANES)) for k in range(9)
    ]


CHUNK = 6


def chunk_rows(m, c0):
    return pl.ds(pl.multiple_of((m * SIDE + c0) * 8, 16), CHUNK * 8), pl.ds(m * SIDE + c0, CHUNK)


def near_partner(me, hi, k):
    index = lax.rem(me + k, 2 * NEAR)
    return index, {"dp": hi * NEAR + lax.div(index, 2), "tensor": lax.rem(index, 2)}


def place():
    dp = lax.axis_index("dp")
    t = lax.axis_index("tensor")
    hi = lax.div(dp, NEAR)
    lo = lax.rem(dp, NEAR)
    return hi, lo, t, lo * 2 + t


def greet(far):
    hi, lo, t, me = place()
    barrier = pltpu.get_barrier_semaphore()
    for k in range(1, 2 * NEAR):
        pl.semaphore_signal(
            barrier, inc=1, device_id=near_partner(me, hi, k)[1], device_id_type=MESH
        )
    for k in range(1, far):
        there = {"dp": lax.rem(hi + k, far) * NEAR + lo, "tensor": t}
        pl.semaphore_signal(barrier, inc=1, device_id=there, device_id_type=MESH)


def met(far):
    pl.semaphore_wait(pltpu.get_barrier_semaphore(), 2 * NEAR - 1 + far - 1)


def remote(src, dst, send, recv, there):
    return pltpu.make_async_remote_copy(
        src_ref=src, dst_ref=dst, send_sem=send, recv_sem=recv, device_id=there, device_id_type=MESH
    )


def far_partner(hi, lo, t, k, far):
    index = lax.rem(hi + k, far)
    return index, {"dp": index * NEAR + lo, "tensor": t}


def all_partners():
    n = lax.axis_size("dp") * 2
    me = lax.axis_index("dp") * 2 + lax.axis_index("tensor")
    out = []
    for k in range(1, n):
        index = lax.rem(me + k, n)
        out.append((index, {"dp": lax.div(index, 2), "tensor": lax.rem(index, 2)}))
    return me, out


def greet_all():
    barrier = pltpu.get_barrier_semaphore()
    for _, there in all_partners()[1]:
        pl.semaphore_signal(barrier, inc=1, device_id=there, device_id_type=MESH)


def met_all():
    pl.semaphore_wait(pltpu.get_barrier_semaphore(), lax.axis_size("dp") * 2 - 1)


def send_tile(tile, slots, sends, recvs):
    me, partners = all_partners()
    for k, (_, there) in enumerate(partners):
        remote(tile, slots.at[me], sends.at[k], recvs.at[me], there).start()
    slots[me] = tile[...]


def sum_tiles(tile, slots, sends, recvs):
    me, partners = all_partners()
    for k, (index, there) in enumerate(partners):
        remote(tile, slots.at[index], sends.at[k], recvs.at[index], there).wait_recv()
    total = jnp.sum(slots[...], 0)
    for k, (index, there) in enumerate(partners):
        remote(tile, slots.at[index], sends.at[k], recvs.at[index], there).wait_send()
    return total


def fill_perm(perm, heads, head):
    shape = (head, perm.shape[1])
    row = lax.broadcasted_iota(jnp.int32, shape, 0)
    lane = lax.broadcasted_iota(jnp.int32, shape, 1)
    for j in range(3):
        for h in range(heads):
            at = (j * heads + h) * head
            perm[at : at + head, :] = jnp.where(lane == row + (3 * h + j) * head, 1.0, 0.0).astype(bf16)


def windows(x):
    return x[:, 0 : 2 * LANES], x[:, LANES : 3 * LANES]


def merge(a, b):
    return jnp.concatenate([a[:, :LANES], a[:, LANES:] + b[:, :LANES], b[:, LANES:]], -1)


def head_spots(heads, head):
    return [(2 * h // heads, h * head - LANES * (2 * h // heads)) for h in range(heads)]


def batch_stats(st):
    row = lambda r: jnp.concatenate([st[r : r + 1, :], st[r + 1 : r + 2, :], st[r + 2 : r + 3, :]], -1)
    inv = cat3(1.0 / st[6:7, :])
    mean = row(0) * inv
    var = row(3) * inv - mean * mean
    return mean, lax.rsqrt(var + 1e-05), inv


def first_kernel(
    cls, sharp, tok, tri, mapw, tri_b, gains, offs, taps, scales, expw, conw, loss,
    first_h, active_h, dgelu_h, low_h, q_h, k_h, v_h, mix_h, xc_h, attn_h, gram_h, rs_o, stat_o, lc_h,
    wt_o, wp_o, win_o, wout_o,
    nat, mask, xm, field, sharp_rows, in_block, sums, wt, wp, win, wout, fexp, fcon, floss, masks, perm, bq,
    first_s, active_s, dgelu_s, low_s, q_s, k_s, v_s, mix_s, xc_s, attn_s, gram_s, lc_s, tile, slots,
    osem, lsem, wsend, wrecv, sends, recvs,
):
    i = pl.program_id(0)
    t = lax.axis_index("tensor")
    own = cls.shape[0] // 2
    heads = sharp.shape[0]
    cells, width = tok.shape
    head = width // heads
    other = {"tensor": 1 - t}
    spots = [wt.at[0], wt.at[1], wt.at[2], wp, win, wout]

    def out_copy(n):
        ref = spots[n]
        return remote(ref.at[t], ref.at[t], wsend.at[n], wrecv.at[n], other)

    def in_copy(n):
        ref = spots[n]
        return remote(ref.at[1 - t], ref.at[1 - t], wsend.at[n], wrecv.at[n], other)

    here = pl.ds(pl.multiple_of(i * cells, 16), cells)
    images = [(first_s, first_h), (active_s, active_h), (dgelu_s, dgelu_h), (low_s, low_h), (q_s, q_h), (k_s, k_h),
              (v_s, v_h), (mix_s, mix_h), (xc_s, xc_h)]
    squares = [(attn_s, attn_h), (gram_s, gram_h)]

    def image_outs(n):
        rows = pl.ds(n * cells if isinstance(n, int) else pl.multiple_of(n * cells, 16), cells)
        copies = [pltpu.make_async_copy(a.at[rows], b.at[rows], osem.at[k, n]) for k, (a, b) in enumerate(images)]
        return copies + [
            pltpu.make_async_copy(a.at[n], b.at[n], osem.at[len(images) + k, n]) for k, (a, b) in enumerate(squares)
        ]

    first_o, active_o, dgelu_o, low_o, q_o, k_o, v_o, mix_o, xc_o = [a.at[here] for a, _ in images]
    loads = [
        pltpu.make_async_copy(expw, fexp, lsem.at[0]),
        pltpu.make_async_copy(conw, fcon, lsem.at[1]),
        pltpu.make_async_copy(loss, floss, lsem.at[2]),
    ]

    @pl.when(i == 0)
    def _():
        greet_all()
        for c in loads:
            c.start()
        fill_perm(perm, heads // 2, head)
        turned = dg(perm[...], tri[...].astype(bf16), 1, 0).astype(bf16)
        part = turned.shape[0] // 3
        bias = jnp.concatenate([tri_b[n : n + 1, :] for n in range(tri_b.shape[0])], -1)
        pieces = jnp.concatenate([x.astype(f32) for x in split3(jnp.broadcast_to(bias, (8, bias.shape[1])))], 0)
        pieces = pieces.astype(bf16)
        sides = []
        for hf in range(2):
            turned_b = dg(pieces[:, hf * 3 * part : (hf + 1) * 3 * part], perm[...], 1, 1)
            sides.append(turned_b[0:1] + turned_b[8:9] + turned_b[16:17])
        for j in range(3):
            bq[j : j + 1, :] = jnp.concatenate([side[:, j * part : (j + 1) * part] for side in sides], -1)
        for j in range(3):
            wt[j, t] = turned[j * part : (j + 1) * part]
        wp[t] = mapw[...].astype(bf16)
        lane = lax.broadcasted_iota(jnp.int32, (head, 2 * LANES), 1)
        sharp_rows[...] = jnp.zeros_like(sharp_rows)
        in_block[...] = jnp.zeros_like(in_block)
        for h, (w, r) in enumerate(head_spots(heads, head)):
            inside = (lane >= r) & (lane < r + head)
            sharp_rows[w, r : r + head, :] = jnp.where(inside, sharp[h], 0.0)
            in_block[w, r : r + head, :] = jnp.where(inside, 1.0, 0.0)
        clear_edges(field)
        sums[...] = jnp.zeros_like(sums)
        loads[0].wait()
        loads[1].wait()
        win[t] = fexp[...].astype(bf16)
        wout[t] = fcon[...].astype(bf16)

    fill_mask(mask, side_of(cls, t * own + i))
    mk = cat3(mask[...].reshape(-1, LANES))
    to_canvas(tok, nat, xm)
    x = xm[...] * mk
    xc_o[...] = x.astype(bf16)
    normed, _ = layer_stats(x)
    low_o[...] = ((normed * gains[0:1, :] + offs[0:1, :]) * mk).astype(bf16)

    @pl.when(i == 0)
    def _():
        met_all()
        for n in range(4):
            out_copy(n).start()
        for n in range(4):
            in_copy(n).wait_recv()
        for n in range(4, 6):
            out_copy(n).start()

    low = low_o[...]
    lows = []
    for j in range(2):
        value = (dg(low, wt[j].reshape(width, width), 1, 1) + bq[j : j + 1, :]) * mk
        scale = lax.rsqrt(rowsum(value * value) + 1e-06)
        rs_o[i, j : j + 1, :] = scale
        unit = (value * scale).astype(bf16)
        (q_o, k_o)[j][...] = unit
        lows.append(windows(unit))
    value_low = ((dg(low, wt[2].reshape(width, width), 1, 1) + bq[2:3, :]) * mk).astype(bf16)
    v_o[...] = value_low
    parts = []
    for w in range(2):
        gram = dg(lows[0][w], lows[1][w], 0, 0)
        gram_s[i, w] = gram
        inside = in_block[w]
        logits = jnp.where(inside > 0.0, gram * sharp_rows[w], -1e30)
        powers = jnp.exp(logits - jnp.max(logits, -1, keepdims=True)) * inside
        attn = powers / jnp.maximum(jnp.sum(powers, -1, keepdims=True), 0.5)
        attn_s[i, w] = attn
        parts.append(dg(windows(value_low)[w], attn.astype(bf16), 1, 1))
    mixed = merge(*parts).astype(bf16)
    mix_o[...] = mixed
    branch = dg(mixed, wp[...].reshape(width, width), 1, 0) + offs[4:5, :]
    first = xm[...] * mk + scales[0:1, :] * branch * mk
    first_o[...] = first
    normed, _ = layer_stats(first)
    put_field(field, (normed * gains[1:2, :] + offs[1:2, :]) * mk)
    for l in range(3):
        lanes = slice(l * LANES, (l + 1) * LANES)
        w = tap_rows(taps, 0, lanes)
        tot = jnp.zeros((8, LANES), f32)
        sq = jnp.zeros((8, LANES), f32)

        def step(n, carry):
            tot, sq = carry
            c0 = n * CHUNK
            conv = conv_chunk(field[:, pl.ds(c0, CHUNK + 2), :, lanes], w, CHUNK, False)
            act, back = gelu_pair(conv)
            for m in range(TRIO):
                rows, cells8 = chunk_rows(m, c0)
                am = act[m] * mask[cells8]
                active_o[rows, lanes] = am.reshape(CHUNK * 8, LANES)
                dgelu_o[rows, lanes] = back[m].reshape(CHUNK * 8, LANES)
                tot = tot + jnp.sum(am, 0)
                sq = sq + jnp.sum(am * am, 0)
            return tot, sq

        tot, sq = lax.fori_loop(0, SIDE // CHUNK, step, (tot, sq))
        sums[0, :, lanes] += tot
        sums[1, :, lanes] += sq
    for c in image_outs(i):
        c.start()

    @pl.when(i == own - 1)
    def _():
        cells_in = 0
        for n in range(own):
            s = side_of(cls, t * own + n)
            cells_in = cells_in + s * s
        for k in range(2):
            row = rowsum(sums[k])
            for l in range(3):
                tile[3 * k + l : 3 * k + l + 1, :] = row[:, l * LANES : (l + 1) * LANES]
        tile[6:8, :] = jnp.full((2, LANES), 1.0, f32) * cells_in.astype(f32)
        send_tile(tile, slots, sends, recvs)
        loads[2].wait()

        @pl.loop(0, own)
        def _(n):
            rows = pl.ds(pl.multiple_of(n * cells, 16), cells)
            fill_mask(masks, side_of(cls, t * own + n))
            to_canvas(floss.at[rows], nat, xm)
            lc_s[rows, :] = (xm[...] * cat3(masks[...].reshape(-1, LANES))).astype(bf16)

        for n in range(4, 6):
            in_copy(n).wait_recv()
        for n in range(6):
            out_copy(n).wait_send()
        stores = [
            pltpu.make_async_copy(src, dst, lsem.at[n])
            for n, (src, dst) in enumerate(
                ((wt, wt_o), (wp, wp_o), (win, win_o), (wout, wout_o), (lc_s, lc_h))
            )
        ]
        for c in stores:
            c.start()
        stat_o[...] = sum_tiles(tile, slots, sends, recvs)
        for c in stores:
            c.wait()
        for n in range(own):
            for c in image_outs(n):
                c.wait()


def middle_kernel(
    cls, first, active, lc, st, win_h, wout_h, bin_, gains, offs, taps, scales, ei, eo,
    out_h, gsec_h, gsh_h, gin_h, gout_h, mo_h, vec_o, inb_o, stat_o, st_o,
    nat, mask, field, gfield, loc, nrm, scl, macc, gacc, l3s, gms, hs, gs, acc, inb, win, wout, out_s, gsec_s, gsh_s, gin_o, gout_o, ein, eout, osem, gsem, wsem, tile, slots, sends, recvs,
):
    i = pl.program_id(0)
    t = lax.axis_index("tensor")
    own = cls.shape[0] // 2
    held = [pltpu.make_async_copy(win_h, win, wsem.at[0]), pltpu.make_async_copy(wout_h, wout, wsem.at[1])]
    errors = [pltpu.make_async_copy(ei.at[0], ein, wsem.at[2]), pltpu.make_async_copy(eo.at[0], eout, wsem.at[3])]
    rows_n = first.shape[0]
    base = pl.multiple_of(i * rows_n, 16)
    images = [(out_s, out_h), (gsec_s, gsec_h), (gsh_s, gsh_h)]

    def image_outs(n):
        rows = pl.ds(n * rows_n if isinstance(n, int) else pl.multiple_of(n * rows_n, 16), rows_n)
        return [pltpu.make_async_copy(a.at[rows], b.at[rows], osem.at[k, n]) for k, (a, b) in enumerate(images)]

    out_o, gsec_o, gsh_o = [a.at[pl.ds(base, rows_n)] for a, _ in images]
    hidden = win.shape[0] * win.shape[2]
    half = win.shape[2]

    @pl.when(i == 0)
    def _():
        greet_all()
        for c in held + errors:
            c.start()
        clear_edges(field)
        clear_edges(gfield)
        acc[...] = jnp.zeros_like(acc)
        inb[...] = jnp.zeros_like(inb)

    fill_mask(mask, side_of(cls, t * own + i))
    mk = cat3(mask[...].reshape(-1, LANES))
    mean, rstd, _ = batch_stats(st)
    zhat = (active[...] - mean) * rstd
    put_field(field, (zhat * gains[2:3, :] + offs[2:3, :]) * mk)
    for l in range(3):
        lanes = slice(l * LANES, (l + 1) * LANES)
        w = tap_rows(taps, 9, lanes)
        bias = offs[5:6, lanes]

        def step(n, carry):
            c0 = n * CHUNK
            conv = conv_chunk(field[:, pl.ds(c0, CHUNK + 2), :, lanes], w, CHUNK, False)
            for m in range(TRIO):
                rows, cells8 = chunk_rows(m, c0)
                loc[rows, lanes] = ((conv[m] + bias) * mask[cells8]).reshape(CHUNK * 8, LANES)
            return carry

        lax.fori_loop(0, SIDE // CHUNK, step, 0)
    second = first[...] + scales[1:2, :] * loc[...]
    normed, scale = layer_stats(second)
    nrm[...] = normed
    scl[...] = jnp.broadcast_to(scale, scl.shape)
    l3 = ((normed * gains[3:4, :] + offs[3:4, :]) * mk).astype(bf16)
    l3s[pl.ds(base, rows_n), :] = l3
    gm = (lc[...].astype(f32) * scales[2:3, :]).astype(bf16)
    gms[pl.ds(base, rows_n), :] = gm
    acc[3] += colsum(gm.astype(f32))

    @pl.when(i == 0)
    def _():
        for c in held:
            c.wait()

    step = 384
    for n in range(hidden // step):
        hf, cols = n * step // half, slice(n * step % half, n * step % half + step)
        allc = slice(n * step, (n + 1) * step)
        pre = dg(l3s[pl.ds(base, rows_n), :], win[hf, :, cols], 1, 0) + jnp.concatenate(
            [bin_[3 * n + r : 3 * n + r + 1, :] for r in range(3)], -1
        )
        act, back = gelu_pair(pre)
        h = act.astype(bf16)
        hs[pl.ds(base, rows_n), allc] = h
        g = (dg(gms[pl.ds(base, rows_n), :], wout[hf, cols, :], 1, 1) * back).astype(bf16)
        gs[pl.ds(base, rows_n), allc] = g
        inb[:, allc] += colsum(g.astype(f32))
        m_part = dg(h, wout[hf, cols, :], 1, 0)
        g_part = dg(g, win[hf, :, cols], 1, 1)
        if n == 0:
            macc[...] = m_part
            gacc[...] = g_part
        else:
            macc[...] += m_part
            gacc[...] += g_part

    mlp = macc[...] + offs[6:7, :]
    second = first[...] + scales[1:2, :] * loc[...]
    from_canvas(second + scales[2:3, :] * mlp * mk, nat, out_o)
    acc[5] += colsum(lc[...].astype(f32) * mlp)
    normed, scale = nrm[...], cat3(scl[...])
    dout = gacc[...]
    acc[0] += colsum(dout)
    acc[1] += colsum(dout * normed)
    gsec = lc[...].astype(f32) + norm_back(dout, normed, scale, gains[3:4, :])
    gsec_o[...] = gsec
    acc[4] += colsum(gsec * loc[...])
    glocal = gsec * scales[1:2, :]
    acc[2] += colsum(glocal)
    put_field(gfield, glocal)
    for l in range(3):
        lanes = slice(l * LANES, (l + 1) * LANES)
        w = tap_rows(taps, 9, lanes)
        tot = jnp.zeros((8, LANES), f32)
        cross = jnp.zeros((8, LANES), f32)
        tap_sum = [jnp.zeros((8, LANES), f32) for _ in range(9)]

        def step(n, carry):
            tot, cross, tap_sum = carry[0], carry[1], list(carry[2:])
            c0 = n * CHUNK
            gwin = gfield[:, pl.ds(c0, CHUNK + 2), :, lanes]
            fwin = field[:, pl.ds(c0, CHUNK + 2), :, lanes]
            conv = conv_chunk(gwin, w, CHUNK, True)
            center = gwin[1 : 1 + TRIO, 1 : 1 + CHUNK]
            for a in range(3):
                for b in range(3):
                    prod = fwin[a : a + TRIO, b : b + CHUNK] * center
                    tap_sum[3 * a + b] += jnp.sum(prod, (0, 1))
            for m in range(TRIO):
                rows, cells8 = chunk_rows(m, c0)
                value = conv[m] * mask[cells8]
                flat = value.reshape(CHUNK * 8, LANES)
                gsh_o[rows, lanes] = flat
                z = (active[rows, lanes] - mean[:, lanes]) * rstd[:, lanes]
                tot = tot + jnp.sum(value, 0)
                cross = cross + colsum(flat * z)
            return (tot, cross, *tap_sum)

        tot, cross, *tap_sum = lax.fori_loop(0, SIDE // CHUNK, step, (tot, cross, *tap_sum))
        acc[6, :, lanes] += cross
        acc[7, :, lanes] += tot
        for k in range(9):
            acc[8 + k, :, lanes] += tap_sum[k]
    for c in image_outs(i):
        c.start()

    @pl.when(i == own - 1)
    def _():
        st_o[...] = st[...]
        cross, tot = rowsum(acc[6]), rowsum(acc[7])
        for l in range(3):
            lanes = slice(l * LANES, (l + 1) * LANES)
            tile[l : l + 1, :] = tot[:, lanes]
            tile[3 + l : 4 + l, :] = cross[:, lanes]
        tile[6:8, :] = jnp.zeros((2, LANES), f32)
        met_all()
        send_tile(tile, slots, sends, recvs)
        vec_o[...] = jnp.zeros_like(vec_o)
        for k in range(17):
            vec_o[k : k + 1, :] = rowsum(acc[k])
        inb_o[...] = jnp.zeros_like(inb_o)
        for k in range(hidden // LANES):
            inb_o[k : k + 1, :] = rowsum(inb[:, k * LANES : (k + 1) * LANES])
        l3_t = l3s[...].T
        gm_t = gms[...].T
        for c in errors:
            c.wait()
        outs = [(gin_o.at[0], gin_h.at[0]), (gin_o.at[1], gin_h.at[1]), (gout_o.at[0], gout_h.at[0]),
                (gout_o.at[1], gout_h.at[1]), (eout, mo_h)]
        outs = [pltpu.make_async_copy(src, dst, gsem.at[n]) for n, (src, dst) in enumerate(outs)]
        for hf in range(2):
            gout_o[hf] = dg(gm_t, hs[:, hf * half : (hf + 1) * half], 1, 0)
            outs[2 + hf].start()
        eout[...] += gout_o[t].T
        outs[4].start()
        for hf in range(2):
            grad = dg(l3_t, gs[:, hf * half : (hf + 1) * half], 1, 0)
            gin_o[hf] = grad + jnp.where(t == hf, ein[...], 0.0)
            outs[hf].start()
        stat_o[...] = sum_tiles(tile, slots, sends, recvs)
        for n in range(own):
            for c in image_outs(n):
                c.wait()
        for c in outs:
            c.wait()


def last_kernel(
    far,
    cls, sharp, tok_h, first, active, dgelu, gsec, gsh, low_h, q, k, v, mix_h, attn, gram, rs,
    st, gst, wt_h, wp_h, gains, offs, taps, scales,
    gin, gout, eq, ep, mo_part, bq, bp, bi, bo, vec2, inb,
    ingrad_o, mq, mp_o, mi, mo, oq_o, op_o, oi_o, oo_o, rq_o, rp_o, ri_o, ro_o, rqs_o, vec_o,
    nat, mask, scl, field, gfield, gfirst, gproj, acc, bias_acc, sharp_rows,
    mp, ai, ao, aq, ap, gt, gp, vec3, qb, obuf, tok, low, mix, wt, wp, perm, bpair, bsem, hsem, lsem, psend, precv,
    *exchange,
):
    lefts, rights, late = Spread(far, *exchange[0:11]), Spread(far, *exchange[11:22]), Spread(far, *exchange[22:33])
    left_qp = Broadcast(far, 0, *exchange[33:41])
    i = pl.program_id(0)
    t = lax.axis_index("tensor")
    own = cls.shape[0] // 2
    heads = sharp.shape[0]
    width = tok.shape[1]
    cells = tok.shape[0] // own
    head = width // heads
    other = {"tensor": 1 - t}
    part = width // 2
    cols_q = bq.shape[1]
    tiles_q = -(-cols_q // LANES)
    right_qp = Broadcast(far, tiles_q, *exchange[41:49])
    base = pl.multiple_of(i * cells, 16)
    here = pl.ds(base, cells)
    own_rows = pl.ds(pl.multiple_of(t * part, 8), part)
    loads = [
        pltpu.make_async_copy(src, dst, lsem.at[n])
        for n, (src, dst) in enumerate(
            ((gin.at[t], mi), (mo_part, mo), (eq.at[0], mq), (ep.at[0], mp_o))
        )
    ]
    held = [
        pltpu.make_async_copy(src, dst, hsem.at[n])
        for n, (src, dst) in enumerate(
            ((tok_h, tok), (wp_h, wp), (low_h, low), (mix_h, mix), (wt_h, wt))
        )
    ]
    pair_in = [remote(gin.at[1 - t], ai, psend.at[0], precv.at[0], other), remote(gout.at[1 - t], ao, psend.at[1], precv.at[1], other)]
    pair_qp = [remote(gt.at[j, 1 - t], aq.at[j], psend.at[2 + j], precv.at[2 + j], other) for j in range(3)]
    pair_qp.append(remote(gp.at[1 - t], ap, psend.at[5], precv.at[5], other))
    @pl.when(i == 0)
    def _():
        greet(far)
        for c in held + loads:
            c.start()
        fill_perm(perm, heads // 2, head)
        pieces = jnp.concatenate([x.astype(f32) for x in split3(bq[...])], 0).astype(bf16)
        turned = dg(pieces, perm[...], 1, 1)
        bpair[t] = turned[0:8] + turned[8:16] + turned[16:24]
        gt[...] = jnp.zeros_like(gt)
        gp[...] = jnp.zeros_like(gp)
        gproj[0:cells] = jnp.zeros((cells, gproj.shape[1]), bf16)
        ingrad_o[0:cells] = jnp.zeros((cells, width), bf16)
        mp[...] = jnp.zeros_like(mp)
        lefts.pay[...] = jnp.zeros_like(lefts.pay)
        rights.pay[...] = jnp.zeros_like(rights.pay)
        vec3[...] = jnp.zeros_like(vec3)
        qb[...] = jnp.zeros_like(qb)
        right_qp.x[...] = jnp.zeros_like(right_qp.x)
        sharp_rows[...] = jnp.zeros_like(sharp_rows)
        for h, (w, r) in enumerate(head_spots(heads, head)):
            sharp_rows[w, r : r + head, :] = jnp.full((head, 2 * LANES), 1.0, f32) * sharp[h]
        clear_edges(field)
        clear_edges(gfield)
        acc[...] = jnp.zeros_like(acc)
        bias_acc[...] = jnp.zeros_like(bias_acc)

    fill_mask(mask, side_of(cls, t * own + i))
    mk = cat3(mask[...].reshape(-1, LANES))
    mean, rstd, inv = batch_stats(st)
    gsum = lambda r: jnp.concatenate([gst[r : r + 1, :], gst[r + 1 : r + 2, :], gst[r + 2 : r + 3, :]], -1)
    gain_bn = gains[2:3, :]
    zhat = (active[...] - mean) * rstd
    gact = rstd * (gsh[...] * gain_bn - gsum(0) * gain_bn * inv - zhat * (gsum(3) * gain_bn * inv)) * mk
    put_field(gfield, gact * dgelu[...])
    normed, scale = layer_stats(first[...])
    gfirst[here, :] = normed
    scl[...] = jnp.broadcast_to(scale, scl.shape)
    put_field(field, (normed * gains[1:2, :] + offs[1:2, :]) * mk)
    for l in range(3):
        lanes = slice(l * LANES, (l + 1) * LANES)
        w = tap_rows(taps, 0, lanes)
        tap_sum = [jnp.zeros((8, LANES), f32) for _ in range(9)]

        def step(n, carry):
            tap_sum = list(carry)
            c0 = n * CHUNK
            gwin = gfield[:, pl.ds(c0, CHUNK + 2), :, lanes]
            fwin = field[:, pl.ds(c0, CHUNK + 2), :, lanes]
            conv = conv_chunk(gwin, w, CHUNK, True)
            center = gwin[1 : 1 + TRIO, 1 : 1 + CHUNK]
            for a in range(3):
                for b in range(3):
                    prod = fwin[a : a + TRIO, b : b + CHUNK] * center
                    tap_sum[3 * a + b] += jnp.sum(prod, (0, 1))
            for m in range(TRIO):
                rows, cells8 = chunk_rows(m, c0)
                nat[l, rows, :] = (conv[m] * mask[cells8]).reshape(CHUNK * 8, LANES)
            return tuple(tap_sum)

        tap_sum = lax.fori_loop(0, SIDE // CHUNK, step, tuple(tap_sum))
        for n in range(9):
            acc[7 + n, :, lanes] += tap_sum[n]

    @pl.when(i == 0)
    def _():
        met(far)
        for c in pair_in:
            c.start()
        remote(bpair.at[t], bpair.at[t], bsem.at[0], bsem.at[1], other).start()
        for c in held:
            c.wait()

    @pl.when(i == own - 2)
    def _():
        for c in loads:
            c.wait()
        for c in pair_in:
            c.wait()
        remote(bpair.at[t], bpair.at[t], bsem.at[0], bsem.at[1], other).wait_send()
        remote(bpair.at[1 - t], bpair.at[1 - t], bsem.at[0], bsem.at[1], other).wait_recv()
        mp[own_rows, :] = mp_o[...]
        for m, tile in enumerate(tiles(thin(bq[...], mq[...], 0)) + tiles(thin(bp[...], mp[...], 1))):
            left_qp.x[m] = tile
        mi[...] += ai[...]
        mo[...] += ao[...].T
        li = tiles(thin(bi[...], mi[...], 1))
        lo = tiles(thin(bo[...], mo[...], 1))
        n = 0
        for tile in li:
            lefts.pay[n] = tile
            n += 1
        for m, tile in enumerate(lo):
            lefts.pay[n + t * len(lo) + m] = tile
        n += 2 * len(lo)
        for tile in row_tiles(vec2) + row_tiles(inb):
            lefts.pay[n] = tile
            n += 1
        lefts.start()

    @pl.when(i == own - 1)
    def _():
        lefts.gather()

    before = pl.ds(pl.multiple_of(jnp.maximum(i - 1, 0) * cells, 16), cells)
    for j in range(3):
        gt[j] += dg(gproj[before, j * width : (j + 1) * width], low[before, :], 0, 0).reshape(2, part, width)
    gp[...] += dg(mix[before, :], ingrad_o[before, :], 0, 0).reshape(2, part, width)
    dout = jnp.concatenate([nat[0], nat[1], nat[2]], -1)
    normed, scale = gfirst[here, :], cat3(scl[...])
    acc[2] += colsum(dout * normed)
    acc[3] += colsum(dout)
    grad = gsec[...] + norm_back(dout, normed, scale, gains[1:2, :])
    gfirst[here, :] = grad
    acc[5] += colsum(grad * (first[...] - tok[here, :].astype(f32)))
    gal = (grad * scales[0:1, :]).astype(bf16)
    acc[4] += colsum(gal.astype(f32))
    ingrad_o[here, :] = gal
    gmix, gmix_lo = split2(dg(gal, wp[...], 1, 1))
    lane1 = lax.broadcasted_iota(jnp.int32, (1, width), 1)
    sharp_lane = jnp.zeros((1, width), f32)
    for h in range(heads):
        sharp_lane = jnp.where((lane1 >= h * head) & (lane1 < (h + 1) * head), sharp[h], sharp_lane)
    ones = jnp.ones((8, 2 * LANES), bf16)
    gval, gqu, gku, chan, chan_k = [], [], [], [], []
    for w in range(2):
        cols = slice(w * LANES, (w + 2) * LANES)
        gw, vw, kw, qw = gmix[:, cols], v[:, cols], k[:, cols], q[:, cols]
        a = attn[0, w]
        gattn = dg(gw, vw, 0, 0) + dg(gmix_lo[:, cols], vw, 0, 0)
        gval.append(dg(gw, a.astype(bf16), 1, 0))
        gsc = a * (gattn - jnp.sum(gattn * a, -1, keepdims=True))
        weighted = gsc * gram[0, w]
        hi, lo = split2(weighted)
        chan.append(dg(ones, hi, 1, 1) + dg(ones, lo, 1, 1))
        chan_k.append(rowsum(weighted * sharp_rows[w]))
        shi, slo = split2(gsc * sharp_rows[w])
        gqu.append(dg(kw, shi, 1, 1) + dg(kw, slo, 1, 1))
        gku.append(dg(qw, shi, 1, 0) + dg(qw, slo, 1, 0))
    chan = merge(*chan)[0:1, :]
    acc[6, 0:1, :] += chan
    gq = rs[i, 0:1, :] * (merge(*gqu) - q[...].astype(f32) * (chan * sharp_lane))
    gk = rs[i, 1:2, :] * (merge(*gku) - k[...].astype(f32) * merge(*chan_k))
    for j, piece in enumerate((gq, gk, merge(*gval))):
        small = piece.astype(bf16)
        gproj[here, j * width : (j + 1) * width] = small
        bias_acc[j] += colsum(small.astype(f32))

    @pl.when(i == own - 2)
    def _():
        lefts.middle()

    @pl.when(i == own - 1)
    def _():
        for j in range(3):
            gt[j] += dg(gproj[here, j * width : (j + 1) * width], low[here, :], 0, 0).reshape(2, part, width)
            pair_qp[j].start()
        gp[...] += dg(mix[here, :], ingrad_o[here, :], 0, 0).reshape(2, part, width)
        pair_qp[3].start()
        thirds = [bpair[hf, :, j * part : (j + 1) * part] for j in range(3) for hf in range(2)]
        left_q = thin(jnp.concatenate(thirds, -1), gt[...].reshape(6 * part, width), 0)
        for m, tile in enumerate(tiles(left_q) + tiles(thin(bp[...], gp[...].reshape(width, width), 1))):
            left_qp.x[m] += tile
        left_qp.start()
        lefts.finish()
        tiles_i = width // LANES
        tiles_o = 2 * mo.shape[0] // LANES
        get = lambda a, b: jnp.concatenate([lefts.full[m] for m in range(a, b)], -1)
        oi, oo = orthonormal([get(0, tiles_i), get(tiles_i, tiles_i + tiles_o)])
        first_vec = tiles_i + tiles_o
        count2, count3 = vec2.shape[0] * 3 // 8, vec3.shape[0] * 3 // 8
        for m in range(count2):
            vec_o[m * 8 : m * 8 + 8, :] = lefts.full[first_vec + m]
        for m in range(2):
            at = (count2 + count3 + m) * 8
            vec_o[at : at + 8, :] = lefts.full[first_vec + count2 + m]
        half_o = mo.shape[0]
        obuf[0] = oo[:, :half_o]
        obuf[1] = oo[:, half_o:]
        oo_own = obuf[t]
        ri = tiles(thin(oi, mi[...], 0))
        ro = tiles(thin(oo_own, mo[...], 0))
        for m, tile in enumerate(ri):
            rights.pay[t * len(ri) + m] = tile
        for m, tile in enumerate(ro):
            rights.pay[2 * len(ri) + m] = tile
        rights.start()

        for c in pair_qp:
            c.wait_recv()
        turned = jnp.concatenate([gt[j, t] + aq[j] for j in range(3)], 0)
        grad_q = None
        for piece in split3(turned):
            term = dg(perm[...], piece, 0, 0)
            grad_q = term if grad_q is None else grad_q + term
        mq[...] += grad_q
        mp_o[...] += gp[t] + ap[...]
        mp[own_rows, :] = mp_o[...]
        def input_dout(n):
            rows = pl.ds(pl.multiple_of(n * cells, 16), cells)
            dout = dg(gproj[rows, :], wt[...].reshape(3 * width, width), 1, 0)
            normed, scale = layer_stats(tok[rows, :].astype(f32))
            return rows, dout, normed, scale

        def input_sums(n):
            _, dout, normed, _ = input_dout(n)
            acc[0] += colsum(dout * normed)
            acc[1] += colsum(dout)

        pl.loop(0, 1)(input_sums)

        def input_out(n):
            rows, dout, normed, scale = input_dout(n)
            result = gfirst[rows, :] + norm_back(dout, normed, scale, gains[0:1, :])
            from_canvas(result, nat, ingrad_o.at[rows])

        left_qp.middle()
        rights.middle()
        pl.loop(1, own)(input_sums)
        for n in range(16):
            vec3[n : n + 1, :] = rowsum(acc[n])
        vec3[5:6, :] = rowsum(acc[5]) / scales[0:1, :]
        third = perm.shape[0] // 3
        lane8 = lax.broadcasted_iota(jnp.int32, (8, width), 1)
        total = None
        for j in range(3):
            rows = perm[j * third : (j + 1) * third, :]
            both = jnp.concatenate([rows, rows], 0)
            pieces = []
            for hf in range(2):
                mine = jnp.where((lane8 >= hf * third) & (lane8 < (hf + 1) * third), bias_acc[j], 0.0)
                pieces += [piece.astype(f32) for piece in split3(mine)]
            term = dg(jnp.concatenate(pieces, 0).astype(bf16), both, 1, 0)
            total = term if total is None else total + term
        row = jnp.concatenate([rowsum(total[0:24]), rowsum(total[24:48])], -1)
        for n in range(row.shape[1] // LANES):
            qb[n : n + 1, :] = row[:, n * LANES : (n + 1) * LANES]
        for m, tile in enumerate(row_tiles(vec3) + row_tiles(qb)):
            late.pay[m] = tile
        late.start()
        pl.loop(0, 1)(input_out)
        rights.gather()
        total = left_qp.finish()
        oq, op = orthonormal(
            [jnp.concatenate([total[m] for m in range(3)], -1), jnp.concatenate([total[m] for m in range(3, 6)], -1)]
        )
        rq = thin(oq, mq[...], 1)
        for m in range(tiles_q):
            wide = min(LANES, cols_q - m * LANES)
            right_qp.x[m, :, 0:wide] = rq[:, m * LANES : m * LANES + wide]
        for m, tile in enumerate(tiles(thin(op, mp[...], 0))):
            right_qp.x[tiles_q + m] = tile
        right_qp.start()
        share = 1.0 / (far * NEAR)
        oq_o[...] = stacked(oq)[1]
        mp[:, 0:48] = stacked(op)[0].T
        op_o[...] = mp[own_rows, 0:48]
        late.middle()
        pl.loop(1, own - 1)(input_out)
        oi_o[...] = stacked(oi)[0].T
        oo_o[...] = stacked(oo_own)[0].T
        right_qp.middle()
        late.gather()
        pl.loop(own - 1, own)(input_out)
        rights.finish()
        for m in range(len(ri)):
            ri_o[:, m * LANES : (m + 1) * LANES] = rights.full[t * len(ri) + m] * share
        for m in range(len(ro)):
            ro_o[:, m * LANES : (m + 1) * LANES] = rights.full[2 * len(ri) + m] * share
        total = right_qp.finish() * share
        for m in range(tiles_q):
            wide = min(LANES, cols_q - m * LANES)
            rq_o[:, m * LANES : m * LANES + wide] = total[m][:, 0:wide]
        for m in range(3):
            rp_o[:, m * LANES : (m + 1) * LANES] = total[tiles_q + m]
        rqs_o[...] = stacked(rq_o[...])[0].T
        late.finish()
        for m in range(count3):
            vec_o[(count2 + m) * 8 : (count2 + m) * 8 + 8, :] = late.full[m]
        for m in range(2):
            at = (count2 + count3 + 2 + m) * 8
            vec_o[at : at + 8, :] = late.full[count3 + m]
        for c in pair_qp:
            c.wait_send()
        for group in (lefts, rights, late, left_qp, right_qp):
            group.drain()


def orthonormal(rows):
    index = lax.broadcasted_iota(jnp.int32, rows[0].shape[:1] + (1,), 0)
    rank = rows[0].shape[0]
    for n in range(rank):
        done = []
        for v in rows:
            column = v[n : n + 1, :]
            dots = jnp.sum(v * column, -1, keepdims=True)
            scale = lax.rsqrt(dots[n : n + 1, :] + 1e-06)
            unit = column * scale
            later = v - (dots * scale) * unit
            done.append(jnp.where(index > n, later, jnp.where(index == n, unit, v)))
        rows = done
    return rows


class Spread:
    def __init__(self, far, pay, slots, part, tops, full, s1, r1, s2, r2, s3, r3):
        self.far, self.pay, self.slots, self.part, self.tops, self.full = far, pay, slots, part, tops, full
        self.sems = s1, r1, s2, r2, s3, r3
        self.per = slots.shape[1]
        self.hi, self.lo, self.t, self.me = place()

    def piece(self, ref, index):
        return ref.at[pl.ds(index * self.per, self.per)]

    def first(self, k, incoming):
        index, there = near_partner(self.me, self.hi, k)
        slot = index if incoming else self.me
        return remote(self.piece(self.pay, index), self.slots.at[slot], self.sems[0].at[k], self.sems[1].at[slot], there)

    def second(self, k, incoming):
        index, there = far_partner(self.hi, self.lo, self.t, k, self.far)
        slot = index if incoming else self.hi
        return remote(self.part, self.tops.at[slot], self.sems[2].at[k], self.sems[3].at[slot], there)

    def third(self, k, incoming):
        index, there = near_partner(self.me, self.hi, k)
        slot = index if incoming else self.me
        return remote(
            self.piece(self.full, self.me), self.piece(self.full, slot), self.sems[4].at[k], self.sems[5].at[slot], there
        )

    def start(self):
        for k in range(1, 2 * NEAR):
            self.first(k, False).start()
        self.slots[self.me] = self.pay[pl.ds(self.me * self.per, self.per)]

    def middle(self):
        for k in range(1, 2 * NEAR):
            self.first(k, True).wait_recv()
        total = jnp.sum(self.slots[...], 0)
        self.part[...] = total
        self.tops[self.hi] = total
        for k in range(1, self.far):
            self.second(k, False).start()

    def gather(self):
        for k in range(1, self.far):
            self.second(k, True).wait_recv()
        self.full[pl.ds(self.me * self.per, self.per)] = jnp.sum(self.tops[...], 0)
        for k in range(1, 2 * NEAR):
            self.third(k, False).start()

    def finish(self):
        for k in range(1, 2 * NEAR):
            self.third(k, True).wait_recv()

    def drain(self):
        for k in range(1, 2 * NEAR):
            self.first(k, False).wait_send()
            self.third(k, False).wait_send()
        for k in range(1, self.far):
            self.second(k, False).wait_send()


def spread_scratch(per, far):
    dma = pltpu.SemaphoreType.DMA
    near = 2 * NEAR
    vm = lambda *shape: pltpu.VMEM(shape + (8, LANES), f32)
    return [
        vm(near * per), vm(near, per), vm(per), vm(far, per), vm(near * per),
        dma((near,)), dma((near,)), dma((far,)), dma((far,)), dma((near,)), dma((near,)),
    ]


class Broadcast:
    def __init__(self, far, own, x, slots, part, tops, s1, r1, s2, r2):
        self.far, self.own, self.x, self.slots, self.part, self.tops = far, own, x, slots, part, tops
        self.sems = s1, r1, s2, r2
        self.hi, self.lo, self.t, self.me = place()

    def first(self, k, incoming):
        index, there = near_partner(self.me, self.hi, k)
        slot = index if incoming else self.me
        skip = self.own if k % 2 else 0
        count = self.x.shape[0] - skip
        return remote(
            self.x.at[pl.ds(skip, count)], self.slots.at[slot, pl.ds(skip, count)],
            self.sems[0].at[k], self.sems[1].at[slot], there,
        )

    def second(self, k, incoming):
        index, there = far_partner(self.hi, self.lo, self.t, k, self.far)
        slot = index if incoming else self.hi
        return remote(self.part, self.tops.at[slot], self.sems[2].at[k], self.sems[3].at[slot], there)

    def start(self):
        for k in range(1, 2 * NEAR):
            self.first(k, False).start()
        self.slots[self.me] = self.x[...]

    def middle(self):
        for k in range(1, 2 * NEAR):
            self.first(k, True).wait_recv()
        own = self.own
        if own:
            total = self.slots[self.t, 0:own]
            for k in range(1, NEAR):
                total = total + self.slots[2 * k + self.t, 0:own]
            self.part[0:own] = total
        self.part[own:] = jnp.sum(self.slots[:, own:], 0)
        self.tops[self.hi] = self.part[...]
        for k in range(1, self.far):
            self.second(k, False).start()

    def finish(self):
        for k in range(1, self.far):
            self.second(k, True).wait_recv()
        return jnp.sum(self.tops[...], 0)

    def drain(self):
        for k in range(1, 2 * NEAR):
            self.first(k, False).wait_send()
        for k in range(1, self.far):
            self.second(k, False).wait_send()


def broadcast_scratch(count, far):
    dma = pltpu.SemaphoreType.DMA
    near = 2 * NEAR
    vm = lambda *shape: pltpu.VMEM(shape + (8, LANES), f32)
    return [vm(count), vm(near, count), vm(count), vm(far, count), dma((near,)), dma((near,)), dma((far,)), dma((far,))]


def row_tiles(ref):
    return [
        ref[r * 8 : r * 8 + 8, c * LANES : (c + 1) * LANES]
        for c in range(ref.shape[1] // LANES)
        for r in range(ref.shape[0] // 8)
    ]


def tiles(x):
    return [x[:, n * LANES : (n + 1) * LANES] for n in range(x.shape[1] // LANES)]


def stacked(x):
    hi, mid, lo = split3(x)
    hi, mid, lo = hi.astype(f32), mid.astype(f32), lo.astype(f32)
    left = jnp.concatenate([hi, hi, mid, hi, mid, lo], 0)
    right = jnp.concatenate([hi, mid, hi, lo, mid, hi], 0)
    return left, right


def update_kernel(
    oq, op, oi, oo, rqs, rp, ri, ro, rq, mq, mp, mi, mo, wq, wp, wi, wo, vq, vp, vi, vo,
    vec, one, two, gains, offs, taps, scales, bq, sharp, bi, gains_v, offs_v, taps_v, scales_v, bq_v, sharp_v, bi_v,
    wq_o, wp_o, wi_o, wo_o, vq_o, vp_o, vi_o, vo_o, eq_o, ep_o, ei_o, eo_o,
    gains_o, offs_o, taps_o, scales_o, bq_o, sharp_o, bi_o,
    gains_m, offs_m, taps_m, scales_m, bq_m, sharp_m, bi_m, tq_o, tp_o, ti_o, to_o, one_o, two_o,
    *, share,
):
    at = pl.program_id(0)
    one_o[...] = one[...]
    two_o[...] = two[pl.ds(pl.multiple_of(at * one.shape[0], 16), one.shape[0]), :]
    groups = (
        (oq, None, mq, wq, vq, wq_o, vq_o, eq_o),
        (op, rp, mp, wp, vp, wp_o, vp_o, ep_o),
        (oi, ri, mi, wi, vi, wi_o, vi_o, ei_o),
        (oo, ro, mo, wo, vo, wo_o, vo_o, eo_o),
    )
    steps = pl.num_programs(0)

    def own_part(ref):
        size = ref.shape[0] // steps
        return ref[pl.ds(pl.multiple_of(at * size, 8), size), :]

    for o, r, m, w, v, w_o, v_o, e_o in groups:
        if r is None:
            approx = dg(own_part(rqs).astype(bf16), o[...].astype(bf16), 1, 0)
        else:
            approx = dg(own_part(o).astype(bf16), stacked(r[...])[1].astype(bf16), 1, 0)
        moment = momentum_decay * v[...] + approx
        v_o[...] = moment
        w_o[...] = w[...] - learn_rate * moment
        size = w.shape[0]
        e_o[0] = m[pl.ds(pl.multiple_of(at * size, 8), size), :] - approx

    @pl.when(pl.program_id(0) == 0)
    def _():
        for r, t_o in ((rq, tq_o), (rp, tp_o), (ri, ti_o), (ro, to_o)):
            t_o[...] = r[...]

        def step(grad, value, moment, v_out, m_out, rows):
            new = momentum_decay * moment[rows, :] + grad * share
            m_out[rows, :] = new
            v_out[rows, :] = value[rows, :] - learn_rate * new

        def row2(a, b):
            return jnp.concatenate([vec[24 * c + a : 24 * c + b, :] for c in range(3)], -1)

        def row3(a, b):
            return jnp.concatenate([vec[72 + 16 * c + a : 72 + 16 * c + b, :] for c in range(3)], -1)

        def each(grads, value, moment, v_out, m_out):
            for n, g in enumerate(grads):
                step(g, value, moment, v_out, m_out, slice(n, n + 1))

        each([row3(0, 1), row3(2, 3), row2(6, 7), row2(1, 2)], gains, gains_v, gains_o, gains_m)
        each(
            [row3(1, 2), row3(3, 4), row2(7, 8), row2(0, 1), row3(4, 5), row2(2, 3), row2(3, 4)],
            offs, offs_v, offs_o, offs_m,
        )
        each([row3(5, 6), row2(4, 5), row2(5, 6)], scales, scales_v, scales_o, scales_m)
        each([row3(7 + n, 8 + n) for n in range(9)] + [row2(8 + n, 9 + n) for n in range(9)],
             taps, taps_v, taps_o, taps_m)
        base = 72 + 48
        half = bi.shape[0]
        step(vec[base : base + half, :], bi, bi_v, bi_o, bi_m, slice(None))
        base += 16
        step(vec[base : base + bq.shape[0], :], bq, bq_v, bq_o, bq_m, slice(None))
        width = gains.shape[1]
        heads = sharp.shape[1]
        head = width // heads
        chan = lax.broadcasted_iota(jnp.int32, (width, heads), 0)
        lane = lax.broadcasted_iota(jnp.int32, (width, heads), 1)
        pick = jnp.where((chan >= lane * head) & (chan < (lane + 1) * head), 1.0, 0.0).astype(f32)
        grad = thin(jnp.broadcast_to(row3(6, 7), (8, width)), pick, 0)
        step(grad[0:1, :], sharp, sharp_v, sharp_o, sharp_m, slice(None))


def body(
    tokens, classes, loss,
    tri, tri_b, sharp, mapw, expw, exp_b, conw, gains, offs, taps, scales,
    tri_v, map_v, exp_v, con_v, tri_b_v, sharp_v, exp_b_v, gains_v, offs_v, taps_v, scales_v,
    tri_e, map_e, exp_e, con_e, tri_f, map_f, exp_f, con_f,
):
    import functools

    far = lax.axis_size("dp") // NEAR
    rows, width = tokens.shape
    own = classes.shape[0] // 2
    cells = rows // own
    heads = sharp.shape[0]
    head = width // heads
    part = width // 2
    cols = tri.shape[1]
    half = expw.shape[1]
    hidden = 2 * half
    vm = pl.BlockSpec(memory_space=pltpu.VMEM)
    sm = pl.BlockSpec(memory_space=pltpu.SMEM)
    anyspace = pl.BlockSpec(memory_space=pl.ANY)

    def whole(*shape):
        return pl.BlockSpec(shape, lambda i: (0,) * len(shape), pipeline_mode=pl.Buffered(1))

    image = pl.BlockSpec((cells, width), lambda i: (i, 0))
    square = pl.BlockSpec((1, 2, 2 * LANES, 2 * LANES), lambda i: (i, 0, 0, 0))
    eight = pl.BlockSpec((1, 8, width), lambda i: (i, 0, 0))
    smem = pl.BlockSpec(memory_space=pltpu.SMEM)
    vecs = [whole(4, width), whole(7, width), whole(18, width), whole(3, width)]
    field = pltpu.VMEM((TRIO + 2, SIDE + 2, GROUPS, width), f32)
    nat = pltpu.VMEM((3, cells, LANES), f32)
    mask = pltpu.VMEM((TRIO * SIDE, GROUPS, LANES), f32)
    canvas = pltpu.VMEM((cells, width), f32)

    dma = pltpu.SemaphoreType.DMA
    devices = lax.axis_size("dp") * 2
    two_windows = pltpu.VMEM((2, 2 * LANES, 2 * LANES), f32)
    tile_exchange = [
        pltpu.VMEM((8, LANES), f32), pltpu.VMEM((devices, 8, LANES), f32),
    ]
    first, active, dgelu, low, q, k, v, mix, xc, attn, gram, rs, stat, lc, wt, wp, win, wout = pl.pallas_call(
        first_kernel,
        grid=(own,),
        out_shape=[sds((rows, width))] * 3
        + [sds((rows, width), bf16)] * 6
        + [sds((own, 2, 2 * LANES, 2 * LANES))] * 2
        + [held((own, 8, width)), held((8, LANES)), sds((rows, width), bf16)]
        + [sds((3, 2, part, width), bf16), sds((2, part, width), bf16),
           sds((2, width, half), bf16), sds((2, half, width), bf16)],
        in_specs=[smem, smem, image, whole(cols, width), whole(part, width), whole(2 * cols // LANES, LANES)]
        + vecs + [anyspace] * 3,
        out_specs=[anyspace] * 11 + [vm] * 2 + [anyspace] * 5,
        scratch_shapes=[
            nat, mask, canvas, field, two_windows, two_windows, pltpu.VMEM((2, 8, width), f32),
            pltpu.VMEM((3, 2, part, width), bf16), pltpu.VMEM((2, part, width), bf16),
            pltpu.VMEM((2, width, half), bf16), pltpu.VMEM((2, half, width), bf16),
            pltpu.VMEM((width, half), f32), pltpu.VMEM((half, width), f32), pltpu.VMEM((rows, width), bf16), mask,
            pltpu.VMEM((cols, cols), bf16), pltpu.VMEM((8, width), f32),
        ] + [pltpu.VMEM((rows, width), f32)] * 3 + [pltpu.VMEM((rows, width), bf16)] * 6
        + [pltpu.VMEM((own, 2, 2 * LANES, 2 * LANES), f32)] * 2 + [pltpu.VMEM((rows, width), bf16)]
        + tile_exchange + [dma((11, own)), dma((5,)), dma((6,)), dma((6,)), dma((devices,)), dma((devices,))],
        compiler_params=params(61, collective_id=0, has_side_effects=True),
        name="first_part",
    )(classes, sharp, tokens, tri.T, mapw, tri_b.reshape(-1, LANES), gains, offs, taps, scales, expw, conw, loss)
    wt = wt.reshape(3, width, width)
    wp = wp.reshape(width, width)

    block_out, gsec, gsh, gin, gout, mo_part, vec2, inb, gstat, stat = pl.pallas_call(
        middle_kernel,
        grid=(own,),
        out_shape=[
            sds((rows, width), bf16), sds((rows, width)), sds((rows, width)),
            sds((2, width, half)), sds((2, width, half)), sds((half, width)), held((24, width)), held((16, LANES)), held((8, LANES)), held((8, LANES)),
        ],
        in_specs=[smem, image, image, image, vm, anyspace, anyspace,
                  whole(hidden // LANES, LANES)] + vecs + [anyspace] * 2,
        out_specs=[anyspace] * 6 + [vm] * 4,
        scratch_shapes=[
            nat, mask, field, field, canvas, canvas, pltpu.VMEM((cells, LANES), f32), canvas, canvas,
            pltpu.VMEM((rows, width), bf16), pltpu.VMEM((rows, width), bf16),
            pltpu.VMEM((rows, hidden), bf16), pltpu.VMEM((rows, hidden), bf16),
            pltpu.VMEM((17, 8, width), f32), pltpu.VMEM((8, hidden), f32),
            pltpu.VMEM((2, width, half), bf16), pltpu.VMEM((2, half, width), bf16),
            pltpu.VMEM((rows, width), bf16), pltpu.VMEM((rows, width), f32), pltpu.VMEM((rows, width), f32),
            pltpu.VMEM((2, width, half), f32), pltpu.VMEM((2, width, half), f32),
            pltpu.VMEM((width, half), f32), pltpu.VMEM((half, width), f32),
            dma((3, own)), dma((5,)), dma((4,)),
        ] + tile_exchange + [dma((devices,)), dma((devices,))],
        compiler_params=params(56, collective_id=1, has_side_effects=True),
        name="middle_part",
    )(classes, first, active, lc, stat, win, wout, exp_b.reshape(hidden // LANES, LANES), gains, offs, taps, scales,
      exp_e, con_e)
    input_grad, mq, mp, mi, mo, oq, op, oi, oo, rq, rp, ri, ro, rqs, vec = pl.pallas_call(
        functools.partial(last_kernel, far),
        grid=(own,),
        out_shape=[
            held((rows, width), bf16),
            held((cols, width)), held((part, width)), held((width, half)), held((half, width)),
            held((48, width)), held((part, 48)), held((width, 48)), held((half, 48)),
            held((8, cols)), held((8, width)), held((8, half)), held((8, width)), held((cols, 48)), held((152, LANES)),
        ],
        in_specs=[smem, smem, anyspace] + [image] * 5 + [anyspace] + [image] * 3
        + [anyspace] + [square, square, vm, vm, vm] + [anyspace] * 2 + vecs
        + [anyspace] * 5 + [whole(8, cols), whole(8, width), whole(8, half), whole(8, width), vm, vm],
        out_specs=[vm] * 15,
        scratch_shapes=[
            nat, mask, pltpu.VMEM((cells, LANES), f32), field, field, pltpu.VMEM((rows, width), f32),
            pltpu.VMEM((rows, 3 * width), bf16),
            pltpu.VMEM((16, 8, width), f32), pltpu.VMEM((3, 8, width), f32), two_windows,
            pltpu.VMEM((width, width), f32),
            pltpu.VMEM((width, half), f32), pltpu.VMEM((width, half), f32),
            pltpu.VMEM((3, part, width), f32), pltpu.VMEM((part, width), f32),
            pltpu.VMEM((3, 2, part, width), f32), pltpu.VMEM((2, part, width), f32),
            pltpu.VMEM((16, width), f32), pltpu.VMEM((16, LANES), f32),
            pltpu.VMEM((2, 8, half), f32),
            pltpu.VMEM((rows, width), bf16), pltpu.VMEM((rows, width), bf16), pltpu.VMEM((rows, width), bf16),
            pltpu.VMEM((3, width, width), bf16), pltpu.VMEM((width, width), bf16), pltpu.VMEM((cols, cols), bf16), pltpu.VMEM((2, 8, cols), f32), dma((2,)),
            dma((6,)), dma((6,)), dma((6,)), dma((6,)),
        ]
        + spread_scratch(4, far) + spread_scratch(2, far) + spread_scratch(1, far)
        + broadcast_scratch(6, far) + broadcast_scratch(-(-cols // LANES) + 3, far),
        compiler_params=params(47 + far // 8, collective_id=2, has_side_effects=True),
        name="last_part",
    )(classes, sharp, xc, first, active, dgelu, gsec, gsh, low, q, k, v, mix, attn, gram, rs, stat, gstat,
      wt, wp, gains, offs, taps, scales, gin, gout, tri_e.swapaxes(1, 2), map_e, mo_part,
      tri_f.T, map_f.T, exp_f.T, con_f.T, vec2, inb)

    steps = 2

    def cut(n, m):
        return pl.BlockSpec((n // steps, m), lambda i: (i, 0))

    def cut3(n, m):
        return pl.BlockSpec((1, n // steps, m), lambda i: (0, i, 0))

    wide = lambda x: x.reshape(-1, LANES)
    mats = [cut(cols, width), cut(part, width), cut(width, half), cut(half, width)]
    small_specs = vecs + [whole(2 * cols // LANES, LANES), whole(1, heads), whole(hidden // LANES, LANES)]
    basis_specs = [whole(8, cols), whole(8, width), whole(8, half), whole(8, width)]
    basis_shapes = [sds((8, cols)), sds((8, width)), sds((8, half)), sds((8, width))]
    small_shapes = [sds((4, width)), sds((7, width)), sds((18, width)), sds((3, width)), sds((2 * cols // LANES, LANES)), sds((1, heads)), sds((hidden // LANES, LANES))]
    mat_shapes = [sds((cols, width)), sds((part, width)), sds((width, half)), sds((half, width))]
    res = pl.pallas_call(
        functools.partial(update_kernel, share=1.0 / (far * NEAR)),
        grid=(steps,),
        out_shape=mat_shapes * 2
        + [sds((1, cols, width)), sds((1, part, width)), sds((1, width, half)), sds((1, half, width))]
        + small_shapes * 2 + basis_shapes + [sds((rows, width), bf16)] * 2,
        in_specs=[vm] * 13 + mats * 2 + [vm, cut(rows, width), vm] + small_specs * 2,
        out_specs=mats * 2
        + [cut3(cols, width), cut3(part, width), cut3(width, half), cut3(half, width)]
        + small_specs * 2 + basis_specs + [cut(rows, width)] * 2,
        compiler_params=params(30),
        name="update",
    )(oq, op, oi, oo, rqs, rp, ri, ro, rq, mq, mp, mi, mo, tri.T, mapw, expw, conw, tri_v.T, map_v, exp_v, con_v,
      vec, block_out, input_grad, gains, offs, taps, scales, wide(tri_b), sharp.reshape(1, heads), wide(exp_b),
      gains_v, offs_v, taps_v, scales_v, wide(tri_b_v), sharp_v.reshape(1, heads), wide(exp_b_v))
    nw, nv, ne, sv, smo, nt = res[0:4], res[4:8], res[8:12], res[12:19], res[19:26], res[26:30]
    block_out, input_grad = res[30:32]
    nw, nv = [nw[0].T, *nw[1:]], [nv[0].T, *nv[1:]]
    ne = [ne[0].swapaxes(1, 2), *ne[1:]]
    nt = [x.T for x in nt]

    def small(x):
        g, o, t_, s, b, sh, bi_ = x
        return (b.reshape(-1), sh.reshape(-1), bi_.reshape(-1), g, o, t_, s)

    return (
        (block_out, input_grad) + tuple(nw) + small(sv) + tuple(nv) + small(smo) + tuple(ne) + tuple(nt)
    )


def solution(mesh):
    rows = P(("dp", "tensor"), None)
    col, row = P(None, "tensor"), P("tensor", None)
    rep = P()
    err = (P("dp", None, "tensor"), P("dp", "tensor", None), P("dp", None, "tensor"), P("dp", "tensor", None))
    mats = (col, row, col, row)
    in_specs = (
        (rows, P("dp"), rows, col, rep, rep, row, col, rep, row, rep, rep, rep, rep)
        + mats + (rep,) * 7 + err + (row, rep, row, rep)
    )
    out_specs = (rows, rows) + mats + (rep,) * 7 + mats + (rep,) * 7 + err + (row, rep, row, rep)
    return jax.shard_map(body, mesh=mesh, in_specs=in_specs, out_specs=out_specs, check_vma=False)
```

```python
import jax
import jax.numpy as jnp
from jax import lax
from jax.experimental import pallas as pl
from jax.experimental.pallas import tpu as pltpu
from jax.sharding import PartitionSpec as P

SIDE = 24
GROUPS = 8
TRIO = 3
LANES = 128
NEAR = 4
learn_rate = 0.02
momentum_decay = 0.9
f32 = jnp.float32
bf16 = jnp.bfloat16
MESH = pl.DeviceIdType.MESH
HALF_ROOT = 0.7071067811865476
GAUSS = 0.3989422804014327


def sds(shape, dtype=f32):
    return jax.ShapeDtypeStruct(shape, dtype)


def params(mib, **kw):
    return pltpu.CompilerParams(vmem_limit_bytes=mib << 20, **kw)


def held(shape, dtype=f32):
    return pltpu.VMEM(shape, dtype)


def dg(a, b, ca, cb):
    return lax.dot_general(
        a, b, (((ca,), (cb,)), ((), ())), preferred_element_type=f32
    )


def thin(a, m, cb):
    pieces = jnp.concatenate([x.astype(f32) for x in split3(a)], 0).astype(bf16)
    hi, lo = split2(m)
    total = dg(pieces, hi, 1, cb) + dg(pieces, lo, 1, cb)
    rows = a.shape[0]
    return total[0:rows] + total[rows : 2 * rows] + total[2 * rows :]


def cat3(m):
    return jnp.concatenate([m, m, m], -1)


def split2(x):
    hi = x.astype(bf16)
    return hi, (x - hi.astype(f32)).astype(bf16)


def split3(x):
    hi = x.astype(bf16)
    rest = x - hi.astype(f32)
    mid = rest.astype(bf16)
    return hi, mid, (rest - mid.astype(f32)).astype(bf16)


def dg2(a, b, ca, cb):
    hi, lo = split2(a)
    return dg(hi, b, ca, cb) + dg(lo, b, ca, cb)


def mean_of(x):
    return jnp.sum(x, -1, keepdims=True) * (1.0 / x.shape[-1])


def layer_stats(x):
    center = x - mean_of(x)
    scale = lax.rsqrt(mean_of(center * center) + 1e-06)
    return center * scale, scale


def norm_back(grad_out, normed, scale, gain):
    grad_normed = grad_out * gain
    return scale * (
        grad_normed - mean_of(grad_normed) - normed * mean_of(grad_normed * normed)
    )


def colsum(x):
    return jnp.sum(x.reshape(x.shape[0] // 8, 8, x.shape[1]), 0)


def rowsum(x):
    return jnp.sum(x, 0, keepdims=True)


def gelu_pair(x):
    phi = 0.5 + 0.5 * lax.erf(x * HALF_ROOT)
    return x * phi, phi + x * jnp.exp(-0.5 * x * x) * GAUSS


def side_of(cls_ref, index):
    bucket = cls_ref[index]
    return SIDE * (7 + 2 * bucket + lax.div(bucket, 2)) // 12


def fill_mask(mask, side):
    shape = (SIDE, GROUPS, LANES)
    col = lax.broadcasted_iota(jnp.int32, shape, 0)
    group = lax.broadcasted_iota(jnp.int32, shape, 1)
    for m in range(TRIO):
        inside = (group * TRIO + m < side) & (col < side)
        mask[pl.ds(m * SIDE, SIDE)] = jnp.where(inside, 1.0, 0.0).astype(f32)


def to_canvas(src, nat, dst):
    per = TRIO * SIDE
    for l in range(3):
        nat[l] = src[:, l * LANES : (l + 1) * LANES].astype(f32)
    for j in range(per):
        for l in range(3):
            dst[pl.ds(j * 8, 8), l * LANES : (l + 1) * LANES] = nat[
                l, pl.ds(j, GROUPS, stride=per), :
            ]


def from_canvas(value, nat, dst):
    per = TRIO * SIDE
    for j in range(per):
        for l in range(3):
            nat[l, pl.ds(j, GROUPS, stride=per), :] = value[
                j * 8 : j * 8 + 8, l * LANES : (l + 1) * LANES
            ]
    for l in range(3):
        dst[:, l * LANES : (l + 1) * LANES] = nat[l].astype(bf16)


def clear_edges(field):
    zero = jnp.zeros((TRIO + 2, 1, GROUPS, field.shape[-1]), f32)
    field[:, 0:1] = zero
    field[:, SIDE + 1 : SIDE + 2] = zero


def put_field(field, value):
    v = value.reshape(TRIO, SIDE, GROUPS, value.shape[-1])
    group = lax.broadcasted_iota(jnp.int32, (SIDE, GROUPS, value.shape[-1]), 1)
    field[1 : TRIO + 1, 1 : SIDE + 1] = v
    field[0, 1 : SIDE + 1] = jnp.where(group == 0, 0.0, pltpu.roll(v[TRIO - 1], 1, 1))
    field[TRIO + 1, 1 : SIDE + 1] = jnp.where(
        group == GROUPS - 1, 0.0, pltpu.roll(v[0], GROUPS - 1, 1)
    )


def conv_chunk(win, weights, width, flip):
    total = None
    for a in range(3):
        for b in range(3):
            ra, rb = (2 - a, 2 - b) if flip else (a, b)
            term = weights[3 * a + b] * win[ra : ra + TRIO, rb : rb + width]
            total = term if total is None else total + term
    return total


def tap_rows(taps, first, lanes):
    return [
        jnp.broadcast_to(taps[first + k : first + k + 1, lanes], (GROUPS, LANES)) for k in range(9)
    ]


CHUNK = 6


def chunk_rows(m, c0):
    return pl.ds(pl.multiple_of((m * SIDE + c0) * 8, 16), CHUNK * 8), pl.ds(m * SIDE + c0, CHUNK)


def near_partner(me, hi, k):
    index = lax.rem(me + k, 2 * NEAR)
    return index, {"dp": hi * NEAR + lax.div(index, 2), "tensor": lax.rem(index, 2)}


def place():
    dp = lax.axis_index("dp")
    t = lax.axis_index("tensor")
    hi = lax.div(dp, NEAR)
    lo = lax.rem(dp, NEAR)
    return hi, lo, t, lo * 2 + t


def greet(far):
    hi, lo, t, me = place()
    barrier = pltpu.get_barrier_semaphore()
    for k in range(1, 2 * NEAR):
        pl.semaphore_signal(
            barrier, inc=1, device_id=near_partner(me, hi, k)[1], device_id_type=MESH
        )
    for k in range(1, far):
        there = {"dp": lax.rem(hi + k, far) * NEAR + lo, "tensor": t}
        pl.semaphore_signal(barrier, inc=1, device_id=there, device_id_type=MESH)


def met(far):
    pl.semaphore_wait(pltpu.get_barrier_semaphore(), 2 * NEAR - 1 + far - 1)


def remote(src, dst, send, recv, there):
    return pltpu.make_async_remote_copy(
        src_ref=src, dst_ref=dst, send_sem=send, recv_sem=recv, device_id=there, device_id_type=MESH
    )


def far_partner(hi, lo, t, k, far):
    index = lax.rem(hi + k, far)
    return index, {"dp": index * NEAR + lo, "tensor": t}


def all_partners():
    n = lax.axis_size("dp") * 2
    me = lax.axis_index("dp") * 2 + lax.axis_index("tensor")
    out = []
    for k in range(1, n):
        index = lax.rem(me + k, n)
        out.append((index, {"dp": lax.div(index, 2), "tensor": lax.rem(index, 2)}))
    return me, out


def greet_all():
    barrier = pltpu.get_barrier_semaphore()
    for _, there in all_partners()[1]:
        pl.semaphore_signal(barrier, inc=1, device_id=there, device_id_type=MESH)


def met_all():
    pl.semaphore_wait(pltpu.get_barrier_semaphore(), lax.axis_size("dp") * 2 - 1)


def send_tile(tile, slots, sends, recvs):
    me, partners = all_partners()
    for k, (_, there) in enumerate(partners):
        remote(tile, slots.at[me], sends.at[k], recvs.at[me], there).start()
    slots[me] = tile[...]


def sum_tiles(tile, slots, sends, recvs):
    me, partners = all_partners()
    for k, (index, there) in enumerate(partners):
        remote(tile, slots.at[index], sends.at[k], recvs.at[index], there).wait_recv()
    total = jnp.sum(slots[...], 0)
    for k, (index, there) in enumerate(partners):
        remote(tile, slots.at[index], sends.at[k], recvs.at[index], there).wait_send()
    return total


def fill_perm(perm, heads, head):
    shape = (head, perm.shape[1])
    row = lax.broadcasted_iota(jnp.int32, shape, 0)
    lane = lax.broadcasted_iota(jnp.int32, shape, 1)
    for j in range(3):
        for h in range(heads):
            at = (j * heads + h) * head
            perm[at : at + head, :] = jnp.where(lane == row + (3 * h + j) * head, 1.0, 0.0).astype(bf16)


def windows(x):
    return x[:, 0 : 2 * LANES], x[:, LANES : 3 * LANES]


def merge(a, b):
    return jnp.concatenate([a[:, :LANES], a[:, LANES:] + b[:, :LANES], b[:, LANES:]], -1)


def head_spots(heads, head):
    return [(2 * h // heads, h * head - LANES * (2 * h // heads)) for h in range(heads)]


def batch_stats(st):
    row = lambda r: jnp.concatenate([st[r : r + 1, :], st[r + 1 : r + 2, :], st[r + 2 : r + 3, :]], -1)
    inv = cat3(1.0 / st[6:7, :])
    mean = row(0) * inv
    var = row(3) * inv - mean * mean
    return mean, lax.rsqrt(var + 1e-05), inv


def first_kernel(
    cls, sharp, tok_h, tri, mapw, tri_b, gains, offs, taps, scales, expw, conw, loss,
    first_h, active_h, dgelu_h, low_h, q_h, k_h, v_h, mix_h, xc_h, attn_h, gram_h, rs_o, stat_o, lc_h,
    wt_o, wp_o, win_o, wout_o,
    nat, mask, xm, field, sharp_rows, in_block, sums, wt, wp, win, wout, fexp, fcon, floss, tok, masks, perm, bq,
    first_s, active_s, dgelu_s, low_s, q_s, k_s, v_s, mix_s, xc_s, attn_s, gram_s, lc_s, tile, slots,
    osem, lsem, wsend, wrecv, sends, recvs,
):
    i = pl.program_id(0)
    t = lax.axis_index("tensor")
    own = cls.shape[0] // 2
    heads = sharp.shape[0]
    width = tok.shape[1]
    cells = tok.shape[0] // own
    head = width // heads
    other = {"tensor": 1 - t}
    spots = [wt.at[0], wt.at[1], wt.at[2], wp, win, wout]

    def out_copy(n):
        ref = spots[n]
        return remote(ref.at[t], ref.at[t], wsend.at[n], wrecv.at[n], other)

    def in_copy(n):
        ref = spots[n]
        return remote(ref.at[1 - t], ref.at[1 - t], wsend.at[n], wrecv.at[n], other)

    here = pl.ds(pl.multiple_of(i * cells, 16), cells)
    images = [(first_s, first_h), (active_s, active_h), (dgelu_s, dgelu_h), (low_s, low_h), (q_s, q_h), (k_s, k_h),
              (v_s, v_h), (mix_s, mix_h), (xc_s, xc_h)]
    squares = [(attn_s, attn_h), (gram_s, gram_h)]

    def image_outs(n):
        rows = pl.ds(n * cells if isinstance(n, int) else pl.multiple_of(n * cells, 16), cells)
        copies = [pltpu.make_async_copy(a.at[rows], b.at[rows], osem.at[k, n]) for k, (a, b) in enumerate(images)]
        return copies + [
            pltpu.make_async_copy(a.at[n], b.at[n], osem.at[len(images) + k, n]) for k, (a, b) in enumerate(squares)
        ]

    first_o, active_o, dgelu_o, low_o, q_o, k_o, v_o, mix_o, xc_o = [a.at[here] for a, _ in images]
    loads = [
        pltpu.make_async_copy(expw, fexp, lsem.at[0]),
        pltpu.make_async_copy(conw, fcon, lsem.at[1]),
        pltpu.make_async_copy(loss, floss, lsem.at[2]),
        pltpu.make_async_copy(tok_h, tok, lsem.at[3]),
    ]

    @pl.when(i == 0)
    def _():
        loads[3].start()
        greet_all()
        for c in loads[:3]:
            c.start()
        fill_perm(perm, heads // 2, head)
        turned = dg(perm[...], tri[...].astype(bf16), 1, 0).astype(bf16)
        part = turned.shape[0] // 3
        bias = jnp.concatenate([tri_b[n : n + 1, :] for n in range(tri_b.shape[0])], -1)
        pieces = jnp.concatenate([x.astype(f32) for x in split3(jnp.broadcast_to(bias, (8, bias.shape[1])))], 0)
        pieces = pieces.astype(bf16)
        sides = []
        for hf in range(2):
            turned_b = dg(pieces[:, hf * 3 * part : (hf + 1) * 3 * part], perm[...], 1, 1)
            sides.append(turned_b[0:1] + turned_b[8:9] + turned_b[16:17])
        for j in range(3):
            bq[j : j + 1, :] = jnp.concatenate([side[:, j * part : (j + 1) * part] for side in sides], -1)
        for j in range(3):
            wt[j, t] = turned[j * part : (j + 1) * part]
        wp[t] = mapw[...].astype(bf16)
        lane = lax.broadcasted_iota(jnp.int32, (head, 2 * LANES), 1)
        sharp_rows[...] = jnp.zeros_like(sharp_rows)
        in_block[...] = jnp.zeros_like(in_block)
        for h, (w, r) in enumerate(head_spots(heads, head)):
            inside = (lane >= r) & (lane < r + head)
            sharp_rows[w, r : r + head, :] = jnp.where(inside, sharp[h], 0.0)
            in_block[w, r : r + head, :] = jnp.where(inside, 1.0, 0.0)
        clear_edges(field)
        sums[...] = jnp.zeros_like(sums)
        loads[0].wait()
        loads[1].wait()
        win[t] = fexp[...].astype(bf16)
        wout[t] = fcon[...].astype(bf16)

    fill_mask(mask, side_of(cls, t * own + i))
    mk = cat3(mask[...].reshape(-1, LANES))

    @pl.when(i == 0)
    def _():
        loads[3].wait()

        @pl.loop(0, own)
        def _(n):
            rows = pl.ds(pl.multiple_of(n * cells, 16), cells)
            fill_mask(masks, side_of(cls, t * own + n))
            inside = cat3(masks[...].reshape(-1, LANES))
            to_canvas(tok.at[rows], nat, xm)
            x = xm[...] * inside
            xc_s[rows, :] = x.astype(bf16)
            normed, _ = layer_stats(x)
            low_s[rows, :] = ((normed * gains[0:1, :] + offs[0:1, :]) * inside).astype(bf16)

        met_all()
        for n in range(4):
            out_copy(n).start()
        for n in range(4):
            in_copy(n).wait_recv()
        for n in range(4, 6):
            out_copy(n).start()

    low = low_o[...]
    lows = []
    projected = dg(low, wt[...].reshape(3 * width, width), 1, 1)
    for j in range(2):
        value = (projected[:, j * width : (j + 1) * width] + bq[j : j + 1, :]) * mk
        scale = lax.rsqrt(rowsum(value * value) + 1e-06)
        rs_o[0, j : j + 1, :] = scale
        unit = (value * scale).astype(bf16)
        (q_o, k_o)[j][...] = unit
        lows.append(windows(unit))
    value_low = ((projected[:, 2 * width :] + bq[2:3, :]) * mk).astype(bf16)
    v_o[...] = value_low
    grams = [dg(lows[0][w], lows[1][w], 0, 0) for w in range(2)]
    gram = jnp.stack(grams)
    gram_s[i] = gram
    inside = in_block[...]
    logits = jnp.where(inside > 0.0, gram * sharp_rows[...], -1e30)
    powers = jnp.exp(logits - jnp.max(logits, -1, keepdims=True)) * inside
    attn = powers / jnp.maximum(jnp.sum(powers, -1, keepdims=True), 0.5)
    attn_s[i] = attn
    parts = [dg(windows(value_low)[w], attn[w].astype(bf16), 1, 1) for w in range(2)]
    mixed = merge(*parts).astype(bf16)
    mix_o[...] = mixed
    branch = dg(mixed, wp[...].reshape(width, width), 1, 0) + offs[4:5, :]
    first = xc_o[...].astype(f32) + scales[0:1, :] * branch * mk
    first_o[...] = first
    normed, _ = layer_stats(first)
    put_field(field, (normed * gains[1:2, :] + offs[1:2, :]) * mk)
    for l in range(3):
        lanes = slice(l * LANES, (l + 1) * LANES)
        w = tap_rows(taps, 0, lanes)
        tot = jnp.zeros((8, LANES), f32)
        sq = jnp.zeros((8, LANES), f32)

        def step(n, carry):
            tot, sq = carry
            c0 = n * CHUNK
            conv = conv_chunk(field[:, pl.ds(c0, CHUNK + 2), :, lanes], w, CHUNK, False)
            act, back = gelu_pair(conv)
            for m in range(TRIO):
                rows, cells8 = chunk_rows(m, c0)
                am = act[m] * mask[cells8]
                active_o[rows, lanes] = am.reshape(CHUNK * 8, LANES)
                dgelu_o[rows, lanes] = back[m].reshape(CHUNK * 8, LANES)
                tot = tot + jnp.sum(am, 0)
                sq = sq + jnp.sum(am * am, 0)
            return tot, sq

        tot, sq = lax.fori_loop(0, SIDE // CHUNK, step, (tot, sq))
        sums[0, :, lanes] += tot
        sums[1, :, lanes] += sq
    for c in image_outs(i):
        c.start()

    @pl.when(i == own - 1)
    def _():
        cells_in = 0
        for n in range(own):
            s = side_of(cls, t * own + n)
            cells_in = cells_in + s * s
        for k in range(2):
            row = rowsum(sums[k])
            for l in range(3):
                tile[3 * k + l : 3 * k + l + 1, :] = row[:, l * LANES : (l + 1) * LANES]
        tile[6:8, :] = jnp.full((2, LANES), 1.0, f32) * cells_in.astype(f32)
        send_tile(tile, slots, sends, recvs)
        loads[2].wait()

        @pl.loop(0, own)
        def _(n):
            rows = pl.ds(pl.multiple_of(n * cells, 16), cells)
            fill_mask(masks, side_of(cls, t * own + n))
            to_canvas(floss.at[rows], nat, xm)
            lc_s[rows, :] = (xm[...] * cat3(masks[...].reshape(-1, LANES))).astype(bf16)

        for n in range(4, 6):
            in_copy(n).wait_recv()
        for n in range(6):
            out_copy(n).wait_send()
        stores = [
            pltpu.make_async_copy(src, dst, lsem.at[n])
            for n, (src, dst) in enumerate(
                ((wt, wt_o), (wp, wp_o), (win, win_o), (wout, wout_o), (lc_s, lc_h))
            )
        ]
        for c in stores:
            c.start()
        stat_o[...] = sum_tiles(tile, slots, sends, recvs)
        for c in stores:
            c.wait()
        for n in range(own):
            for c in image_outs(n):
                c.wait()


def middle_kernel(
    cls, first, active, lc, st, win_h, wout_h, bin_, gains, offs, taps, scales, ei, eo,
    out_h, gsec_h, gsh_h, gin_h, gout_h, mo_h, vec_o, inb_o, stat_o, st_o,
    nat, mask, field, gfield, loc, nrm, scl, macc, gacc, l3s, gms, hs, gs, acc, inb, win, wout, out_s, gsec_s, gsh_s, gin_o, gout_o, ein, eout, osem, gsem, wsem, tile, slots, sends, recvs,
):
    i = pl.program_id(0)
    t = lax.axis_index("tensor")
    own = cls.shape[0] // 2
    held = [pltpu.make_async_copy(win_h, win, wsem.at[0]), pltpu.make_async_copy(wout_h, wout, wsem.at[1])]
    errors = [pltpu.make_async_copy(ei.at[0], ein, wsem.at[2]), pltpu.make_async_copy(eo.at[0], eout, wsem.at[3])]
    rows_n = first.shape[0]
    base = pl.multiple_of(i * rows_n, 16)
    images = [(out_s, out_h), (gsec_s, gsec_h), (gsh_s, gsh_h)]

    def image_outs(n):
        rows = pl.ds(n * rows_n if isinstance(n, int) else pl.multiple_of(n * rows_n, 16), rows_n)
        return [pltpu.make_async_copy(a.at[rows], b.at[rows], osem.at[k, n]) for k, (a, b) in enumerate(images)]

    out_o, gsec_o, gsh_o = [a.at[pl.ds(base, rows_n)] for a, _ in images]
    hidden = win.shape[0] * win.shape[2]
    half = win.shape[2]

    @pl.when(i == 0)
    def _():
        greet_all()
        for c in held + errors:
            c.start()
        clear_edges(field)
        clear_edges(gfield)
        acc[...] = jnp.zeros_like(acc)
        inb[...] = jnp.zeros_like(inb)

    fill_mask(mask, side_of(cls, t * own + i))
    mk = cat3(mask[...].reshape(-1, LANES))
    mean, rstd, _ = batch_stats(st)
    zhat = (active[...] - mean) * rstd
    put_field(field, (zhat * gains[2:3, :] + offs[2:3, :]) * mk)
    for l in range(3):
        lanes = slice(l * LANES, (l + 1) * LANES)
        w = tap_rows(taps, 9, lanes)
        bias = offs[5:6, lanes]

        def step(n, carry):
            c0 = n * CHUNK
            conv = conv_chunk(field[:, pl.ds(c0, CHUNK + 2), :, lanes], w, CHUNK, False)
            for m in range(TRIO):
                rows, cells8 = chunk_rows(m, c0)
                loc[rows, lanes] = ((conv[m] + bias) * mask[cells8]).reshape(CHUNK * 8, LANES)
            return carry

        lax.fori_loop(0, SIDE // CHUNK, step, 0)
    second = first[...] + scales[1:2, :] * loc[...]
    normed, scale = layer_stats(second)
    nrm[...] = normed
    scl[...] = jnp.broadcast_to(scale, scl.shape)
    l3 = ((normed * gains[3:4, :] + offs[3:4, :]) * mk).astype(bf16)
    l3s[pl.ds(base, rows_n), :] = l3
    gm = (lc[...].astype(f32) * scales[2:3, :]).astype(bf16)
    gms[pl.ds(base, rows_n), :] = gm
    acc[3] += colsum(gm.astype(f32))

    @pl.when(i == 0)
    def _():
        for c in held:
            c.wait()

    step = half
    for n in range(hidden // step):
        hf, cols = n * step // half, slice(n * step % half, n * step % half + step)
        allc = slice(n * step, (n + 1) * step)
        pre = dg(l3s[pl.ds(base, rows_n), :], win[hf, :, cols], 1, 0) + jnp.concatenate(
            [bin_[r : r + 1, :] for r in range(n * step // LANES, (n + 1) * step // LANES)], -1
        )
        act, back = gelu_pair(pre)
        h = act.astype(bf16)
        hs[pl.ds(base, rows_n), allc] = h
        g = (dg(gms[pl.ds(base, rows_n), :], wout[hf, cols, :], 1, 1) * back).astype(bf16)
        gs[pl.ds(base, rows_n), allc] = g
        inb[:, allc] += colsum(g.astype(f32))
        m_part = dg(h, wout[hf, cols, :], 1, 0)
        g_part = dg(g, win[hf, :, cols], 1, 1)
        if n == 0:
            macc[...] = m_part
            gacc[...] = g_part
        else:
            macc[...] += m_part
            gacc[...] += g_part

    mlp = macc[...] + offs[6:7, :]
    second = first[...] + scales[1:2, :] * loc[...]
    from_canvas(second + scales[2:3, :] * mlp * mk, nat, out_o)
    acc[5] += colsum(lc[...].astype(f32) * mlp)
    normed, scale = nrm[...], cat3(scl[...])
    dout = gacc[...]
    acc[0] += colsum(dout)
    acc[1] += colsum(dout * normed)
    gsec = lc[...].astype(f32) + norm_back(dout, normed, scale, gains[3:4, :])
    gsec_o[...] = gsec
    acc[4] += colsum(gsec * loc[...])
    glocal = gsec * scales[1:2, :]
    acc[2] += colsum(glocal)
    put_field(gfield, glocal)
    for l in range(3):
        lanes = slice(l * LANES, (l + 1) * LANES)
        w = tap_rows(taps, 9, lanes)
        tot = jnp.zeros((8, LANES), f32)
        cross = jnp.zeros((8, LANES), f32)
        tap_sum = [jnp.zeros((8, LANES), f32) for _ in range(9)]

        def step(n, carry):
            tot, cross, tap_sum = carry[0], carry[1], list(carry[2:])
            c0 = n * CHUNK
            gwin = gfield[:, pl.ds(c0, CHUNK + 2), :, lanes]
            fwin = field[:, pl.ds(c0, CHUNK + 2), :, lanes]
            conv = conv_chunk(gwin, w, CHUNK, True)
            center = gwin[1 : 1 + TRIO, 1 : 1 + CHUNK]
            for a in range(3):
                for b in range(3):
                    prod = fwin[a : a + TRIO, b : b + CHUNK] * center
                    tap_sum[3 * a + b] += jnp.sum(prod, (0, 1))
            for m in range(TRIO):
                rows, cells8 = chunk_rows(m, c0)
                value = conv[m] * mask[cells8]
                flat = value.reshape(CHUNK * 8, LANES)
                gsh_o[rows, lanes] = flat
                z = (active[rows, lanes] - mean[:, lanes]) * rstd[:, lanes]
                tot = tot + jnp.sum(value, 0)
                cross = cross + colsum(flat * z)
            return (tot, cross, *tap_sum)

        tot, cross, *tap_sum = lax.fori_loop(0, SIDE // CHUNK, step, (tot, cross, *tap_sum))
        acc[6, :, lanes] += cross
        acc[7, :, lanes] += tot
        for k in range(9):
            acc[8 + k, :, lanes] += tap_sum[k]
    for c in image_outs(i):
        c.start()

    @pl.when(i == own - 1)
    def _():
        st_o[...] = st[...]
        cross, tot = rowsum(acc[6]), rowsum(acc[7])
        for l in range(3):
            lanes = slice(l * LANES, (l + 1) * LANES)
            tile[l : l + 1, :] = tot[:, lanes]
            tile[3 + l : 4 + l, :] = cross[:, lanes]
        tile[6:8, :] = jnp.zeros((2, LANES), f32)
        met_all()
        send_tile(tile, slots, sends, recvs)
        vec_o[...] = jnp.zeros_like(vec_o)
        for k in range(17):
            vec_o[k : k + 1, :] = rowsum(acc[k])
        inb_o[...] = jnp.zeros_like(inb_o)
        for k in range(hidden // LANES):
            inb_o[k : k + 1, :] = rowsum(inb[:, k * LANES : (k + 1) * LANES])
        l3_t = l3s[...].T
        gm_t = gms[...].T
        for c in errors:
            c.wait()
        outs = [(gin_o.at[0], gin_h.at[0]), (gin_o.at[1], gin_h.at[1]), (gout_o.at[0], gout_h.at[0]),
                (gout_o.at[1], gout_h.at[1]), (eout, mo_h)]
        outs = [pltpu.make_async_copy(src, dst, gsem.at[n]) for n, (src, dst) in enumerate(outs)]
        for hf in range(2):
            gout_o[hf] = dg(gm_t, hs[:, hf * half : (hf + 1) * half], 1, 0)
            outs[2 + hf].start()
        eout[...] += gout_o[t].T
        outs[4].start()
        for hf in range(2):
            grad = dg(l3_t, gs[:, hf * half : (hf + 1) * half], 1, 0)
            gin_o[hf] = grad + jnp.where(t == hf, ein[...], 0.0)
            outs[hf].start()
        stat_o[...] = sum_tiles(tile, slots, sends, recvs)
        for n in range(own):
            for c in image_outs(n):
                c.wait()
        for c in outs:
            c.wait()


def last_kernel(
    far,
    cls, sharp, tok_h, first, active, dgelu, gsec, gsh, low_h, q, k, v, mix_h, attn, gram, rs,
    st, gst, wt_h, wp_h, gains, offs, taps, scales,
    gin, gout, eq, ep, mo_part, bq, bp, bi, bo, vec2, inb,
    ingrad_o, mq, mp_o, mi, mo, oq_o, op_o, oi_o, oo_o, rq_o, rp_o, ri_o, ro_o, rqs_o, vec_o,
    nat, mask, scl, field, gfield, gfirst, gproj, acc, bias_acc, sharp_rows,
    mp, ai, ao, aq, ap, gt, gp, vec3, qb, obuf, tok, low, mix, wt, wp, perm, bpair, bsem, hsem, lsem, psend, precv,
    *exchange,
):
    lefts, rights, late = Spread(far, *exchange[0:11]), Spread(far, *exchange[11:22]), Spread(far, *exchange[22:33])
    left_qp = Broadcast(far, 0, *exchange[33:41])
    i = pl.program_id(0)
    t = lax.axis_index("tensor")
    own = cls.shape[0] // 2
    heads = sharp.shape[0]
    width = tok.shape[1]
    cells = tok.shape[0] // own
    head = width // heads
    other = {"tensor": 1 - t}
    part = width // 2
    cols_q = bq.shape[1]
    tiles_q = -(-cols_q // LANES)
    right_qp = Broadcast(far, tiles_q, *exchange[41:49])
    base = pl.multiple_of(i * cells, 16)
    here = pl.ds(base, cells)
    own_rows = pl.ds(pl.multiple_of(t * part, 8), part)
    loads = [
        pltpu.make_async_copy(src, dst, lsem.at[n])
        for n, (src, dst) in enumerate(
            ((gin.at[t], mi), (mo_part, mo), (eq.at[0], mq), (ep.at[0], mp_o))
        )
    ]
    held = [
        pltpu.make_async_copy(src, dst, hsem.at[n])
        for n, (src, dst) in enumerate(
            ((tok_h, tok), (wp_h, wp), (low_h, low), (mix_h, mix), (wt_h, wt))
        )
    ]
    pair_in = [remote(gin.at[1 - t], ai, psend.at[0], precv.at[0], other), remote(gout.at[1 - t], ao, psend.at[1], precv.at[1], other)]
    pair_qp = [remote(gt.at[j, 1 - t], aq.at[j], psend.at[2 + j], precv.at[2 + j], other) for j in range(3)]
    pair_qp.append(remote(gp.at[1 - t], ap, psend.at[5], precv.at[5], other))
    @pl.when(i == 0)
    def _():
        greet(far)
        for c in held + loads:
            c.start()
        fill_perm(perm, heads // 2, head)
        pieces = jnp.concatenate([x.astype(f32) for x in split3(bq[...])], 0).astype(bf16)
        turned = dg(pieces, perm[...], 1, 1)
        bpair[t] = turned[0:8] + turned[8:16] + turned[16:24]
        gt[...] = jnp.zeros_like(gt)
        gp[...] = jnp.zeros_like(gp)
        gproj[0:cells] = jnp.zeros((cells, gproj.shape[1]), bf16)
        ingrad_o[0:cells] = jnp.zeros((cells, width), bf16)
        mp[...] = jnp.zeros_like(mp)
        lefts.pay[...] = jnp.zeros_like(lefts.pay)
        rights.pay[...] = jnp.zeros_like(rights.pay)
        vec3[...] = jnp.zeros_like(vec3)
        qb[...] = jnp.zeros_like(qb)
        right_qp.x[...] = jnp.zeros_like(right_qp.x)
        sharp_rows[...] = jnp.zeros_like(sharp_rows)
        for h, (w, r) in enumerate(head_spots(heads, head)):
            sharp_rows[w, r : r + head, :] = jnp.full((head, 2 * LANES), 1.0, f32) * sharp[h]
        clear_edges(field)
        clear_edges(gfield)
        acc[...] = jnp.zeros_like(acc)
        bias_acc[...] = jnp.zeros_like(bias_acc)

    fill_mask(mask, side_of(cls, t * own + i))
    mk = cat3(mask[...].reshape(-1, LANES))
    mean, rstd, inv = batch_stats(st)
    gsum = lambda r: jnp.concatenate([gst[r : r + 1, :], gst[r + 1 : r + 2, :], gst[r + 2 : r + 3, :]], -1)
    gain_bn = gains[2:3, :]
    zhat = (active[...] - mean) * rstd
    gact = rstd * (gsh[...] * gain_bn - gsum(0) * gain_bn * inv - zhat * (gsum(3) * gain_bn * inv)) * mk
    put_field(gfield, gact * dgelu[...])
    normed, scale = layer_stats(first[...])
    gfirst[here, :] = normed
    scl[...] = jnp.broadcast_to(scale, scl.shape)
    put_field(field, (normed * gains[1:2, :] + offs[1:2, :]) * mk)
    for l in range(3):
        lanes = slice(l * LANES, (l + 1) * LANES)
        w = tap_rows(taps, 0, lanes)
        tap_sum = [jnp.zeros((8, LANES), f32) for _ in range(9)]

        def step(n, carry):
            tap_sum = list(carry)
            c0 = n * CHUNK
            gwin = gfield[:, pl.ds(c0, CHUNK + 2), :, lanes]
            fwin = field[:, pl.ds(c0, CHUNK + 2), :, lanes]
            conv = conv_chunk(gwin, w, CHUNK, True)
            center = gwin[1 : 1 + TRIO, 1 : 1 + CHUNK]
            for a in range(3):
                for b in range(3):
                    prod = fwin[a : a + TRIO, b : b + CHUNK] * center
                    tap_sum[3 * a + b] += jnp.sum(prod, (0, 1))
            for m in range(TRIO):
                rows, cells8 = chunk_rows(m, c0)
                nat[l, rows, :] = (conv[m] * mask[cells8]).reshape(CHUNK * 8, LANES)
            return tuple(tap_sum)

        tap_sum = lax.fori_loop(0, SIDE // CHUNK, step, tuple(tap_sum))
        for n in range(9):
            acc[7 + n, :, lanes] += tap_sum[n]

    @pl.when(i == 0)
    def _():
        met(far)
        for c in pair_in:
            c.start()
        remote(bpair.at[t], bpair.at[t], bsem.at[0], bsem.at[1], other).start()
        for c in held:
            c.wait()

    @pl.when(i == own - 2)
    def _():
        for c in loads:
            c.wait()
        for c in pair_in:
            c.wait()
        remote(bpair.at[t], bpair.at[t], bsem.at[0], bsem.at[1], other).wait_send()
        remote(bpair.at[1 - t], bpair.at[1 - t], bsem.at[0], bsem.at[1], other).wait_recv()
        mp[own_rows, :] = mp_o[...]
        for m, tile in enumerate(tiles(thin(bq[...], mq[...], 0)) + tiles(thin(bp[...], mp[...], 1))):
            left_qp.x[m] = tile
        mi[...] += ai[...]
        mo[...] += ao[...].T
        li = tiles(thin(bi[...], mi[...], 1))
        lo = tiles(thin(bo[...], mo[...], 1))
        n = 0
        for tile in li:
            lefts.pay[n] = tile
            n += 1
        for m, tile in enumerate(lo):
            lefts.pay[n + t * len(lo) + m] = tile
        n += 2 * len(lo)
        for tile in row_tiles(vec2) + row_tiles(inb):
            lefts.pay[n] = tile
            n += 1
        lefts.start()

    @pl.when(i == own - 1)
    def _():
        lefts.gather()

    before = pl.ds(pl.multiple_of(jnp.maximum(i - 1, 0) * cells, 16), cells)
    for j in range(3):
        gt[j] += dg(gproj[before, j * width : (j + 1) * width], low[before, :], 0, 0).reshape(2, part, width)
    gp[...] += dg(mix[before, :], ingrad_o[before, :], 0, 0).reshape(2, part, width)
    dout = jnp.concatenate([nat[0], nat[1], nat[2]], -1)
    normed, scale = gfirst[here, :], cat3(scl[...])
    acc[2] += colsum(dout * normed)
    acc[3] += colsum(dout)
    grad = gsec[...] + norm_back(dout, normed, scale, gains[1:2, :])
    gfirst[here, :] = grad
    acc[5] += colsum(grad * (first[...] - tok[here, :].astype(f32)))
    gal = (grad * scales[0:1, :]).astype(bf16)
    acc[4] += colsum(gal.astype(f32))
    ingrad_o[here, :] = gal
    gmix, gmix_lo = split2(dg(gal, wp[...], 1, 1))
    lane1 = lax.broadcasted_iota(jnp.int32, (1, width), 1)
    sharp_lane = jnp.zeros((1, width), f32)
    for h in range(heads):
        sharp_lane = jnp.where((lane1 >= h * head) & (lane1 < (h + 1) * head), sharp[h], sharp_lane)
    ones = jnp.ones((8, 2 * LANES), bf16)
    wins = [slice(w * LANES, (w + 2) * LANES) for w in range(2)]
    a = attn[0]
    gattn = jnp.stack([dg(gmix[:, c], v[:, c], 0, 0) + dg(gmix_lo[:, c], v[:, c], 0, 0) for c in wins])
    gval = [dg(gmix[:, c], a[w].astype(bf16), 1, 0) for w, c in enumerate(wins)]
    gsc = a * (gattn - jnp.sum(gattn * a, -1, keepdims=True))
    shi, slo = split2(gsc * sharp_rows[...])
    gqu = [dg(k[:, c], shi[w], 1, 1) + dg(k[:, c], slo[w], 1, 1) for w, c in enumerate(wins)]
    gku = [dg(q[:, c], shi[w], 1, 0) + dg(q[:, c], slo[w], 1, 0) for w, c in enumerate(wins)]
    weighted = gsc * gram[0]
    hi, lo = split2(weighted)
    chan = [dg(ones, hi[w], 1, 1) + dg(ones, lo[w], 1, 1) for w in range(2)]
    chan_k = [rowsum(weighted[w] * sharp_rows[w]) for w in range(2)]
    chan = merge(*chan)[0:1, :]
    acc[6, 0:1, :] += chan
    gq = rs[0, 0:1, :] * (merge(*gqu) - q[...].astype(f32) * (chan * sharp_lane))
    gk = rs[0, 1:2, :] * (merge(*gku) - k[...].astype(f32) * merge(*chan_k))
    for j, piece in enumerate((gq, gk, merge(*gval))):
        small = piece.astype(bf16)
        gproj[here, j * width : (j + 1) * width] = small
        bias_acc[j] += colsum(small.astype(f32))

    @pl.when(i == own - 2)
    def _():
        lefts.middle()

    @pl.when(i == own - 1)
    def _():
        for j in range(3):
            gt[j] += dg(gproj[here, j * width : (j + 1) * width], low[here, :], 0, 0).reshape(2, part, width)
            pair_qp[j].start()
        gp[...] += dg(mix[here, :], ingrad_o[here, :], 0, 0).reshape(2, part, width)
        pair_qp[3].start()
        thirds = [bpair[hf, :, j * part : (j + 1) * part] for j in range(3) for hf in range(2)]
        left_q = thin(jnp.concatenate(thirds, -1), gt[...].reshape(6 * part, width), 0)
        for m, tile in enumerate(tiles(left_q) + tiles(thin(bp[...], gp[...].reshape(width, width), 1))):
            left_qp.x[m] += tile
        left_qp.start()
        lefts.finish()
        tiles_i = width // LANES
        tiles_o = 2 * mo.shape[0] // LANES
        get = lambda a, b: jnp.concatenate([lefts.full[m] for m in range(a, b)], -1)
        oi, oo = orthonormal([get(0, tiles_i), get(tiles_i, tiles_i + tiles_o)])
        first_vec = tiles_i + tiles_o
        count2, count3 = vec2.shape[0] * 3 // 8, vec3.shape[0] * 3 // 8
        for m in range(count2):
            vec_o[m * 8 : m * 8 + 8, :] = lefts.full[first_vec + m]
        for m in range(2):
            at = (count2 + count3 + m) * 8
            vec_o[at : at + 8, :] = lefts.full[first_vec + count2 + m]
        half_o = mo.shape[0]
        obuf[0] = oo[:, :half_o]
        obuf[1] = oo[:, half_o:]
        oo_own = obuf[t]
        ri = tiles(thin(oi, mi[...], 0))
        ro = tiles(thin(oo_own, mo[...], 0))
        for m, tile in enumerate(ri):
            rights.pay[t * len(ri) + m] = tile
        for m, tile in enumerate(ro):
            rights.pay[2 * len(ri) + m] = tile
        rights.start()

        for c in pair_qp:
            c.wait_recv()
        turned = jnp.concatenate([gt[j, t] + aq[j] for j in range(3)], 0)
        grad_q = None
        for piece in split3(turned):
            term = dg(perm[...], piece, 0, 0)
            grad_q = term if grad_q is None else grad_q + term
        mq[...] += grad_q
        mp_o[...] += gp[t] + ap[...]
        mp[own_rows, :] = mp_o[...]
        def input_dout(n):
            rows = pl.ds(pl.multiple_of(n * cells, 16), cells)
            dout = dg(gproj[rows, :], wt[...].reshape(3 * width, width), 1, 0)
            normed, scale = layer_stats(tok[rows, :].astype(f32))
            return rows, dout, normed, scale

        def input_sums(n):
            _, dout, normed, _ = input_dout(n)
            acc[0] += colsum(dout * normed)
            acc[1] += colsum(dout)

        pl.loop(0, 1)(input_sums)

        def input_out(n):
            rows, dout, normed, scale = input_dout(n)
            result = gfirst[rows, :] + norm_back(dout, normed, scale, gains[0:1, :])
            from_canvas(result, nat, ingrad_o.at[rows])

        left_qp.middle()
        rights.middle()
        pl.loop(1, own)(input_sums)
        for n in range(16):
            vec3[n : n + 1, :] = rowsum(acc[n])
        vec3[5:6, :] = rowsum(acc[5]) / scales[0:1, :]
        third = perm.shape[0] // 3
        lane8 = lax.broadcasted_iota(jnp.int32, (8, width), 1)
        total = None
        for j in range(3):
            rows = perm[j * third : (j + 1) * third, :]
            both = jnp.concatenate([rows, rows], 0)
            pieces = []
            for hf in range(2):
                mine = jnp.where((lane8 >= hf * third) & (lane8 < (hf + 1) * third), bias_acc[j], 0.0)
                pieces += [piece.astype(f32) for piece in split3(mine)]
            term = dg(jnp.concatenate(pieces, 0).astype(bf16), both, 1, 0)
            total = term if total is None else total + term
        row = jnp.concatenate([rowsum(total[0:24]), rowsum(total[24:48])], -1)
        for n in range(row.shape[1] // LANES):
            qb[n : n + 1, :] = row[:, n * LANES : (n + 1) * LANES]
        for m, tile in enumerate(row_tiles(vec3) + row_tiles(qb)):
            late.pay[m] = tile
        late.start()
        pl.loop(0, 1)(input_out)
        rights.gather()
        total = left_qp.finish()
        oq, op = orthonormal(
            [jnp.concatenate([total[m] for m in range(3)], -1), jnp.concatenate([total[m] for m in range(3, 6)], -1)]
        )
        rq = thin(oq, mq[...], 1)
        for m in range(tiles_q):
            wide = min(LANES, cols_q - m * LANES)
            right_qp.x[m, :, 0:wide] = rq[:, m * LANES : m * LANES + wide]
        for m, tile in enumerate(tiles(thin(op, mp[...], 0))):
            right_qp.x[tiles_q + m] = tile
        right_qp.start()
        share = 1.0 / (far * NEAR)
        oq_o[...] = stacked(oq)[1]
        mp[:, 0:48] = stacked(op)[0].T
        op_o[...] = mp[own_rows, 0:48]
        late.middle()
        pl.loop(1, own - 1)(input_out)
        oi_o[...] = stacked(oi)[0].T
        oo_o[...] = stacked(oo_own)[0].T
        right_qp.middle()
        late.gather()
        pl.loop(own - 1, own)(input_out)
        rights.finish()
        for m in range(len(ri)):
            ri_o[:, m * LANES : (m + 1) * LANES] = rights.full[t * len(ri) + m] * share
        for m in range(len(ro)):
            ro_o[:, m * LANES : (m + 1) * LANES] = rights.full[2 * len(ri) + m] * share
        total = right_qp.finish() * share
        for m in range(tiles_q):
            wide = min(LANES, cols_q - m * LANES)
            rq_o[:, m * LANES : m * LANES + wide] = total[m][:, 0:wide]
        for m in range(3):
            rp_o[:, m * LANES : (m + 1) * LANES] = total[tiles_q + m]
        rqs_o[...] = stacked(rq_o[...])[0].T
        late.finish()
        for m in range(count3):
            vec_o[(count2 + m) * 8 : (count2 + m) * 8 + 8, :] = late.full[m]
        for m in range(2):
            at = (count2 + count3 + 2 + m) * 8
            vec_o[at : at + 8, :] = late.full[count3 + m]
        for c in pair_qp:
            c.wait_send()
        for group in (lefts, rights, late, left_qp, right_qp):
            group.drain()


def orthonormal(rows):
    index = lax.broadcasted_iota(jnp.int32, rows[0].shape[:1] + (1,), 0)
    rank = rows[0].shape[0]
    for n in range(rank):
        done = []
        for v in rows:
            column = v[n : n + 1, :]
            dots = jnp.sum(v * column, -1, keepdims=True)
            scale = lax.rsqrt(dots[n : n + 1, :] + 1e-06)
            unit = column * scale
            later = v - (dots * scale) * unit
            done.append(jnp.where(index > n, later, jnp.where(index == n, unit, v)))
        rows = done
    return rows


class Spread:
    def __init__(self, far, pay, slots, part, tops, full, s1, r1, s2, r2, s3, r3):
        self.far, self.pay, self.slots, self.part, self.tops, self.full = far, pay, slots, part, tops, full
        self.sems = s1, r1, s2, r2, s3, r3
        self.per = slots.shape[1]
        self.hi, self.lo, self.t, self.me = place()

    def piece(self, ref, index):
        return ref.at[pl.ds(index * self.per, self.per)]

    def first(self, k, incoming):
        index, there = near_partner(self.me, self.hi, k)
        slot = index if incoming else self.me
        return remote(self.piece(self.pay, index), self.slots.at[slot], self.sems[0].at[k], self.sems[1].at[slot], there)

    def second(self, k, incoming):
        index, there = far_partner(self.hi, self.lo, self.t, k, self.far)
        slot = index if incoming else self.hi
        return remote(self.part, self.tops.at[slot], self.sems[2].at[k], self.sems[3].at[slot], there)

    def third(self, k, incoming):
        index, there = near_partner(self.me, self.hi, k)
        slot = index if incoming else self.me
        return remote(
            self.piece(self.full, self.me), self.piece(self.full, slot), self.sems[4].at[k], self.sems[5].at[slot], there
        )

    def start(self):
        for k in range(1, 2 * NEAR):
            self.first(k, False).start()
        self.slots[self.me] = self.pay[pl.ds(self.me * self.per, self.per)]

    def middle(self):
        for k in range(1, 2 * NEAR):
            self.first(k, True).wait_recv()
        total = jnp.sum(self.slots[...], 0)
        self.part[...] = total
        self.tops[self.hi] = total
        for k in range(1, self.far):
            self.second(k, False).start()

    def gather(self):
        for k in range(1, self.far):
            self.second(k, True).wait_recv()
        self.full[pl.ds(self.me * self.per, self.per)] = jnp.sum(self.tops[...], 0)
        for k in range(1, 2 * NEAR):
            self.third(k, False).start()

    def finish(self):
        for k in range(1, 2 * NEAR):
            self.third(k, True).wait_recv()

    def drain(self):
        for k in range(1, 2 * NEAR):
            self.first(k, False).wait_send()
            self.third(k, False).wait_send()
        for k in range(1, self.far):
            self.second(k, False).wait_send()


def spread_scratch(per, far):
    dma = pltpu.SemaphoreType.DMA
    near = 2 * NEAR
    vm = lambda *shape: pltpu.VMEM(shape + (8, LANES), f32)
    return [
        vm(near * per), vm(near, per), vm(per), vm(far, per), vm(near * per),
        dma((near,)), dma((near,)), dma((far,)), dma((far,)), dma((near,)), dma((near,)),
    ]


class Broadcast:
    def __init__(self, far, own, x, slots, part, tops, s1, r1, s2, r2):
        self.far, self.own, self.x, self.slots, self.part, self.tops = far, own, x, slots, part, tops
        self.sems = s1, r1, s2, r2
        self.hi, self.lo, self.t, self.me = place()

    def first(self, k, incoming):
        index, there = near_partner(self.me, self.hi, k)
        slot = index if incoming else self.me
        skip = self.own if k % 2 else 0
        count = self.x.shape[0] - skip
        return remote(
            self.x.at[pl.ds(skip, count)], self.slots.at[slot, pl.ds(skip, count)],
            self.sems[0].at[k], self.sems[1].at[slot], there,
        )

    def second(self, k, incoming):
        index, there = far_partner(self.hi, self.lo, self.t, k, self.far)
        slot = index if incoming else self.hi
        return remote(self.part, self.tops.at[slot], self.sems[2].at[k], self.sems[3].at[slot], there)

    def start(self):
        for k in range(1, 2 * NEAR):
            self.first(k, False).start()
        self.slots[self.me] = self.x[...]

    def middle(self):
        for k in range(1, 2 * NEAR):
            self.first(k, True).wait_recv()
        own = self.own
        if own:
            total = self.slots[self.t, 0:own]
            for k in range(1, NEAR):
                total = total + self.slots[2 * k + self.t, 0:own]
            self.part[0:own] = total
        self.part[own:] = jnp.sum(self.slots[:, own:], 0)
        self.tops[self.hi] = self.part[...]
        for k in range(1, self.far):
            self.second(k, False).start()

    def finish(self):
        for k in range(1, self.far):
            self.second(k, True).wait_recv()
        return jnp.sum(self.tops[...], 0)

    def drain(self):
        for k in range(1, 2 * NEAR):
            self.first(k, False).wait_send()
        for k in range(1, self.far):
            self.second(k, False).wait_send()


def broadcast_scratch(count, far):
    dma = pltpu.SemaphoreType.DMA
    near = 2 * NEAR
    vm = lambda *shape: pltpu.VMEM(shape + (8, LANES), f32)
    return [vm(count), vm(near, count), vm(count), vm(far, count), dma((near,)), dma((near,)), dma((far,)), dma((far,))]


def row_tiles(ref):
    return [
        ref[r * 8 : r * 8 + 8, c * LANES : (c + 1) * LANES]
        for c in range(ref.shape[1] // LANES)
        for r in range(ref.shape[0] // 8)
    ]


def tiles(x):
    return [x[:, n * LANES : (n + 1) * LANES] for n in range(x.shape[1] // LANES)]


def stacked(x):
    hi, mid, lo = split3(x)
    hi, mid, lo = hi.astype(f32), mid.astype(f32), lo.astype(f32)
    left = jnp.concatenate([hi, hi, mid, hi, mid, lo], 0)
    right = jnp.concatenate([hi, mid, hi, lo, mid, hi], 0)
    return left, right


def update_kernel(
    oq, op, oi, oo, rqs, rp, ri, ro, rq, mq, mp, mi, mo, wq, wp, wi, wo, vq, vp, vi, vo,
    vec, one, two, gains, offs, taps, scales, bq, sharp, bi, gains_v, offs_v, taps_v, scales_v, bq_v, sharp_v, bi_v,
    wq_o, wp_o, wi_o, wo_o, vq_o, vp_o, vi_o, vo_o, eq_o, ep_o, ei_o, eo_o,
    gains_o, offs_o, taps_o, scales_o, bq_o, sharp_o, bi_o,
    gains_m, offs_m, taps_m, scales_m, bq_m, sharp_m, bi_m, tq_o, tp_o, ti_o, to_o, one_o, two_o,
    *, share,
):
    at = pl.program_id(0)
    one_o[...] = one[...]
    two_o[...] = two[pl.ds(pl.multiple_of(at * one.shape[0], 16), one.shape[0]), :]
    groups = (
        (oq, None, mq, wq, vq, wq_o, vq_o, eq_o),
        (op, rp, mp, wp, vp, wp_o, vp_o, ep_o),
        (oi, ri, mi, wi, vi, wi_o, vi_o, ei_o),
        (oo, ro, mo, wo, vo, wo_o, vo_o, eo_o),
    )
    steps = pl.num_programs(0)

    def own_part(ref):
        size = ref.shape[0] // steps
        return ref[pl.ds(pl.multiple_of(at * size, 8), size), :]

    for o, r, m, w, v, w_o, v_o, e_o in groups:
        if r is None:
            approx = dg(own_part(rqs).astype(bf16), o[...].astype(bf16), 1, 0)
        else:
            approx = dg(own_part(o).astype(bf16), stacked(r[...])[1].astype(bf16), 1, 0)
        moment = momentum_decay * v[...] + approx
        v_o[...] = moment
        w_o[...] = w[...] - learn_rate * moment
        size = w.shape[0]
        e_o[0] = m[pl.ds(pl.multiple_of(at * size, 8), size), :] - approx

    @pl.when(pl.program_id(0) == 0)
    def _():
        for r, t_o in ((rq, tq_o), (rp, tp_o), (ri, ti_o), (ro, to_o)):
            t_o[...] = r[...]

        def step(grad, value, moment, v_out, m_out, rows):
            new = momentum_decay * moment[rows, :] + grad * share
            m_out[rows, :] = new
            v_out[rows, :] = value[rows, :] - learn_rate * new

        def row2(a, b):
            return jnp.concatenate([vec[24 * c + a : 24 * c + b, :] for c in range(3)], -1)

        def row3(a, b):
            return jnp.concatenate([vec[72 + 16 * c + a : 72 + 16 * c + b, :] for c in range(3)], -1)

        def each(grads, value, moment, v_out, m_out):
            for n, g in enumerate(grads):
                step(g, value, moment, v_out, m_out, slice(n, n + 1))

        each([row3(0, 1), row3(2, 3), row2(6, 7), row2(1, 2)], gains, gains_v, gains_o, gains_m)
        each(
            [row3(1, 2), row3(3, 4), row2(7, 8), row2(0, 1), row3(4, 5), row2(2, 3), row2(3, 4)],
            offs, offs_v, offs_o, offs_m,
        )
        each([row3(5, 6), row2(4, 5), row2(5, 6)], scales, scales_v, scales_o, scales_m)
        each([row3(7 + n, 8 + n) for n in range(9)] + [row2(8 + n, 9 + n) for n in range(9)],
             taps, taps_v, taps_o, taps_m)
        base = 72 + 48
        half = bi.shape[0]
        step(vec[base : base + half, :], bi, bi_v, bi_o, bi_m, slice(None))
        base += 16
        step(vec[base : base + bq.shape[0], :], bq, bq_v, bq_o, bq_m, slice(None))
        width = gains.shape[1]
        heads = sharp.shape[1]
        head = width // heads
        chan = lax.broadcasted_iota(jnp.int32, (width, heads), 0)
        lane = lax.broadcasted_iota(jnp.int32, (width, heads), 1)
        pick = jnp.where((chan >= lane * head) & (chan < (lane + 1) * head), 1.0, 0.0).astype(f32)
        grad = thin(jnp.broadcast_to(row3(6, 7), (8, width)), pick, 0)
        step(grad[0:1, :], sharp, sharp_v, sharp_o, sharp_m, slice(None))


def body(
    tokens, classes, loss,
    tri, tri_b, sharp, mapw, expw, exp_b, conw, gains, offs, taps, scales,
    tri_v, map_v, exp_v, con_v, tri_b_v, sharp_v, exp_b_v, gains_v, offs_v, taps_v, scales_v,
    tri_e, map_e, exp_e, con_e, tri_f, map_f, exp_f, con_f,
):
    import functools

    far = lax.axis_size("dp") // NEAR
    rows, width = tokens.shape
    own = classes.shape[0] // 2
    cells = rows // own
    heads = sharp.shape[0]
    head = width // heads
    part = width // 2
    cols = tri.shape[1]
    half = expw.shape[1]
    hidden = 2 * half
    vm = pl.BlockSpec(memory_space=pltpu.VMEM)
    sm = pl.BlockSpec(memory_space=pltpu.SMEM)
    anyspace = pl.BlockSpec(memory_space=pl.ANY)

    def whole(*shape):
        return pl.BlockSpec(shape, lambda i: (0,) * len(shape), pipeline_mode=pl.Buffered(1))

    image = pl.BlockSpec((cells, width), lambda i: (i, 0))
    square = pl.BlockSpec((1, 2, 2 * LANES, 2 * LANES), lambda i: (i, 0, 0, 0))
    eight = pl.BlockSpec((1, 8, width), lambda i: (i, 0, 0))
    smem = pl.BlockSpec(memory_space=pltpu.SMEM)
    vecs = [whole(4, width), whole(7, width), whole(18, width), whole(3, width)]
    field = pltpu.VMEM((TRIO + 2, SIDE + 2, GROUPS, width), f32)
    nat = pltpu.VMEM((3, cells, LANES), f32)
    mask = pltpu.VMEM((TRIO * SIDE, GROUPS, LANES), f32)
    canvas = pltpu.VMEM((cells, width), f32)

    dma = pltpu.SemaphoreType.DMA
    devices = lax.axis_size("dp") * 2
    two_windows = pltpu.VMEM((2, 2 * LANES, 2 * LANES), f32)
    tile_exchange = [
        pltpu.VMEM((8, LANES), f32), pltpu.VMEM((devices, 8, LANES), f32),
    ]
    first, active, dgelu, low, q, k, v, mix, xc, attn, gram, rs, stat, lc, wt, wp, win, wout = pl.pallas_call(
        first_kernel,
        grid=(own,),
        out_shape=[sds((rows, width))] * 3
        + [sds((rows, width), bf16)] * 6
        + [sds((own, 2, 2 * LANES, 2 * LANES))] * 2
        + [sds((own, 8, width)), sds((8, LANES)), sds((rows, width), bf16)]
        + [sds((3, 2, part, width), bf16), sds((2, part, width), bf16),
           sds((2, width, half), bf16), sds((2, half, width), bf16)],
        in_specs=[smem, smem, anyspace, whole(cols, width), whole(part, width), whole(2 * cols // LANES, LANES)]
        + vecs + [anyspace] * 3,
        out_specs=[anyspace] * 11 + [eight, whole(8, LANES)] + [anyspace] * 5,
        scratch_shapes=[
            nat, mask, canvas, field, two_windows, two_windows, pltpu.VMEM((2, 8, width), f32),
            pltpu.VMEM((3, 2, part, width), bf16), pltpu.VMEM((2, part, width), bf16),
            pltpu.VMEM((2, width, half), bf16), pltpu.VMEM((2, half, width), bf16),
            pltpu.VMEM((width, half), f32), pltpu.VMEM((half, width), f32), pltpu.VMEM((rows, width), bf16),
            pltpu.VMEM((rows, width), bf16), mask,
            pltpu.VMEM((cols, cols), bf16), pltpu.VMEM((8, width), f32),
        ] + [pltpu.VMEM((rows, width), f32)] * 3 + [pltpu.VMEM((rows, width), bf16)] * 6
        + [pltpu.VMEM((own, 2, 2 * LANES, 2 * LANES), f32)] * 2 + [pltpu.VMEM((rows, width), bf16)]
        + tile_exchange + [dma((11, own)), dma((5,)), dma((6,)), dma((6,)), dma((devices,)), dma((devices,))],
        compiler_params=params(61, collective_id=0, has_side_effects=True),
        name="first_part",
    )(classes, sharp, tokens, tri.T, mapw, tri_b.reshape(-1, LANES), gains, offs, taps, scales, expw, conw, loss)
    wt = wt.reshape(3, width, width)
    wp = wp.reshape(width, width)

    block_out, gsec, gsh, gin, gout, mo_part, vec2, inb, gstat, stat = pl.pallas_call(
        middle_kernel,
        grid=(own,),
        out_shape=[
            sds((rows, width), bf16), sds((rows, width)), sds((rows, width)),
            sds((2, width, half)), sds((2, width, half)), sds((half, width)), held((24, width)), held((16, LANES)), held((8, LANES)), held((8, LANES)),
        ],
        in_specs=[smem, image, image, image, whole(8, LANES), anyspace, anyspace,
                  whole(hidden // LANES, LANES)] + vecs + [anyspace] * 2,
        out_specs=[anyspace] * 6 + [vm] * 4,
        scratch_shapes=[
            nat, mask, field, field, canvas, canvas, pltpu.VMEM((cells, LANES), f32), canvas, canvas,
            pltpu.VMEM((rows, width), bf16), pltpu.VMEM((rows, width), bf16),
            pltpu.VMEM((rows, hidden), bf16), pltpu.VMEM((rows, hidden), bf16),
            pltpu.VMEM((17, 8, width), f32), pltpu.VMEM((8, hidden), f32),
            pltpu.VMEM((2, width, half), bf16), pltpu.VMEM((2, half, width), bf16),
            pltpu.VMEM((rows, width), bf16), pltpu.VMEM((rows, width), f32), pltpu.VMEM((rows, width), f32),
            pltpu.VMEM((2, width, half), f32), pltpu.VMEM((2, width, half), f32),
            pltpu.VMEM((width, half), f32), pltpu.VMEM((half, width), f32),
            dma((3, own)), dma((5,)), dma((4,)),
        ] + tile_exchange + [dma((devices,)), dma((devices,))],
        compiler_params=params(56, collective_id=1, has_side_effects=True),
        name="middle_part",
    )(classes, first, active, lc, stat, win, wout, exp_b.reshape(hidden // LANES, LANES), gains, offs, taps, scales,
      exp_e, con_e)
    input_grad, mq, mp, mi, mo, oq, op, oi, oo, rq, rp, ri, ro, rqs, vec = pl.pallas_call(
        functools.partial(last_kernel, far),
        grid=(own,),
        out_shape=[
            held((rows, width), bf16),
            held((cols, width)), held((part, width)), held((width, half)), held((half, width)),
            held((48, width)), held((part, 48)), held((width, 48)), held((half, 48)),
            held((8, cols)), held((8, width)), held((8, half)), held((8, width)), held((cols, 48)), held((152, LANES)),
        ],
        in_specs=[smem, smem, anyspace] + [image] * 5 + [anyspace] + [image] * 3
        + [anyspace] + [square, square, eight, vm, vm] + [anyspace] * 2 + vecs
        + [anyspace] * 5 + [whole(8, cols), whole(8, width), whole(8, half), whole(8, width), vm, vm],
        out_specs=[vm] * 15,
        scratch_shapes=[
            nat, mask, pltpu.VMEM((cells, LANES), f32), field, field, pltpu.VMEM((rows, width), f32),
            pltpu.VMEM((rows, 3 * width), bf16),
            pltpu.VMEM((16, 8, width), f32), pltpu.VMEM((3, 8, width), f32), two_windows,
            pltpu.VMEM((width, width), f32),
            pltpu.VMEM((width, half), f32), pltpu.VMEM((width, half), f32),
            pltpu.VMEM((3, part, width), f32), pltpu.VMEM((part, width), f32),
            pltpu.VMEM((3, 2, part, width), f32), pltpu.VMEM((2, part, width), f32),
            pltpu.VMEM((16, width), f32), pltpu.VMEM((16, LANES), f32),
            pltpu.VMEM((2, 8, half), f32),
            pltpu.VMEM((rows, width), bf16), pltpu.VMEM((rows, width), bf16), pltpu.VMEM((rows, width), bf16),
            pltpu.VMEM((3, width, width), bf16), pltpu.VMEM((width, width), bf16), pltpu.VMEM((cols, cols), bf16), pltpu.VMEM((2, 8, cols), f32), dma((2,)),
            dma((6,)), dma((6,)), dma((6,)), dma((6,)),
        ]
        + spread_scratch(4, far) + spread_scratch(2, far) + spread_scratch(1, far)
        + broadcast_scratch(6, far) + broadcast_scratch(-(-cols // LANES) + 3, far),
        compiler_params=params(47 + far // 8, collective_id=2, has_side_effects=True),
        name="last_part",
    )(classes, sharp, xc, first, active, dgelu, gsec, gsh, low, q, k, v, mix, attn, gram, rs, stat, gstat,
      wt, wp, gains, offs, taps, scales, gin, gout, tri_e.swapaxes(1, 2), map_e, mo_part,
      tri_f.T, map_f.T, exp_f.T, con_f.T, vec2, inb)

    steps = 2

    def cut(n, m):
        return pl.BlockSpec((n // steps, m), lambda i: (i, 0))

    def cut3(n, m):
        return pl.BlockSpec((1, n // steps, m), lambda i: (0, i, 0))

    wide = lambda x: x.reshape(-1, LANES)
    mats = [cut(cols, width), cut(part, width), cut(width, half), cut(half, width)]
    small_specs = vecs + [whole(2 * cols // LANES, LANES), whole(1, heads), whole(hidden // LANES, LANES)]
    basis_specs = [whole(8, cols), whole(8, width), whole(8, half), whole(8, width)]
    basis_shapes = [sds((8, cols)), sds((8, width)), sds((8, half)), sds((8, width))]
    small_shapes = [sds((4, width)), sds((7, width)), sds((18, width)), sds((3, width)), sds((2 * cols // LANES, LANES)), sds((1, heads)), sds((hidden // LANES, LANES))]
    mat_shapes = [sds((cols, width)), sds((part, width)), sds((width, half)), sds((half, width))]
    res = pl.pallas_call(
        functools.partial(update_kernel, share=1.0 / (far * NEAR)),
        grid=(steps,),
        out_shape=mat_shapes * 2
        + [sds((1, cols, width)), sds((1, part, width)), sds((1, width, half)), sds((1, half, width))]
        + small_shapes * 2 + basis_shapes + [sds((rows, width), bf16)] * 2,
        in_specs=[vm] * 13 + mats * 2 + [vm, cut(rows, width), vm] + small_specs * 2,
        out_specs=mats * 2
        + [cut3(cols, width), cut3(part, width), cut3(width, half), cut3(half, width)]
        + small_specs * 2 + basis_specs + [cut(rows, width)] * 2,
        compiler_params=params(30),
        name="update",
    )(oq, op, oi, oo, rqs, rp, ri, ro, rq, mq, mp, mi, mo, tri.T, mapw, expw, conw, tri_v.T, map_v, exp_v, con_v,
      vec, block_out, input_grad, gains, offs, taps, scales, wide(tri_b), sharp.reshape(1, heads), wide(exp_b),
      gains_v, offs_v, taps_v, scales_v, wide(tri_b_v), sharp_v.reshape(1, heads), wide(exp_b_v))
    nw, nv, ne, sv, smo, nt = res[0:4], res[4:8], res[8:12], res[12:19], res[19:26], res[26:30]
    block_out, input_grad = res[30:32]
    nw, nv = [nw[0].T, *nw[1:]], [nv[0].T, *nv[1:]]
    ne = [ne[0].swapaxes(1, 2), *ne[1:]]
    nt = [x.T for x in nt]

    def small(x):
        g, o, t_, s, b, sh, bi_ = x
        return (b.reshape(-1), sh.reshape(-1), bi_.reshape(-1), g, o, t_, s)

    return (
        (block_out, input_grad) + tuple(nw) + small(sv) + tuple(nv) + small(smo) + tuple(ne) + tuple(nt)
    )


def solution(mesh):
    rows = P(("dp", "tensor"), None)
    col, row = P(None, "tensor"), P("tensor", None)
    rep = P()
    err = (P("dp", None, "tensor"), P("dp", "tensor", None), P("dp", None, "tensor"), P("dp", "tensor", None))
    mats = (col, row, col, row)
    in_specs = (
        (rows, P("dp"), rows, col, rep, rep, row, col, rep, row, rep, rep, rep, rep)
        + mats + (rep,) * 7 + err + (row, rep, row, rep)
    )
    out_specs = (rows, rows) + mats + (rep,) * 7 + mats + (rep,) * 7 + err + (row, rep, row, rep)
    return jax.shard_map(body, mesh=mesh, in_specs=in_specs, out_specs=out_specs, check_vma=False)
```

```python
import jax
import jax.numpy as jnp
from jax import lax
from jax.experimental import pallas as pl
from jax.experimental.pallas import tpu as pltpu
from jax.sharding import PartitionSpec as P

SIDE = 24
GROUPS = 8
TRIO = 3
LANES = 128
NEAR = 4
learn_rate = 0.02
momentum_decay = 0.9
f32 = jnp.float32
bf16 = jnp.bfloat16
MESH = pl.DeviceIdType.MESH
HALF_ROOT = 0.7071067811865476
GAUSS = 0.3989422804014327


def sds(shape, dtype=f32):
    return jax.ShapeDtypeStruct(shape, dtype)


def params(mib, **kw):
    return pltpu.CompilerParams(vmem_limit_bytes=mib << 20, **kw)


def held(shape, dtype=f32):
    return pltpu.VMEM(shape, dtype)


def dg(a, b, ca, cb):
    return lax.dot_general(
        a, b, (((ca,), (cb,)), ((), ())), preferred_element_type=f32
    )


def thin(a, m, cb):
    pieces = jnp.concatenate([x.astype(f32) for x in split3(a)], 0).astype(bf16)
    hi, lo = split2(m)
    total = dg(pieces, hi, 1, cb) + dg(pieces, lo, 1, cb)
    rows = a.shape[0]
    return total[0:rows] + total[rows : 2 * rows] + total[2 * rows :]


def cat3(m):
    return jnp.concatenate([m, m, m], -1)


def split2(x):
    hi = x.astype(bf16)
    return hi, (x - hi.astype(f32)).astype(bf16)


def split3(x):
    hi = x.astype(bf16)
    rest = x - hi.astype(f32)
    mid = rest.astype(bf16)
    return hi, mid, (rest - mid.astype(f32)).astype(bf16)


def dg2(a, b, ca, cb):
    hi, lo = split2(a)
    return dg(hi, b, ca, cb) + dg(lo, b, ca, cb)


def mean_of(x):
    return jnp.sum(x, -1, keepdims=True) * (1.0 / x.shape[-1])


def layer_stats(x):
    center = x - mean_of(x)
    scale = lax.rsqrt(mean_of(center * center) + 1e-06)
    return center * scale, scale


def norm_back(grad_out, normed, scale, gain):
    grad_normed = grad_out * gain
    return scale * (
        grad_normed - mean_of(grad_normed) - normed * mean_of(grad_normed * normed)
    )


def colsum(x):
    return jnp.sum(x.reshape(x.shape[0] // 8, 8, x.shape[1]), 0)


def rowsum(x):
    return jnp.sum(x, 0, keepdims=True)


def gelu_pair(x):
    phi = 0.5 + 0.5 * lax.erf(x * HALF_ROOT)
    return x * phi, phi + x * jnp.exp(-0.5 * x * x) * GAUSS


def side_of(cls_ref, index):
    bucket = cls_ref[index]
    return SIDE * (7 + 2 * bucket + lax.div(bucket, 2)) // 12


def fill_mask(mask, side):
    shape = (SIDE, GROUPS, LANES)
    col = lax.broadcasted_iota(jnp.int32, shape, 0)
    group = lax.broadcasted_iota(jnp.int32, shape, 1)
    for m in range(TRIO):
        inside = (group * TRIO + m < side) & (col < side)
        mask[pl.ds(m * SIDE, SIDE)] = jnp.where(inside, 1.0, 0.0).astype(f32)


def to_canvas(src, nat, dst):
    per = TRIO * SIDE
    for l in range(3):
        nat[l] = src[:, l * LANES : (l + 1) * LANES].astype(f32)
    for j in range(per):
        for l in range(3):
            dst[pl.ds(j * 8, 8), l * LANES : (l + 1) * LANES] = nat[
                l, pl.ds(j, GROUPS, stride=per), :
            ]


def from_canvas(value, nat, dst):
    per = TRIO * SIDE
    for j in range(per):
        for l in range(3):
            nat[l, pl.ds(j, GROUPS, stride=per), :] = value[
                j * 8 : j * 8 + 8, l * LANES : (l + 1) * LANES
            ]
    for l in range(3):
        dst[:, l * LANES : (l + 1) * LANES] = nat[l].astype(bf16)


def clear_edges(field):
    zero = jnp.zeros((TRIO + 2, 1, GROUPS, field.shape[-1]), f32)
    field[:, 0:1] = zero
    field[:, SIDE + 1 : SIDE + 2] = zero


def put_field(field, value):
    v = value.reshape(TRIO, SIDE, GROUPS, value.shape[-1])
    group = lax.broadcasted_iota(jnp.int32, (SIDE, GROUPS, value.shape[-1]), 1)
    field[1 : TRIO + 1, 1 : SIDE + 1] = v
    field[0, 1 : SIDE + 1] = jnp.where(group == 0, 0.0, pltpu.roll(v[TRIO - 1], 1, 1))
    field[TRIO + 1, 1 : SIDE + 1] = jnp.where(
        group == GROUPS - 1, 0.0, pltpu.roll(v[0], GROUPS - 1, 1)
    )


def conv_chunk(win, weights, width, flip):
    total = None
    for a in range(3):
        for b in range(3):
            ra, rb = (2 - a, 2 - b) if flip else (a, b)
            term = weights[3 * a + b] * win[ra : ra + TRIO, rb : rb + width]
            total = term if total is None else total + term
    return total


def tap_rows(taps, first, lanes):
    return [
        jnp.broadcast_to(taps[first + k : first + k + 1, lanes], (GROUPS, LANES)) for k in range(9)
    ]


CHUNK = 6


def chunk_rows(m, c0):
    return pl.ds(pl.multiple_of((m * SIDE + c0) * 8, 16), CHUNK * 8), pl.ds(m * SIDE + c0, CHUNK)


def near_partner(me, hi, k):
    index = lax.rem(me + k, 2 * NEAR)
    return index, {"dp": hi * NEAR + lax.div(index, 2), "tensor": lax.rem(index, 2)}


def place():
    dp = lax.axis_index("dp")
    t = lax.axis_index("tensor")
    hi = lax.div(dp, NEAR)
    lo = lax.rem(dp, NEAR)
    return hi, lo, t, lo * 2 + t


def greet(far):
    hi, lo, t, me = place()
    barrier = pltpu.get_barrier_semaphore()
    for k in range(1, 2 * NEAR):
        pl.semaphore_signal(
            barrier, inc=1, device_id=near_partner(me, hi, k)[1], device_id_type=MESH
        )
    for k in range(1, far):
        there = {"dp": lax.rem(hi + k, far) * NEAR + lo, "tensor": t}
        pl.semaphore_signal(barrier, inc=1, device_id=there, device_id_type=MESH)


def met(far):
    pl.semaphore_wait(pltpu.get_barrier_semaphore(), 2 * NEAR - 1 + far - 1)


def remote(src, dst, send, recv, there):
    return pltpu.make_async_remote_copy(
        src_ref=src, dst_ref=dst, send_sem=send, recv_sem=recv, device_id=there, device_id_type=MESH
    )


def far_partner(hi, lo, t, k, far):
    index = lax.rem(hi + k, far)
    return index, {"dp": index * NEAR + lo, "tensor": t}


def all_partners():
    n = lax.axis_size("dp") * 2
    me = lax.axis_index("dp") * 2 + lax.axis_index("tensor")
    out = []
    for k in range(1, n):
        index = lax.rem(me + k, n)
        out.append((index, {"dp": lax.div(index, 2), "tensor": lax.rem(index, 2)}))
    return me, out


def greet_all():
    barrier = pltpu.get_barrier_semaphore()
    for _, there in all_partners()[1]:
        pl.semaphore_signal(barrier, inc=1, device_id=there, device_id_type=MESH)


def met_all():
    pl.semaphore_wait(pltpu.get_barrier_semaphore(), lax.axis_size("dp") * 2 - 1)


def send_tile(tile, slots, sends, recvs):
    me, partners = all_partners()
    for k, (_, there) in enumerate(partners):
        remote(tile, slots.at[me], sends.at[k], recvs.at[me], there).start()
    slots[me] = tile[...]


def sum_tiles(tile, slots, sends, recvs):
    me, partners = all_partners()
    for k, (index, there) in enumerate(partners):
        remote(tile, slots.at[index], sends.at[k], recvs.at[index], there).wait_recv()
    total = jnp.sum(slots[...], 0)
    for k, (index, there) in enumerate(partners):
        remote(tile, slots.at[index], sends.at[k], recvs.at[index], there).wait_send()
    return total


def fill_perm(perm, heads, head):
    shape = (head, perm.shape[1])
    row = lax.broadcasted_iota(jnp.int32, shape, 0)
    lane = lax.broadcasted_iota(jnp.int32, shape, 1)
    for j in range(3):
        for h in range(heads):
            at = (j * heads + h) * head
            perm[at : at + head, :] = jnp.where(lane == row + (3 * h + j) * head, 1.0, 0.0).astype(bf16)


def windows(x):
    return x[:, 0 : 2 * LANES], x[:, LANES : 3 * LANES]


def merge(a, b):
    return jnp.concatenate([a[:, :LANES], a[:, LANES:] + b[:, :LANES], b[:, LANES:]], -1)


def head_spots(heads, head):
    return [(2 * h // heads, h * head - LANES * (2 * h // heads)) for h in range(heads)]


def batch_stats(st):
    row = lambda r: jnp.concatenate([st[r : r + 1, :], st[r + 1 : r + 2, :], st[r + 2 : r + 3, :]], -1)
    inv = cat3(1.0 / st[6:7, :])
    mean = row(0) * inv
    var = row(3) * inv - mean * mean
    return mean, lax.rsqrt(var + 1e-05), inv


def first_kernel(
    cls, sharp, tok_h, tri, mapw, tri_b, gains, offs, taps, scales, expw, conw, loss,
    first_h, active_h, dgelu_h, low_h, q_h, k_h, v_h, mix_h, xc_h, attn_h, gram_h, rs_o, stat_o, lc_h,
    wt_o, wp_o, win_o, wout_o,
    nat, mask, xm, field, sharp_rows, in_block, sums, wt, wp, win, wout, fexp, fcon, floss, tok, masks, perm, bq,
    first_s, active_s, dgelu_s, low_s, q_s, k_s, v_s, mix_s, xc_s, attn_s, gram_s, lc_s, tile, slots,
    osem, lsem, wsend, wrecv, sends, recvs,
):
    i = pl.program_id(0)
    t = lax.axis_index("tensor")
    own = cls.shape[0] // 2
    heads = sharp.shape[0]
    width = tok.shape[1]
    cells = tok.shape[0] // own
    head = width // heads
    other = {"tensor": 1 - t}
    spots = [wt.at[0], wt.at[1], wt.at[2], wp, win, wout]

    def out_copy(n):
        ref = spots[n]
        return remote(ref.at[t], ref.at[t], wsend.at[n], wrecv.at[n], other)

    def in_copy(n):
        ref = spots[n]
        return remote(ref.at[1 - t], ref.at[1 - t], wsend.at[n], wrecv.at[n], other)

    here = pl.ds(pl.multiple_of(i * cells, 16), cells)
    images = [(first_s, first_h), (active_s, active_h), (dgelu_s, dgelu_h), (low_s, low_h), (q_s, q_h), (k_s, k_h),
              (v_s, v_h), (mix_s, mix_h), (xc_s, xc_h)]
    squares = [(attn_s, attn_h), (gram_s, gram_h)]

    def image_outs(n):
        rows = pl.ds(n * cells if isinstance(n, int) else pl.multiple_of(n * cells, 16), cells)
        copies = [pltpu.make_async_copy(a.at[rows], b.at[rows], osem.at[k, n]) for k, (a, b) in enumerate(images)]
        return copies + [
            pltpu.make_async_copy(a.at[n], b.at[n], osem.at[len(images) + k, n]) for k, (a, b) in enumerate(squares)
        ]

    first_o, active_o, dgelu_o, low_o, q_o, k_o, v_o, mix_o, xc_o = [a.at[here] for a, _ in images]
    loads = [
        pltpu.make_async_copy(expw, fexp, lsem.at[0]),
        pltpu.make_async_copy(conw, fcon, lsem.at[1]),
        pltpu.make_async_copy(loss, floss, lsem.at[2]),
        pltpu.make_async_copy(tok_h, tok, lsem.at[3]),
    ]

    @pl.when(i == 0)
    def _():
        loads[3].start()
        greet_all()
        for c in loads[:3]:
            c.start()
        fill_perm(perm, heads // 2, head)
        turned = dg(perm[...], tri[...].astype(bf16), 1, 0).astype(bf16)
        part = turned.shape[0] // 3
        bias = jnp.concatenate([tri_b[n : n + 1, :] for n in range(tri_b.shape[0])], -1)
        pieces = jnp.concatenate([x.astype(f32) for x in split3(jnp.broadcast_to(bias, (8, bias.shape[1])))], 0)
        pieces = pieces.astype(bf16)
        sides = []
        for hf in range(2):
            turned_b = dg(pieces[:, hf * 3 * part : (hf + 1) * 3 * part], perm[...], 1, 1)
            sides.append(turned_b[0:1] + turned_b[8:9] + turned_b[16:17])
        for j in range(3):
            bq[j : j + 1, :] = jnp.concatenate([side[:, j * part : (j + 1) * part] for side in sides], -1)
        for j in range(3):
            wt[j, t] = turned[j * part : (j + 1) * part]
        wp[t] = mapw[...].astype(bf16)
        lane = lax.broadcasted_iota(jnp.int32, (head, 2 * LANES), 1)
        sharp_rows[...] = jnp.zeros_like(sharp_rows)
        in_block[...] = jnp.zeros_like(in_block)
        for h, (w, r) in enumerate(head_spots(heads, head)):
            inside = (lane >= r) & (lane < r + head)
            sharp_rows[w, r : r + head, :] = jnp.where(inside, sharp[h], 0.0)
            in_block[w, r : r + head, :] = jnp.where(inside, 1.0, 0.0)
        clear_edges(field)
        sums[...] = jnp.zeros_like(sums)
        loads[0].wait()
        loads[1].wait()
        win[t] = fexp[...].astype(bf16)
        wout[t] = fcon[...].astype(bf16)

    fill_mask(mask, side_of(cls, t * own + i))
    mk = cat3(mask[...].reshape(-1, LANES))

    @pl.when(i == 0)
    def _():
        loads[3].wait()

        @pl.loop(0, own)
        def _(n):
            rows = pl.ds(pl.multiple_of(n * cells, 16), cells)
            fill_mask(masks, side_of(cls, t * own + n))
            inside = cat3(masks[...].reshape(-1, LANES))
            to_canvas(tok.at[rows], nat, xm)
            x = xm[...] * inside
            xc_s[rows, :] = x.astype(bf16)
            normed, _ = layer_stats(x)
            low_s[rows, :] = ((normed * gains[0:1, :] + offs[0:1, :]) * inside).astype(bf16)

        met_all()
        for n in range(4):
            out_copy(n).start()
        for n in range(4):
            in_copy(n).wait_recv()
        for n in range(4, 6):
            out_copy(n).start()

    low = low_o[...]
    lows = []
    projected = dg(low, wt[...].reshape(3 * width, width), 1, 1)
    for j in range(2):
        value = (projected[:, j * width : (j + 1) * width] + bq[j : j + 1, :]) * mk
        scale = lax.rsqrt(rowsum(value * value) + 1e-06)
        rs_o[0, j : j + 1, :] = scale
        unit = (value * scale).astype(bf16)
        (q_o, k_o)[j][...] = unit
        lows.append(windows(unit))
    value_low = ((projected[:, 2 * width :] + bq[2:3, :]) * mk).astype(bf16)
    v_o[...] = value_low
    grams = [dg(lows[0][w], lows[1][w], 0, 0) for w in range(2)]
    gram = jnp.stack(grams)
    gram_s[i] = gram
    inside = in_block[...]
    logits = jnp.where(inside > 0.0, gram * sharp_rows[...], -1e30)
    powers = jnp.exp(logits - jnp.max(logits, -1, keepdims=True)) * inside
    attn = powers / jnp.maximum(jnp.sum(powers, -1, keepdims=True), 0.5)
    attn_s[i] = attn
    parts = [dg(windows(value_low)[w], attn[w].astype(bf16), 1, 1) for w in range(2)]
    mixed = merge(*parts).astype(bf16)
    mix_o[...] = mixed
    branch = dg(mixed, wp[...].reshape(width, width), 1, 0) + offs[4:5, :]
    first = xc_o[...].astype(f32) + scales[0:1, :] * branch * mk
    first_o[...] = first
    normed, _ = layer_stats(first)
    put_field(field, (normed * gains[1:2, :] + offs[1:2, :]) * mk)
    for l in range(3):
        lanes = slice(l * LANES, (l + 1) * LANES)
        w = tap_rows(taps, 0, lanes)
        tot = jnp.zeros((8, LANES), f32)
        sq = jnp.zeros((8, LANES), f32)

        def step(n, carry):
            tot, sq = carry
            c0 = n * CHUNK
            conv = conv_chunk(field[:, pl.ds(c0, CHUNK + 2), :, lanes], w, CHUNK, False)
            act, back = gelu_pair(conv)
            for m in range(TRIO):
                rows, cells8 = chunk_rows(m, c0)
                am = act[m] * mask[cells8]
                active_o[rows, lanes] = am.reshape(CHUNK * 8, LANES)
                dgelu_o[rows, lanes] = back[m].reshape(CHUNK * 8, LANES)
                tot = tot + jnp.sum(am, 0)
                sq = sq + jnp.sum(am * am, 0)
            return tot, sq

        tot, sq = lax.fori_loop(0, SIDE // CHUNK, step, (tot, sq))
        sums[0, :, lanes] += tot
        sums[1, :, lanes] += sq
    for c in image_outs(i):
        c.start()

    @pl.when(i == own - 1)
    def _():
        cells_in = 0
        for n in range(own):
            s = side_of(cls, t * own + n)
            cells_in = cells_in + s * s
        for k in range(2):
            row = rowsum(sums[k])
            for l in range(3):
                tile[3 * k + l : 3 * k + l + 1, :] = row[:, l * LANES : (l + 1) * LANES]
        tile[6:8, :] = jnp.full((2, LANES), 1.0, f32) * cells_in.astype(f32)
        send_tile(tile, slots, sends, recvs)
        loads[2].wait()

        @pl.loop(0, own)
        def _(n):
            rows = pl.ds(pl.multiple_of(n * cells, 16), cells)
            fill_mask(masks, side_of(cls, t * own + n))
            to_canvas(floss.at[rows], nat, xm)
            lc_s[rows, :] = (xm[...] * cat3(masks[...].reshape(-1, LANES))).astype(bf16)

        for n in range(4, 6):
            in_copy(n).wait_recv()
        for n in range(6):
            out_copy(n).wait_send()
        stores = [
            pltpu.make_async_copy(src, dst, lsem.at[n])
            for n, (src, dst) in enumerate(
                ((wt, wt_o), (wp, wp_o), (win, win_o), (wout, wout_o), (lc_s, lc_h))
            )
        ]
        for c in stores:
            c.start()
        stat_o[...] = sum_tiles(tile, slots, sends, recvs)
        for c in stores:
            c.wait()
        for n in range(own):
            for c in image_outs(n):
                c.wait()


def middle_kernel(
    cls, first, active, lc, st, win_h, wout_h, bin_, gains, offs, taps, scales, ei, eo,
    out_h, gsec_h, gsh_h, gin_h, gout_h, mo_h, vec_o, inb_o, stat_o, st_o,
    nat, mask, field, gfield, loc, nrm, scl, macc, gacc, l3s, gms, hs, gs, acc, inb, win, wout, out_s, gsec_s, gsh_s, gin_o, gout_o, ein, eout, osem, gsem, wsem, tile, slots, sends, recvs,
):
    i = pl.program_id(0)
    t = lax.axis_index("tensor")
    own = cls.shape[0] // 2
    held = [pltpu.make_async_copy(win_h, win, wsem.at[0]), pltpu.make_async_copy(wout_h, wout, wsem.at[1])]
    errors = [pltpu.make_async_copy(ei.at[0], ein, wsem.at[2]), pltpu.make_async_copy(eo.at[0], eout, wsem.at[3])]
    rows_n = first.shape[0]
    base = pl.multiple_of(i * rows_n, 16)
    images = [(out_s, out_h), (gsec_s, gsec_h), (gsh_s, gsh_h)]

    def image_outs(n):
        rows = pl.ds(n * rows_n if isinstance(n, int) else pl.multiple_of(n * rows_n, 16), rows_n)
        return [pltpu.make_async_copy(a.at[rows], b.at[rows], osem.at[k, n]) for k, (a, b) in enumerate(images)]

    out_o, gsec_o, gsh_o = [a.at[pl.ds(base, rows_n)] for a, _ in images]
    hidden = win.shape[0] * win.shape[2]
    half = win.shape[2]

    @pl.when(i == 0)
    def _():
        greet_all()
        for c in held + errors:
            c.start()
        clear_edges(field)
        clear_edges(gfield)
        acc[...] = jnp.zeros_like(acc)
        inb[...] = jnp.zeros_like(inb)

    fill_mask(mask, side_of(cls, t * own + i))
    mk = cat3(mask[...].reshape(-1, LANES))
    mean, rstd, _ = batch_stats(st)
    zhat = (active[...] - mean) * rstd
    put_field(field, (zhat * gains[2:3, :] + offs[2:3, :]) * mk)
    for l in range(3):
        lanes = slice(l * LANES, (l + 1) * LANES)
        w = tap_rows(taps, 9, lanes)
        bias = offs[5:6, lanes]

        def step(n, carry):
            c0 = n * CHUNK
            conv = conv_chunk(field[:, pl.ds(c0, CHUNK + 2), :, lanes], w, CHUNK, False)
            for m in range(TRIO):
                rows, cells8 = chunk_rows(m, c0)
                loc[rows, lanes] = ((conv[m] + bias) * mask[cells8]).reshape(CHUNK * 8, LANES)
            return carry

        lax.fori_loop(0, SIDE // CHUNK, step, 0)
    second = first[...] + scales[1:2, :] * loc[...]
    normed, scale = layer_stats(second)
    nrm[...] = normed
    scl[...] = jnp.broadcast_to(scale, scl.shape)
    l3 = ((normed * gains[3:4, :] + offs[3:4, :]) * mk).astype(bf16)
    l3s[pl.ds(base, rows_n), :] = l3
    gm = (lc[...].astype(f32) * scales[2:3, :]).astype(bf16)
    gms[pl.ds(base, rows_n), :] = gm
    acc[3] += colsum(gm.astype(f32))

    @pl.when(i == 0)
    def _():
        for c in held:
            c.wait()

    step = half
    m_parts, g_parts = [], []
    for n in range(hidden // step):
        hf, cols = n * step // half, slice(n * step % half, n * step % half + step)
        allc = slice(n * step, (n + 1) * step)
        pre = dg(l3s[pl.ds(base, rows_n), :], win[hf, :, cols], 1, 0) + jnp.concatenate(
            [bin_[r : r + 1, :] for r in range(n * step // LANES, (n + 1) * step // LANES)], -1
        )
        act, back = gelu_pair(pre)
        h = act.astype(bf16)
        hs[pl.ds(base, rows_n), allc] = h
        g = (dg(gms[pl.ds(base, rows_n), :], wout[hf, cols, :], 1, 1) * back).astype(bf16)
        gs[pl.ds(base, rows_n), allc] = g
        inb[:, allc] += colsum(g.astype(f32))
        m_parts.append(dg(h, wout[hf, cols, :], 1, 0))
        g_parts.append(dg(g, win[hf, :, cols], 1, 1))
    macc[...] = sum(m_parts[1:], m_parts[0])
    gacc[...] = sum(g_parts[1:], g_parts[0])

    mlp = macc[...] + offs[6:7, :]
    second = first[...] + scales[1:2, :] * loc[...]
    from_canvas(second + scales[2:3, :] * mlp * mk, nat, out_o)
    acc[5] += colsum(lc[...].astype(f32) * mlp)
    normed, scale = nrm[...], cat3(scl[...])
    dout = gacc[...]
    acc[0] += colsum(dout)
    acc[1] += colsum(dout * normed)
    gsec = lc[...].astype(f32) + norm_back(dout, normed, scale, gains[3:4, :])
    gsec_o[...] = gsec
    acc[4] += colsum(gsec * loc[...])
    glocal = gsec * scales[1:2, :]
    acc[2] += colsum(glocal)
    put_field(gfield, glocal)
    for l in range(3):
        lanes = slice(l * LANES, (l + 1) * LANES)
        w = tap_rows(taps, 9, lanes)
        tot = jnp.zeros((8, LANES), f32)
        cross = jnp.zeros((8, LANES), f32)
        tap_sum = [jnp.zeros((8, LANES), f32) for _ in range(9)]

        def step(n, carry):
            tot, cross, tap_sum = carry[0], carry[1], list(carry[2:])
            c0 = n * CHUNK
            gwin = gfield[:, pl.ds(c0, CHUNK + 2), :, lanes]
            fwin = field[:, pl.ds(c0, CHUNK + 2), :, lanes]
            conv = conv_chunk(gwin, w, CHUNK, True)
            center = gwin[1 : 1 + TRIO, 1 : 1 + CHUNK]
            for a in range(3):
                for b in range(3):
                    prod = fwin[a : a + TRIO, b : b + CHUNK] * center
                    tap_sum[3 * a + b] += jnp.sum(prod, (0, 1))
            for m in range(TRIO):
                rows, cells8 = chunk_rows(m, c0)
                value = conv[m] * mask[cells8]
                flat = value.reshape(CHUNK * 8, LANES)
                gsh_o[rows, lanes] = flat
                z = (active[rows, lanes] - mean[:, lanes]) * rstd[:, lanes]
                tot = tot + jnp.sum(value, 0)
                cross = cross + colsum(flat * z)
            return (tot, cross, *tap_sum)

        tot, cross, *tap_sum = lax.fori_loop(0, SIDE // CHUNK, step, (tot, cross, *tap_sum))
        acc[6, :, lanes] += cross
        acc[7, :, lanes] += tot
        for k in range(9):
            acc[8 + k, :, lanes] += tap_sum[k]
    for c in image_outs(i):
        c.start()

    @pl.when(i == own - 1)
    def _():
        st_o[...] = st[...]
        cross, tot = rowsum(acc[6]), rowsum(acc[7])
        for l in range(3):
            lanes = slice(l * LANES, (l + 1) * LANES)
            tile[l : l + 1, :] = tot[:, lanes]
            tile[3 + l : 4 + l, :] = cross[:, lanes]
        tile[6:8, :] = jnp.zeros((2, LANES), f32)
        met_all()
        send_tile(tile, slots, sends, recvs)
        vec_o[...] = jnp.zeros_like(vec_o)
        for k in range(17):
            vec_o[k : k + 1, :] = rowsum(acc[k])
        inb_o[...] = jnp.zeros_like(inb_o)
        for k in range(hidden // LANES):
            inb_o[k : k + 1, :] = rowsum(inb[:, k * LANES : (k + 1) * LANES])
        l3_t = l3s[...].T
        gm_t = gms[...].T
        for c in errors:
            c.wait()
        outs = [(gin_o.at[0], gin_h.at[0]), (gin_o.at[1], gin_h.at[1]), (gout_o.at[0], gout_h.at[0]),
                (gout_o.at[1], gout_h.at[1]), (eout, mo_h)]
        outs = [pltpu.make_async_copy(src, dst, gsem.at[n]) for n, (src, dst) in enumerate(outs)]
        for hf in range(2):
            gout_o[hf] = dg(gm_t, hs[:, hf * half : (hf + 1) * half], 1, 0)
            outs[2 + hf].start()
        eout[...] += gout_o[t].T
        outs[4].start()
        for hf in range(2):
            grad = dg(l3_t, gs[:, hf * half : (hf + 1) * half], 1, 0)
            gin_o[hf] = grad + jnp.where(t == hf, ein[...], 0.0)
            outs[hf].start()
        stat_o[...] = sum_tiles(tile, slots, sends, recvs)
        for n in range(own):
            for c in image_outs(n):
                c.wait()
        for c in outs:
            c.wait()


def last_kernel(
    far,
    cls, sharp, tok_h, first, active, dgelu, gsec, gsh, low_h, q, k, v, mix_h, attn, gram, rs,
    st, gst, wt_h, wp_h, gains, offs, taps, scales,
    gin, gout, eq, ep, mo_part, bq, bp, bi, bo, vec2, inb,
    ingrad_o, mq, mp_o, mi, mo, oq_o, op_o, oi_o, oo_o, rq_o, rp_o, ri_o, ro_o, rqs_o, vec_o,
    nat, mask, scl, field, gfield, gfirst, gproj, acc, bias_acc, sharp_rows,
    mp, ai, ao, aq, ap, gt, gp, vec3, qb, obuf, tok, low, mix, wt, wp, perm, bpair, bsem, hsem, lsem, psend, precv,
    *exchange,
):
    lefts, rights, late = Spread(far, *exchange[0:11]), Spread(far, *exchange[11:22]), Spread(far, *exchange[22:33])
    left_qp = Broadcast(far, 0, *exchange[33:41])
    i = pl.program_id(0)
    t = lax.axis_index("tensor")
    own = cls.shape[0] // 2
    heads = sharp.shape[0]
    width = tok.shape[1]
    cells = tok.shape[0] // own
    head = width // heads
    other = {"tensor": 1 - t}
    part = width // 2
    cols_q = bq.shape[1]
    tiles_q = -(-cols_q // LANES)
    right_qp = Broadcast(far, tiles_q, *exchange[41:49])
    base = pl.multiple_of(i * cells, 16)
    here = pl.ds(base, cells)
    own_rows = pl.ds(pl.multiple_of(t * part, 8), part)
    loads = [
        pltpu.make_async_copy(src, dst, lsem.at[n])
        for n, (src, dst) in enumerate(
            ((gin.at[t], mi), (mo_part, mo), (eq.at[0], mq), (ep.at[0], mp_o))
        )
    ]
    held = [
        pltpu.make_async_copy(src, dst, hsem.at[n])
        for n, (src, dst) in enumerate(
            ((tok_h, tok), (wp_h, wp), (low_h, low), (mix_h, mix), (wt_h, wt))
        )
    ]
    pair_in = [remote(gin.at[1 - t], ai, psend.at[0], precv.at[0], other), remote(gout.at[1 - t], ao, psend.at[1], precv.at[1], other)]
    pair_qp = [remote(gt.at[j, 1 - t], aq.at[j], psend.at[2 + j], precv.at[2 + j], other) for j in range(3)]
    pair_qp.append(remote(gp.at[1 - t], ap, psend.at[5], precv.at[5], other))
    @pl.when(i == 0)
    def _():
        greet(far)
        for c in held + loads:
            c.start()
        fill_perm(perm, heads // 2, head)
        pieces = jnp.concatenate([x.astype(f32) for x in split3(bq[...])], 0).astype(bf16)
        turned = dg(pieces, perm[...], 1, 1)
        bpair[t] = turned[0:8] + turned[8:16] + turned[16:24]
        gt[...] = jnp.zeros_like(gt)
        gp[...] = jnp.zeros_like(gp)
        gproj[0:cells] = jnp.zeros((cells, gproj.shape[1]), bf16)
        ingrad_o[0:cells] = jnp.zeros((cells, width), bf16)
        mp[...] = jnp.zeros_like(mp)
        lefts.pay[...] = jnp.zeros_like(lefts.pay)
        rights.pay[...] = jnp.zeros_like(rights.pay)
        vec3[...] = jnp.zeros_like(vec3)
        qb[...] = jnp.zeros_like(qb)
        right_qp.x[...] = jnp.zeros_like(right_qp.x)
        sharp_rows[...] = jnp.zeros_like(sharp_rows)
        for h, (w, r) in enumerate(head_spots(heads, head)):
            sharp_rows[w, r : r + head, :] = jnp.full((head, 2 * LANES), 1.0, f32) * sharp[h]
        clear_edges(field)
        clear_edges(gfield)
        acc[...] = jnp.zeros_like(acc)
        bias_acc[...] = jnp.zeros_like(bias_acc)

    fill_mask(mask, side_of(cls, t * own + i))
    mk = cat3(mask[...].reshape(-1, LANES))
    mean, rstd, inv = batch_stats(st)
    gsum = lambda r: jnp.concatenate([gst[r : r + 1, :], gst[r + 1 : r + 2, :], gst[r + 2 : r + 3, :]], -1)
    gain_bn = gains[2:3, :]
    zhat = (active[...] - mean) * rstd
    gact = rstd * (gsh[...] * gain_bn - gsum(0) * gain_bn * inv - zhat * (gsum(3) * gain_bn * inv)) * mk
    put_field(gfield, gact * dgelu[...])
    normed, scale = layer_stats(first[...])
    gfirst[here, :] = normed
    scl[...] = jnp.broadcast_to(scale, scl.shape)
    put_field(field, (normed * gains[1:2, :] + offs[1:2, :]) * mk)
    for l in range(3):
        lanes = slice(l * LANES, (l + 1) * LANES)
        w = tap_rows(taps, 0, lanes)
        tap_sum = [jnp.zeros((8, LANES), f32) for _ in range(9)]

        def step(n, carry):
            tap_sum = list(carry)
            c0 = n * CHUNK
            gwin = gfield[:, pl.ds(c0, CHUNK + 2), :, lanes]
            fwin = field[:, pl.ds(c0, CHUNK + 2), :, lanes]
            conv = conv_chunk(gwin, w, CHUNK, True)
            center = gwin[1 : 1 + TRIO, 1 : 1 + CHUNK]
            for a in range(3):
                for b in range(3):
                    prod = fwin[a : a + TRIO, b : b + CHUNK] * center
                    tap_sum[3 * a + b] += jnp.sum(prod, (0, 1))
            for m in range(TRIO):
                rows, cells8 = chunk_rows(m, c0)
                nat[l, rows, :] = (conv[m] * mask[cells8]).reshape(CHUNK * 8, LANES)
            return tuple(tap_sum)

        tap_sum = lax.fori_loop(0, SIDE // CHUNK, step, tuple(tap_sum))
        for n in range(9):
            acc[7 + n, :, lanes] += tap_sum[n]

    @pl.when(i == 0)
    def _():
        met(far)
        for c in pair_in:
            c.start()
        remote(bpair.at[t], bpair.at[t], bsem.at[0], bsem.at[1], other).start()
        for c in held:
            c.wait()

    @pl.when(i == own - 2)
    def _():
        for c in loads:
            c.wait()
        for c in pair_in:
            c.wait()
        remote(bpair.at[t], bpair.at[t], bsem.at[0], bsem.at[1], other).wait_send()
        remote(bpair.at[1 - t], bpair.at[1 - t], bsem.at[0], bsem.at[1], other).wait_recv()
        mp[own_rows, :] = mp_o[...]
        for m, tile in enumerate(tiles(thin(bq[...], mq[...], 0)) + tiles(thin(bp[...], mp[...], 1))):
            left_qp.x[m] = tile
        mi[...] += ai[...]
        mo[...] += ao[...].T
        li = tiles(thin(bi[...], mi[...], 1))
        lo = tiles(thin(bo[...], mo[...], 1))
        n = 0
        for tile in li:
            lefts.pay[n] = tile
            n += 1
        for m, tile in enumerate(lo):
            lefts.pay[n + t * len(lo) + m] = tile
        n += 2 * len(lo)
        for tile in row_tiles(vec2) + row_tiles(inb):
            lefts.pay[n] = tile
            n += 1
        lefts.start()

    @pl.when(i == own - 1)
    def _():
        lefts.gather()

    before = pl.ds(pl.multiple_of(jnp.maximum(i - 1, 0) * cells, 16), cells)
    gt[...] += dg(gproj[before, :], low[before, :], 0, 0).reshape(3, 2, part, width)
    gp[...] += dg(mix[before, :], ingrad_o[before, :], 0, 0).reshape(2, part, width)
    dout = jnp.concatenate([nat[0], nat[1], nat[2]], -1)
    normed, scale = gfirst[here, :], cat3(scl[...])
    acc[2] += colsum(dout * normed)
    acc[3] += colsum(dout)
    grad = gsec[...] + norm_back(dout, normed, scale, gains[1:2, :])
    gfirst[here, :] = grad
    acc[5] += colsum(grad * (first[...] - tok[here, :].astype(f32)))
    gal = (grad * scales[0:1, :]).astype(bf16)
    acc[4] += colsum(gal.astype(f32))
    ingrad_o[here, :] = gal
    gmix, gmix_lo = split2(dg(gal, wp[...], 1, 1))
    lane1 = lax.broadcasted_iota(jnp.int32, (1, width), 1)
    sharp_lane = jnp.zeros((1, width), f32)
    for h in range(heads):
        sharp_lane = jnp.where((lane1 >= h * head) & (lane1 < (h + 1) * head), sharp[h], sharp_lane)
    ones = jnp.ones((8, 2 * LANES), bf16)
    wins = [slice(w * LANES, (w + 2) * LANES) for w in range(2)]
    a = attn[0]
    gattn = jnp.stack([dg(gmix[:, c], v[:, c], 0, 0) + dg(gmix_lo[:, c], v[:, c], 0, 0) for c in wins])
    gval = [dg(gmix[:, c], a[w].astype(bf16), 1, 0) for w, c in enumerate(wins)]
    gsc = a * (gattn - jnp.sum(gattn * a, -1, keepdims=True))
    shi, slo = split2(gsc * sharp_rows[...])
    gqu = [dg(k[:, c], shi[w], 1, 1) + dg(k[:, c], slo[w], 1, 1) for w, c in enumerate(wins)]
    gku = [dg(q[:, c], shi[w], 1, 0) + dg(q[:, c], slo[w], 1, 0) for w, c in enumerate(wins)]
    weighted = gsc * gram[0]
    hi, lo = split2(weighted)
    chan = [dg(ones, hi[w], 1, 1) + dg(ones, lo[w], 1, 1) for w in range(2)]
    chan_k = [rowsum(weighted[w] * sharp_rows[w]) for w in range(2)]
    chan = merge(*chan)[0:1, :]
    acc[6, 0:1, :] += chan
    gq = rs[0, 0:1, :] * (merge(*gqu) - q[...].astype(f32) * (chan * sharp_lane))
    gk = rs[0, 1:2, :] * (merge(*gku) - k[...].astype(f32) * merge(*chan_k))
    for j, piece in enumerate((gq, gk, merge(*gval))):
        small = piece.astype(bf16)
        gproj[here, j * width : (j + 1) * width] = small
        bias_acc[j] += colsum(small.astype(f32))

    @pl.when(i == own - 2)
    def _():
        lefts.middle()

    @pl.when(i == own - 1)
    def _():
        gt[...] += dg(gproj[here, :], low[here, :], 0, 0).reshape(3, 2, part, width)
        for c in pair_qp[:3]:
            c.start()
        gp[...] += dg(mix[here, :], ingrad_o[here, :], 0, 0).reshape(2, part, width)
        pair_qp[3].start()
        thirds = [bpair[hf, :, j * part : (j + 1) * part] for j in range(3) for hf in range(2)]
        left_q = thin(jnp.concatenate(thirds, -1), gt[...].reshape(6 * part, width), 0)
        for m, tile in enumerate(tiles(left_q) + tiles(thin(bp[...], gp[...].reshape(width, width), 1))):
            left_qp.x[m] += tile
        left_qp.start()
        lefts.finish()
        tiles_i = width // LANES
        tiles_o = 2 * mo.shape[0] // LANES
        get = lambda a, b: jnp.concatenate([lefts.full[m] for m in range(a, b)], -1)
        oi, oo = orthonormal([get(0, tiles_i), get(tiles_i, tiles_i + tiles_o)])
        first_vec = tiles_i + tiles_o
        count2, count3 = vec2.shape[0] * 3 // 8, vec3.shape[0] * 3 // 8
        for m in range(count2):
            vec_o[m * 8 : m * 8 + 8, :] = lefts.full[first_vec + m]
        for m in range(2):
            at = (count2 + count3 + m) * 8
            vec_o[at : at + 8, :] = lefts.full[first_vec + count2 + m]
        half_o = mo.shape[0]
        obuf[0] = oo[:, :half_o]
        obuf[1] = oo[:, half_o:]
        oo_own = obuf[t]
        ri = tiles(thin(oi, mi[...], 0))
        ro = tiles(thin(oo_own, mo[...], 0))
        for m, tile in enumerate(ri):
            rights.pay[t * len(ri) + m] = tile
        for m, tile in enumerate(ro):
            rights.pay[2 * len(ri) + m] = tile
        rights.start()

        for c in pair_qp:
            c.wait_recv()
        turned = jnp.concatenate([gt[j, t] + aq[j] for j in range(3)], 0)
        grad_q = None
        for piece in split3(turned):
            term = dg(perm[...], piece, 0, 0)
            grad_q = term if grad_q is None else grad_q + term
        mq[...] += grad_q
        mp_o[...] += gp[t] + ap[...]
        mp[own_rows, :] = mp_o[...]
        def input_dout(n):
            rows = pl.ds(pl.multiple_of(n * cells, 16), cells)
            dout = dg(gproj[rows, :], wt[...].reshape(3 * width, width), 1, 0)
            normed, scale = layer_stats(tok[rows, :].astype(f32))
            return rows, dout, normed, scale

        def input_sums(n):
            _, dout, normed, _ = input_dout(n)
            acc[0] += colsum(dout * normed)
            acc[1] += colsum(dout)

        pl.loop(0, 1)(input_sums)

        def input_out(n):
            rows, dout, normed, scale = input_dout(n)
            result = gfirst[rows, :] + norm_back(dout, normed, scale, gains[0:1, :])
            from_canvas(result, nat, ingrad_o.at[rows])

        left_qp.middle()
        rights.middle()
        pl.loop(1, own)(input_sums)
        for n in range(16):
            vec3[n : n + 1, :] = rowsum(acc[n])
        vec3[5:6, :] = rowsum(acc[5]) / scales[0:1, :]
        third = perm.shape[0] // 3
        lane8 = lax.broadcasted_iota(jnp.int32, (8, width), 1)
        total = None
        for j in range(3):
            rows = perm[j * third : (j + 1) * third, :]
            both = jnp.concatenate([rows, rows], 0)
            pieces = []
            for hf in range(2):
                mine = jnp.where((lane8 >= hf * third) & (lane8 < (hf + 1) * third), bias_acc[j], 0.0)
                pieces += [piece.astype(f32) for piece in split3(mine)]
            term = dg(jnp.concatenate(pieces, 0).astype(bf16), both, 1, 0)
            total = term if total is None else total + term
        row = jnp.concatenate([rowsum(total[0:24]), rowsum(total[24:48])], -1)
        for n in range(row.shape[1] // LANES):
            qb[n : n + 1, :] = row[:, n * LANES : (n + 1) * LANES]
        for m, tile in enumerate(row_tiles(vec3) + row_tiles(qb)):
            late.pay[m] = tile
        late.start()
        pl.loop(0, 1)(input_out)
        rights.gather()
        total = left_qp.finish()
        oq, op = orthonormal(
            [jnp.concatenate([total[m] for m in range(3)], -1), jnp.concatenate([total[m] for m in range(3, 6)], -1)]
        )
        rq = thin(oq, mq[...], 1)
        for m in range(tiles_q):
            wide = min(LANES, cols_q - m * LANES)
            right_qp.x[m, :, 0:wide] = rq[:, m * LANES : m * LANES + wide]
        for m, tile in enumerate(tiles(thin(op, mp[...], 0))):
            right_qp.x[tiles_q + m] = tile
        right_qp.start()
        share = 1.0 / (far * NEAR)
        oq_o[...] = stacked(oq)[1]
        mp[:, 0:48] = stacked(op)[0].T
        op_o[...] = mp[own_rows, 0:48]
        late.middle()
        pl.loop(1, own - 1)(input_out)
        oi_o[...] = stacked(oi)[0].T
        oo_o[...] = stacked(oo_own)[0].T
        right_qp.middle()
        late.gather()
        pl.loop(own - 1, own)(input_out)
        rights.finish()
        for m in range(len(ri)):
            ri_o[:, m * LANES : (m + 1) * LANES] = rights.full[t * len(ri) + m] * share
        for m in range(len(ro)):
            ro_o[:, m * LANES : (m + 1) * LANES] = rights.full[2 * len(ri) + m] * share
        total = right_qp.finish() * share
        for m in range(tiles_q):
            wide = min(LANES, cols_q - m * LANES)
            rq_o[:, m * LANES : m * LANES + wide] = total[m][:, 0:wide]
        for m in range(3):
            rp_o[:, m * LANES : (m + 1) * LANES] = total[tiles_q + m]
        rqs_o[...] = stacked(rq_o[...])[0].T
        late.finish()
        for m in range(count3):
            vec_o[(count2 + m) * 8 : (count2 + m) * 8 + 8, :] = late.full[m]
        for m in range(2):
            at = (count2 + count3 + 2 + m) * 8
            vec_o[at : at + 8, :] = late.full[count3 + m]
        for c in pair_qp:
            c.wait_send()
        for group in (lefts, rights, late, left_qp, right_qp):
            group.drain()


def orthonormal(rows):
    index = lax.broadcasted_iota(jnp.int32, rows[0].shape[:1] + (1,), 0)
    rank = rows[0].shape[0]
    for n in range(rank):
        done = []
        for v in rows:
            column = v[n : n + 1, :]
            dots = jnp.sum(v * column, -1, keepdims=True)
            scale = lax.rsqrt(dots[n : n + 1, :] + 1e-06)
            unit = column * scale
            later = v - (dots * scale) * unit
            done.append(jnp.where(index > n, later, jnp.where(index == n, unit, v)))
        rows = done
    return rows


class Spread:
    def __init__(self, far, pay, slots, part, tops, full, s1, r1, s2, r2, s3, r3):
        self.far, self.pay, self.slots, self.part, self.tops, self.full = far, pay, slots, part, tops, full
        self.sems = s1, r1, s2, r2, s3, r3
        self.per = slots.shape[1]
        self.hi, self.lo, self.t, self.me = place()

    def piece(self, ref, index):
        return ref.at[pl.ds(index * self.per, self.per)]

    def first(self, k, incoming):
        index, there = near_partner(self.me, self.hi, k)
        slot = index if incoming else self.me
        return remote(self.piece(self.pay, index), self.slots.at[slot], self.sems[0].at[k], self.sems[1].at[slot], there)

    def second(self, k, incoming):
        index, there = far_partner(self.hi, self.lo, self.t, k, self.far)
        slot = index if incoming else self.hi
        return remote(self.part, self.tops.at[slot], self.sems[2].at[k], self.sems[3].at[slot], there)

    def third(self, k, incoming):
        index, there = near_partner(self.me, self.hi, k)
        slot = index if incoming else self.me
        return remote(
            self.piece(self.full, self.me), self.piece(self.full, slot), self.sems[4].at[k], self.sems[5].at[slot], there
        )

    def start(self):
        for k in range(1, 2 * NEAR):
            self.first(k, False).start()
        self.slots[self.me] = self.pay[pl.ds(self.me * self.per, self.per)]

    def middle(self):
        for k in range(1, 2 * NEAR):
            self.first(k, True).wait_recv()
        total = jnp.sum(self.slots[...], 0)
        self.part[...] = total
        self.tops[self.hi] = total
        for k in range(1, self.far):
            self.second(k, False).start()

    def gather(self):
        for k in range(1, self.far):
            self.second(k, True).wait_recv()
        self.full[pl.ds(self.me * self.per, self.per)] = jnp.sum(self.tops[...], 0)
        for k in range(1, 2 * NEAR):
            self.third(k, False).start()

    def finish(self):
        for k in range(1, 2 * NEAR):
            self.third(k, True).wait_recv()

    def drain(self):
        for k in range(1, 2 * NEAR):
            self.first(k, False).wait_send()
            self.third(k, False).wait_send()
        for k in range(1, self.far):
            self.second(k, False).wait_send()


def spread_scratch(per, far):
    dma = pltpu.SemaphoreType.DMA
    near = 2 * NEAR
    vm = lambda *shape: pltpu.VMEM(shape + (8, LANES), f32)
    return [
        vm(near * per), vm(near, per), vm(per), vm(far, per), vm(near * per),
        dma((near,)), dma((near,)), dma((far,)), dma((far,)), dma((near,)), dma((near,)),
    ]


class Broadcast:
    def __init__(self, far, own, x, slots, part, tops, s1, r1, s2, r2):
        self.far, self.own, self.x, self.slots, self.part, self.tops = far, own, x, slots, part, tops
        self.sems = s1, r1, s2, r2
        self.hi, self.lo, self.t, self.me = place()

    def first(self, k, incoming):
        index, there = near_partner(self.me, self.hi, k)
        slot = index if incoming else self.me
        skip = self.own if k % 2 else 0
        count = self.x.shape[0] - skip
        return remote(
            self.x.at[pl.ds(skip, count)], self.slots.at[slot, pl.ds(skip, count)],
            self.sems[0].at[k], self.sems[1].at[slot], there,
        )

    def second(self, k, incoming):
        index, there = far_partner(self.hi, self.lo, self.t, k, self.far)
        slot = index if incoming else self.hi
        return remote(self.part, self.tops.at[slot], self.sems[2].at[k], self.sems[3].at[slot], there)

    def start(self):
        for k in range(1, 2 * NEAR):
            self.first(k, False).start()
        self.slots[self.me] = self.x[...]

    def middle(self):
        for k in range(1, 2 * NEAR):
            self.first(k, True).wait_recv()
        own = self.own
        if own:
            total = self.slots[self.t, 0:own]
            for k in range(1, NEAR):
                total = total + self.slots[2 * k + self.t, 0:own]
            self.part[0:own] = total
        self.part[own:] = jnp.sum(self.slots[:, own:], 0)
        self.tops[self.hi] = self.part[...]
        for k in range(1, self.far):
            self.second(k, False).start()

    def finish(self):
        for k in range(1, self.far):
            self.second(k, True).wait_recv()
        return jnp.sum(self.tops[...], 0)

    def drain(self):
        for k in range(1, 2 * NEAR):
            self.first(k, False).wait_send()
        for k in range(1, self.far):
            self.second(k, False).wait_send()


def broadcast_scratch(count, far):
    dma = pltpu.SemaphoreType.DMA
    near = 2 * NEAR
    vm = lambda *shape: pltpu.VMEM(shape + (8, LANES), f32)
    return [vm(count), vm(near, count), vm(count), vm(far, count), dma((near,)), dma((near,)), dma((far,)), dma((far,))]


def row_tiles(ref):
    return [
        ref[r * 8 : r * 8 + 8, c * LANES : (c + 1) * LANES]
        for c in range(ref.shape[1] // LANES)
        for r in range(ref.shape[0] // 8)
    ]


def tiles(x):
    return [x[:, n * LANES : (n + 1) * LANES] for n in range(x.shape[1] // LANES)]


def stacked(x):
    hi, mid, lo = split3(x)
    hi, mid, lo = hi.astype(f32), mid.astype(f32), lo.astype(f32)
    left = jnp.concatenate([hi, hi, mid, hi, mid, lo], 0)
    right = jnp.concatenate([hi, mid, hi, lo, mid, hi], 0)
    return left, right


def update_kernel(
    oq, op, oi, oo, rqs, rp, ri, ro, rq, mq, mp, mi, mo, wq, wp, wi, wo, vq, vp, vi, vo,
    vec, one, two, gains, offs, taps, scales, bq, sharp, bi, gains_v, offs_v, taps_v, scales_v, bq_v, sharp_v, bi_v,
    wq_o, wp_o, wi_o, wo_o, vq_o, vp_o, vi_o, vo_o, eq_o, ep_o, ei_o, eo_o,
    gains_o, offs_o, taps_o, scales_o, bq_o, sharp_o, bi_o,
    gains_m, offs_m, taps_m, scales_m, bq_m, sharp_m, bi_m, tq_o, tp_o, ti_o, to_o, one_o, two_o,
    *, share,
):
    at = pl.program_id(0)
    one_o[...] = one[...]
    two_o[...] = two[pl.ds(pl.multiple_of(at * one.shape[0], 16), one.shape[0]), :]
    groups = (
        (oq, None, mq, wq, vq, wq_o, vq_o, eq_o),
        (op, rp, mp, wp, vp, wp_o, vp_o, ep_o),
        (oi, ri, mi, wi, vi, wi_o, vi_o, ei_o),
        (oo, ro, mo, wo, vo, wo_o, vo_o, eo_o),
    )
    steps = pl.num_programs(0)

    def own_part(ref):
        size = ref.shape[0] // steps
        return ref[pl.ds(pl.multiple_of(at * size, 8), size), :]

    for o, r, m, w, v, w_o, v_o, e_o in groups:
        if r is None:
            approx = dg(own_part(rqs).astype(bf16), o[...].astype(bf16), 1, 0)
        else:
            approx = dg(own_part(o).astype(bf16), stacked(r[...])[1].astype(bf16), 1, 0)
        moment = momentum_decay * v[...] + approx
        v_o[...] = moment
        w_o[...] = w[...] - learn_rate * moment
        size = w.shape[0]
        e_o[0] = m[pl.ds(pl.multiple_of(at * size, 8), size), :] - approx

    @pl.when(pl.program_id(0) == 0)
    def _():
        for r, t_o in ((rq, tq_o), (rp, tp_o), (ri, ti_o), (ro, to_o)):
            t_o[...] = r[...]

        def step(grad, value, moment, v_out, m_out, rows):
            new = momentum_decay * moment[rows, :] + grad * share
            m_out[rows, :] = new
            v_out[rows, :] = value[rows, :] - learn_rate * new

        def row2(a, b):
            return jnp.concatenate([vec[24 * c + a : 24 * c + b, :] for c in range(3)], -1)

        def row3(a, b):
            return jnp.concatenate([vec[72 + 16 * c + a : 72 + 16 * c + b, :] for c in range(3)], -1)

        def each(grads, value, moment, v_out, m_out):
            for n, g in enumerate(grads):
                step(g, value, moment, v_out, m_out, slice(n, n + 1))

        each([row3(0, 1), row3(2, 3), row2(6, 7), row2(1, 2)], gains, gains_v, gains_o, gains_m)
        each(
            [row3(1, 2), row3(3, 4), row2(7, 8), row2(0, 1), row3(4, 5), row2(2, 3), row2(3, 4)],
            offs, offs_v, offs_o, offs_m,
        )
        each([row3(5, 6), row2(4, 5), row2(5, 6)], scales, scales_v, scales_o, scales_m)
        each([row3(7 + n, 8 + n) for n in range(9)] + [row2(8 + n, 9 + n) for n in range(9)],
             taps, taps_v, taps_o, taps_m)
        base = 72 + 48
        half = bi.shape[0]
        step(vec[base : base + half, :], bi, bi_v, bi_o, bi_m, slice(None))
        base += 16
        step(vec[base : base + bq.shape[0], :], bq, bq_v, bq_o, bq_m, slice(None))
        width = gains.shape[1]
        heads = sharp.shape[1]
        head = width // heads
        chan = lax.broadcasted_iota(jnp.int32, (width, heads), 0)
        lane = lax.broadcasted_iota(jnp.int32, (width, heads), 1)
        pick = jnp.where((chan >= lane * head) & (chan < (lane + 1) * head), 1.0, 0.0).astype(f32)
        grad = thin(jnp.broadcast_to(row3(6, 7), (8, width)), pick, 0)
        step(grad[0:1, :], sharp, sharp_v, sharp_o, sharp_m, slice(None))


def body(
    tokens, classes, loss,
    tri, tri_b, sharp, mapw, expw, exp_b, conw, gains, offs, taps, scales,
    tri_v, map_v, exp_v, con_v, tri_b_v, sharp_v, exp_b_v, gains_v, offs_v, taps_v, scales_v,
    tri_e, map_e, exp_e, con_e, tri_f, map_f, exp_f, con_f,
):
    import functools

    far = lax.axis_size("dp") // NEAR
    rows, width = tokens.shape
    own = classes.shape[0] // 2
    cells = rows // own
    heads = sharp.shape[0]
    head = width // heads
    part = width // 2
    cols = tri.shape[1]
    half = expw.shape[1]
    hidden = 2 * half
    vm = pl.BlockSpec(memory_space=pltpu.VMEM)
    sm = pl.BlockSpec(memory_space=pltpu.SMEM)
    anyspace = pl.BlockSpec(memory_space=pl.ANY)

    def whole(*shape):
        return pl.BlockSpec(shape, lambda i: (0,) * len(shape), pipeline_mode=pl.Buffered(1))

    image = pl.BlockSpec((cells, width), lambda i: (i, 0))
    square = pl.BlockSpec((1, 2, 2 * LANES, 2 * LANES), lambda i: (i, 0, 0, 0))
    eight = pl.BlockSpec((1, 8, width), lambda i: (i, 0, 0))
    smem = pl.BlockSpec(memory_space=pltpu.SMEM)
    vecs = [whole(4, width), whole(7, width), whole(18, width), whole(3, width)]
    field = pltpu.VMEM((TRIO + 2, SIDE + 2, GROUPS, width), f32)
    nat = pltpu.VMEM((3, cells, LANES), f32)
    mask = pltpu.VMEM((TRIO * SIDE, GROUPS, LANES), f32)
    canvas = pltpu.VMEM((cells, width), f32)

    dma = pltpu.SemaphoreType.DMA
    devices = lax.axis_size("dp") * 2
    two_windows = pltpu.VMEM((2, 2 * LANES, 2 * LANES), f32)
    tile_exchange = [
        pltpu.VMEM((8, LANES), f32), pltpu.VMEM((devices, 8, LANES), f32),
    ]
    first, active, dgelu, low, q, k, v, mix, xc, attn, gram, rs, stat, lc, wt, wp, win, wout = pl.pallas_call(
        first_kernel,
        grid=(own,),
        out_shape=[sds((rows, width))] * 3
        + [sds((rows, width), bf16)] * 6
        + [sds((own, 2, 2 * LANES, 2 * LANES))] * 2
        + [sds((own, 8, width)), sds((8, LANES)), sds((rows, width), bf16)]
        + [sds((3, 2, part, width), bf16), sds((2, part, width), bf16),
           sds((2, width, half), bf16), sds((2, half, width), bf16)],
        in_specs=[smem, smem, anyspace, whole(cols, width), whole(part, width), whole(2 * cols // LANES, LANES)]
        + vecs + [anyspace] * 3,
        out_specs=[anyspace] * 11 + [eight, whole(8, LANES)] + [anyspace] * 5,
        scratch_shapes=[
            nat, mask, canvas, field, two_windows, two_windows, pltpu.VMEM((2, 8, width), f32),
            pltpu.VMEM((3, 2, part, width), bf16), pltpu.VMEM((2, part, width), bf16),
            pltpu.VMEM((2, width, half), bf16), pltpu.VMEM((2, half, width), bf16),
            pltpu.VMEM((width, half), f32), pltpu.VMEM((half, width), f32), pltpu.VMEM((rows, width), bf16),
            pltpu.VMEM((rows, width), bf16), mask,
            pltpu.VMEM((cols, cols), bf16), pltpu.VMEM((8, width), f32),
        ] + [pltpu.VMEM((rows, width), f32)] * 3 + [pltpu.VMEM((rows, width), bf16)] * 6
        + [pltpu.VMEM((own, 2, 2 * LANES, 2 * LANES), f32)] * 2 + [pltpu.VMEM((rows, width), bf16)]
        + tile_exchange + [dma((11, own)), dma((5,)), dma((6,)), dma((6,)), dma((devices,)), dma((devices,))],
        compiler_params=params(61, collective_id=0, has_side_effects=True),
        name="first_part",
    )(classes, sharp, tokens, tri.T, mapw, tri_b.reshape(-1, LANES), gains, offs, taps, scales, expw, conw, loss)
    wt = wt.reshape(3, width, width)
    wp = wp.reshape(width, width)

    block_out, gsec, gsh, gin, gout, mo_part, vec2, inb, gstat, stat = pl.pallas_call(
        middle_kernel,
        grid=(own,),
        out_shape=[
            sds((rows, width), bf16), sds((rows, width)), sds((rows, width)),
            sds((2, width, half)), sds((2, width, half)), sds((half, width)), held((24, width)), held((16, LANES)), held((8, LANES)), held((8, LANES)),
        ],
        in_specs=[smem, image, image, image, whole(8, LANES), anyspace, anyspace,
                  whole(hidden // LANES, LANES)] + vecs + [anyspace] * 2,
        out_specs=[anyspace] * 6 + [vm] * 4,
        scratch_shapes=[
            nat, mask, field, field, canvas, canvas, pltpu.VMEM((cells, LANES), f32), canvas, canvas,
            pltpu.VMEM((rows, width), bf16), pltpu.VMEM((rows, width), bf16),
            pltpu.VMEM((rows, hidden), bf16), pltpu.VMEM((rows, hidden), bf16),
            pltpu.VMEM((17, 8, width), f32), pltpu.VMEM((8, hidden), f32),
            pltpu.VMEM((2, width, half), bf16), pltpu.VMEM((2, half, width), bf16),
            pltpu.VMEM((rows, width), bf16), pltpu.VMEM((rows, width), f32), pltpu.VMEM((rows, width), f32),
            pltpu.VMEM((2, width, half), f32), pltpu.VMEM((2, width, half), f32),
            pltpu.VMEM((width, half), f32), pltpu.VMEM((half, width), f32),
            dma((3, own)), dma((5,)), dma((4,)),
        ] + tile_exchange + [dma((devices,)), dma((devices,))],
        compiler_params=params(56, collective_id=1, has_side_effects=True),
        name="middle_part",
    )(classes, first, active, lc, stat, win, wout, exp_b.reshape(hidden // LANES, LANES), gains, offs, taps, scales,
      exp_e, con_e)
    input_grad, mq, mp, mi, mo, oq, op, oi, oo, rq, rp, ri, ro, rqs, vec = pl.pallas_call(
        functools.partial(last_kernel, far),
        grid=(own,),
        out_shape=[
            held((rows, width), bf16),
            held((cols, width)), held((part, width)), held((width, half)), held((half, width)),
            held((48, width)), held((part, 48)), held((width, 48)), held((half, 48)),
            held((8, cols)), held((8, width)), held((8, half)), held((8, width)), held((cols, 48)), held((152, LANES)),
        ],
        in_specs=[smem, smem, anyspace] + [image] * 5 + [anyspace] + [image] * 3
        + [anyspace] + [square, square, eight, vm, vm] + [anyspace] * 2 + vecs
        + [anyspace] * 5 + [whole(8, cols), whole(8, width), whole(8, half), whole(8, width), vm, vm],
        out_specs=[vm] * 15,
        scratch_shapes=[
            nat, mask, pltpu.VMEM((cells, LANES), f32), field, field, pltpu.VMEM((rows, width), f32),
            pltpu.VMEM((rows, 3 * width), bf16),
            pltpu.VMEM((16, 8, width), f32), pltpu.VMEM((3, 8, width), f32), two_windows,
            pltpu.VMEM((width, width), f32),
            pltpu.VMEM((width, half), f32), pltpu.VMEM((width, half), f32),
            pltpu.VMEM((3, part, width), f32), pltpu.VMEM((part, width), f32),
            pltpu.VMEM((3, 2, part, width), f32), pltpu.VMEM((2, part, width), f32),
            pltpu.VMEM((16, width), f32), pltpu.VMEM((16, LANES), f32),
            pltpu.VMEM((2, 8, half), f32),
            pltpu.VMEM((rows, width), bf16), pltpu.VMEM((rows, width), bf16), pltpu.VMEM((rows, width), bf16),
            pltpu.VMEM((3, width, width), bf16), pltpu.VMEM((width, width), bf16), pltpu.VMEM((cols, cols), bf16), pltpu.VMEM((2, 8, cols), f32), dma((2,)),
            dma((6,)), dma((6,)), dma((6,)), dma((6,)),
        ]
        + spread_scratch(4, far) + spread_scratch(2, far) + spread_scratch(1, far)
        + broadcast_scratch(6, far) + broadcast_scratch(-(-cols // LANES) + 3, far),
        compiler_params=params(47 + far // 8, collective_id=2, has_side_effects=True),
        name="last_part",
    )(classes, sharp, xc, first, active, dgelu, gsec, gsh, low, q, k, v, mix, attn, gram, rs, stat, gstat,
      wt, wp, gains, offs, taps, scales, gin, gout, tri_e.swapaxes(1, 2), map_e, mo_part,
      tri_f.T, map_f.T, exp_f.T, con_f.T, vec2, inb)

    steps = 3

    def cut(n, m):
        return pl.BlockSpec((n // steps, m), lambda i: (i, 0))

    def cut3(n, m):
        return pl.BlockSpec((1, n // steps, m), lambda i: (0, i, 0))

    wide = lambda x: x.reshape(-1, LANES)
    mats = [cut(cols, width), cut(part, width), cut(width, half), cut(half, width)]
    small_specs = vecs + [whole(2 * cols // LANES, LANES), whole(1, heads), whole(hidden // LANES, LANES)]
    basis_specs = [whole(8, cols), whole(8, width), whole(8, half), whole(8, width)]
    basis_shapes = [sds((8, cols)), sds((8, width)), sds((8, half)), sds((8, width))]
    small_shapes = [sds((4, width)), sds((7, width)), sds((18, width)), sds((3, width)), sds((2 * cols // LANES, LANES)), sds((1, heads)), sds((hidden // LANES, LANES))]
    mat_shapes = [sds((cols, width)), sds((part, width)), sds((width, half)), sds((half, width))]
    res = pl.pallas_call(
        functools.partial(update_kernel, share=1.0 / (far * NEAR)),
        grid=(steps,),
        out_shape=mat_shapes * 2
        + [sds((1, cols, width)), sds((1, part, width)), sds((1, width, half)), sds((1, half, width))]
        + small_shapes * 2 + basis_shapes + [sds((rows, width), bf16)] * 2,
        in_specs=[vm] * 13 + mats * 2 + [vm, cut(rows, width), vm] + small_specs * 2,
        out_specs=mats * 2
        + [cut3(cols, width), cut3(part, width), cut3(width, half), cut3(half, width)]
        + small_specs * 2 + basis_specs + [cut(rows, width)] * 2,
        compiler_params=params(30),
        name="update",
    )(oq, op, oi, oo, rqs, rp, ri, ro, rq, mq, mp, mi, mo, tri.T, mapw, expw, conw, tri_v.T, map_v, exp_v, con_v,
      vec, block_out, input_grad, gains, offs, taps, scales, wide(tri_b), sharp.reshape(1, heads), wide(exp_b),
      gains_v, offs_v, taps_v, scales_v, wide(tri_b_v), sharp_v.reshape(1, heads), wide(exp_b_v))
    nw, nv, ne, sv, smo, nt = res[0:4], res[4:8], res[8:12], res[12:19], res[19:26], res[26:30]
    block_out, input_grad = res[30:32]
    nw, nv = [nw[0].T, *nw[1:]], [nv[0].T, *nv[1:]]
    ne = [ne[0].swapaxes(1, 2), *ne[1:]]
    nt = [x.T for x in nt]

    def small(x):
        g, o, t_, s, b, sh, bi_ = x
        return (b.reshape(-1), sh.reshape(-1), bi_.reshape(-1), g, o, t_, s)

    return (
        (block_out, input_grad) + tuple(nw) + small(sv) + tuple(nv) + small(smo) + tuple(ne) + tuple(nt)
    )


def solution(mesh):
    rows = P(("dp", "tensor"), None)
    col, row = P(None, "tensor"), P("tensor", None)
    rep = P()
    err = (P("dp", None, "tensor"), P("dp", "tensor", None), P("dp", None, "tensor"), P("dp", "tensor", None))
    mats = (col, row, col, row)
    in_specs = (
        (rows, P("dp"), rows, col, rep, rep, row, col, rep, row, rep, rep, rep, rep)
        + mats + (rep,) * 7 + err + (row, rep, row, rep)
    )
    out_specs = (rows, rows) + mats + (rep,) * 7 + mats + (rep,) * 7 + err + (row, rep, row, rep)
    return jax.shard_map(body, mesh=mesh, in_specs=in_specs, out_specs=out_specs, check_vma=False)
```
